32 devices in a mesh: dp: 8 (over z, x), chan: 4 (over y, core).
Axes of the slice: x: 2, y: 2, z: 4, core: 2. Of those that a mesh axis runs over, the one named last changes fastest.
Arguments:
- images: bfloat16 [256, 7, 7, 2048], P('dp'), may hold values from -6 to 6
- crop_image: int32 [256], P('dp'), may hold values from 0 to 15
- slot_rows: int32 [4096], replicated, may hold values from 0 to 2048, as said below
- squeeze_weight: float32 [4096, 512], P('dp', 'chan'), may hold values from -0.125 to 0.125
- squeeze_moment: float32 [4096, 512], P('dp', 'chan'), may hold values from -320 to 320
- squeeze_second: float32 [4096, 512], P('dp', 'chan'), may hold values from 2829.9302 to 11319.721
- spatial_weight: float32 [4608, 512], P('dp', 'chan'), may hold values from -0.09375 to 0.09375
- spatial_moment: float32 [4608, 512], P('dp', 'chan'), may hold values from -256 to 256
- spatial_second: float32 [4608, 512], P('dp', 'chan'), may hold values from 1599.999 to 6399.996
- expand_weight: float32 [4096, 512], P('dp', 'chan'), may hold values from -0.25 to 0.25
- expand_moment: float32 [4096, 512], P('dp', 'chan'), may hold values from -128 to 128
- expand_second: float32 [4096, 512], P('dp', 'chan'), may hold values from 399.99976 to 1599.999
- hidden_weight: float32 [4096, 2048], P('dp', 'chan'), may hold values from -0.125 to 0.125
- hidden_moment: float32 [4096, 2048], P('dp', 'chan'), may hold values from -160 to 160
- hidden_second: float32 [4096, 2048], P('dp', 'chan'), may hold values from 799.9995 to 3199.998
- project_weight: float32 [4096, 128], P('dp'), may hold values from -0.125 to 0.125
- project_moment: float32 [4096, 128], P('dp'), may hold values from -640 to 640
- project_second: float32 [4096, 128], P('dp'), may hold values from 13866.658 to 55466.633
- prototypes: float32 [128, 3000], replicated, may hold values from -0.2 to 0.2
- proto_moment: float32 [128, 3000], replicated, may hold values from -112 to 112
- proto_second: float32 [128, 3000], replicated, may hold values from 355.55533 to 1422.2213
- norm_params: float32 [2, 4, 1280], P(None, 'chan'), may hold values from 0.25 to 1.75
- norm_moment: float32 [2, 4, 1280], P(None, 'chan'), may hold values from -139.9708 to 139.9708
- norm_second: float32 [2, 4, 1280], P(None, 'chan'), may hold values from 272.10867 to 8707.478
- queue_rows: bfloat16 [3840, 128], P('dp'), may hold values from -1.25 to 1.25
- queue_valid: int32 [3840], P('dp'), may hold values 0 or 1
- queue_fill: int32 [1], replicated, may hold values from 960 to 3839
- iteration: int32 [1], replicated, may hold values from 1 to 4
Outputs:
- block_out: bfloat16 [256, 7, 7, 2048], P('dp', None, None, 'chan')
- loss: float32 [1], replicated
- images_grad: float32 [256, 7, 7, 2048], P('dp', None, None, 'chan')
- squeeze_weight_new: float32 [4096, 512], P('dp', 'chan')
- squeeze_moment_new: float32 [4096, 512], P('dp', 'chan')
- squeeze_second_new: float32 [4096, 512], P('dp', 'chan')
- spatial_weight_new: float32 [4608, 512], P('dp', 'chan')
- spatial_moment_new: float32 [4608, 512], P('dp', 'chan')
- spatial_second_new: float32 [4608, 512], P('dp', 'chan')
- expand_weight_new: float32 [4096, 512], P('dp', 'chan')
- expand_moment_new: float32 [4096, 512], P('dp', 'chan')
- expand_second_new: float32 [4096, 512], P('dp', 'chan')
- hidden_weight_new: float32 [4096, 2048], P('dp', 'chan')
- hidden_moment_new: float32 [4096, 2048], P('dp', 'chan')
- hidden_second_new: float32 [4096, 2048], P('dp', 'chan')
- project_weight_new: float32 [4096, 128], P('dp')
- project_moment_new: float32 [4096, 128], P('dp')
- project_second_new: float32 [4096, 128], P('dp')
- prototypes_new: float32 [128, 3000], replicated
- proto_moment_new: float32 [128, 3000], replicated
- proto_second_new: float32 [128, 3000], replicated
- norm_params_new: float32 [2, 4, 1280], P(None, 'chan')
- norm_moment_new: float32 [2, 4, 1280], P(None, 'chan')
- norm_second_new: float32 [2, 4, 1280], P(None, 'chan')
The draws below stay inside these ranges and needn't reach their ends.
Inputs may be any that keep to these rules, and one draw needn't show every extreme that they name: `slot_rows`: every channel 0 to 2047 stands in exactly one slot; the value 2048 marks an empty slot. Slots k * 512 onward belong to owner k of dp; loads are uneven, and one owner's slots are all used in every draw. `crop_image`: crops with the same label in one device's block of 32 crops are views of one image.
All inputs are finite; a program needn't handle non-finite values. No bound on the sum of `queue_valid` on one device may be relied on, other than what follows from the above.
Results may differ from the reference program's by a relative error of at most 0.028.
Values may be sent and summed in bfloat16 or wider, within the bound.
No kernel may reach another device: no remote copies, remote signals or barrier semaphores. Data moves between devices by JAX's collectives and lax.ppermute only.
A program may use at most 256 MiB of HBM per device.

```python
import math
import jax
import jax.numpy as jnp
from jax import lax

C_IN = 2048
C_MID = 512
HID = 2048
PROJ = 128
PROTO = 3000
QUEUE = 3840
CROPS_DEV = 32
SIDE = 7
SINK_ITERS = 3
HW = 49
CROPS = 256
DEAL_CAP = 512
SLOTS = 4096
NORM_GROUP = 1280
N_DP = 8
N_CHAN = 4


def draw_slot_rows(key, part):
    key_owner, key_order, key_rows = jax.random.split(key, 3)
    full_owner = jax.random.randint(key_owner, (), 0, N_DP)
    owner_of = jnp.arange(SLOTS, dtype=jnp.int32) // DEAL_CAP
    noise_bits = jax.random.randint(key_order, (SLOTS,), 0, 1 << 16)
    ranked = noise_bits * SLOTS + jnp.arange(SLOTS, dtype=jnp.int32)
    ranked = jnp.where(owner_of == full_owner, ranked - (1 << 16) * SLOTS, ranked)
    slot_order = jnp.argsort(ranked, stable=True)
    chosen = slot_order[:C_IN]
    channels = jax.random.permutation(key_rows, C_IN).astype(jnp.int32)
    return jnp.full((SLOTS,), C_IN, jnp.int32).at[chosen].set(channels)


def norm_square():
    scale_base = CROPS * min(2000000.0, float(1600000000 // PROTO))
    mid_width = C_MID // N_CHAN
    out_width = C_IN // N_CHAN
    column = jnp.arange(NORM_GROUP)
    gain_part = jnp.where(column < 2 * mid_width, 0.2 * scale_base / (HW * C_MID), jnp.where(column < 2 * mid_width + out_width, 0.2 * scale_base / (HW * C_IN), 0.012 * scale_base / HID))
    bias_part = jnp.where(column < 2 * mid_width, 0.4 * scale_base / (HW * C_MID), jnp.where(column < 2 * mid_width + out_width, 0.4 * scale_base / (HW * C_IN), 0.012 * scale_base / HID))
    return jnp.stack([gain_part, bias_part]).astype(jnp.float32)[:, None, :]


def draw_norm_moment(key, part):
    key = jax.random.fold_in(key, 11)
    normal_vals = jnp.clip(jax.random.normal(key, (2, N_CHAN, NORM_GROUP), jnp.float32), -3.0, 3.0)
    return normal_vals * jnp.sqrt(norm_square())


def draw_norm_second(key, part):
    key = jax.random.fold_in(key, 12)
    log_part = jax.random.uniform(key, (2, N_CHAN, NORM_GROUP), jnp.float32, 0.0, 1.3862944)
    return norm_square() * jnp.exp(log_part)


def plant(array, key, least, top_value):
    place = [jax.random.randint(jax.random.fold_in(key, axis), (), 0, length) for axis, length in enumerate(array.shape)]
    widest = array.shape.index(max(array.shape))
    neighbour = place[:widest] + [(place[widest] + 1) % array.shape[widest]] + place[widest + 1:]
    return array.at[tuple(place)].set(least).at[tuple(neighbour)].set(top_value)


def level_of(key, dims, shards, smallest, high):
    loudness = 1.0
    for dim, parts in shards:
        steps = jax.random.uniform(jax.random.fold_in(jax.random.fold_in(key, 6), dim), (parts,), jnp.float32, smallest / len(shards), high / len(shards))
        loudness = loudness * jnp.repeat(jnp.exp(steps), dims[dim] // parts).reshape((-1,) + (1,) * (len(dims) - 1 - dim))
    return loudness


def normal_values(stream_key, dims, deviation, most, shards=(), held_as=jnp.bfloat16):
    factor_of = level_of(stream_key, dims, shards, -0.22, 0.18) if shards else 1.0
    result = jax.random.normal(stream_key, dims, jnp.float32) * deviation * factor_of
    return jnp.minimum(jnp.maximum(result, -most), most).astype(held_as)


def setup_inputs(seed: int = 0) -> dict:
    keys = jax.random.split(jax.random.key(seed), 29)
    images = normal_values(keys[0], (CROPS, SIDE, SIDE, C_IN), 1.0, 6.0, ((0, 8),))
    crop_image = plant(jax.random.randint(keys[1], (CROPS,), 0, CROPS_DEV // 2), jax.random.fold_in(keys[1], 1), 0, (CROPS_DEV // 2) - 1).astype(jnp.int32)
    slot_rows = draw_slot_rows(jax.random.fold_in(keys[28], 71), 0)
    squeeze_weight = normal_values(keys[3], (SLOTS, C_MID), C_IN ** -0.5, 0.125, ((0, 8), (1, 4)), jnp.float32)
    squeeze_moment = normal_values(keys[4], (SLOTS, C_MID), ((0.52 * CROPS * min(2000000, 1600000000 // PROTO) * (HW * C_MID) ** -1) ** 0.5), 320.0, ((0, 8), (1, 4)), jnp.float32)
    squeeze_second = jnp.clip(jnp.exp(math.log(11319.721) - 1.3862944 * jax.random.uniform(keys[5], (SLOTS, C_MID), jnp.float32) ** level_of(keys[5], (SLOTS, C_MID), ((0, 8), (1, 4)), -0.2, 0.2)), 2829.9302, 11319.721)
    spatial_weight = normal_values(keys[6], (9 * C_MID, C_MID), (9 * C_MID) ** -0.5, 0.09375, ((0, 8), (1, 4)), jnp.float32)
    spatial_moment = normal_values(keys[7], (9 * C_MID, C_MID), ((0.006 * CROPS * min(2000000, 1600000000 // PROTO) * C_MID ** -1) ** 0.5), 256.0, ((0, 8), (1, 4)), jnp.float32)
    spatial_second = jnp.clip(jnp.exp(math.log(6399.996) - 1.3862944 * jax.random.uniform(keys[8], (9 * C_MID, C_MID), jnp.float32) ** level_of(keys[8], (9 * C_MID, C_MID), ((0, 8), (1, 4)), -0.2, 0.2)), 1599.999, 6399.996)
    expand_weight = normal_values(keys[9], (SLOTS, C_MID), C_MID ** -0.5, 0.25, ((0, 8), (1, 4)), jnp.float32)
    expand_moment = normal_values(keys[10], (SLOTS, C_MID), ((0.006 * CROPS * min(2000000, 1600000000 // PROTO) * C_IN ** -1) ** 0.5), 128.0, ((0, 8), (1, 4)), jnp.float32)
    expand_second = jnp.clip(jnp.exp(math.log(1599.999) - 1.3862944 * jax.random.uniform(keys[11], (SLOTS, C_MID), jnp.float32) ** level_of(keys[11], (SLOTS, C_MID), ((0, 8), (1, 4)), -0.2, 0.2)), 399.99976, 1599.999)
    hidden_weight = normal_values(keys[12], (SLOTS, HID), C_IN ** -0.5, 0.125, ((0, 8), (1, 4)), jnp.float32)
    hidden_moment = normal_values(keys[13], (SLOTS, HID), ((0.012 * CROPS * min(2000000, 1600000000 // PROTO) * HID ** -1) ** 0.5), 160.0, ((0, 8), (1, 4)), jnp.float32)
    hidden_second = jnp.clip(jnp.exp(math.log(3199.998) - 1.3862944 * jax.random.uniform(keys[14], (SLOTS, HID), jnp.float32) ** level_of(keys[14], (SLOTS, HID), ((0, 8), (1, 4)), -0.2, 0.2)), 799.9995, 3199.998)
    project_weight = normal_values(keys[15], (SLOTS, PROJ), HID ** -0.5, 0.125, ((0, 8),), jnp.float32)
    project_moment = normal_values(keys[16], (SLOTS, PROJ), ((0.013 * CROPS * min(2000000, 1600000000 // PROTO) * PROJ ** -1) ** 0.5), 640.0, ((0, 8),), jnp.float32)
    project_second = jnp.clip(jnp.exp(math.log(55466.633) - 1.3862944 * jax.random.uniform(keys[17], (SLOTS, PROJ), jnp.float32) ** level_of(keys[17], (SLOTS, PROJ), ((0, 8),), -0.2, 0.2)), 13866.658, 55466.633)
    prototypes = jnp.clip(jax.random.uniform(keys[18], (PROJ, PROTO), jnp.float32, -0.2, 0.2), -0.2, 0.2)
    proto_moment = normal_values(keys[19], (PROJ, PROTO), ((CROPS * min(2000000, 1600000000 // PROTO) * (PROJ * PROTO) ** -1) ** 0.5), 112.0, (), jnp.float32)
    proto_second = jnp.clip(jnp.exp(jax.random.uniform(keys[20], (PROJ, PROTO), jnp.float32, math.log(355.55533), math.log(1422.2213))), 355.55533, 1422.2213)
    norm_params = jnp.clip(1.0 + 0.15 * jax.random.normal(keys[21], (2, N_CHAN, NORM_GROUP), jnp.float32), 0.25, 1.75)
    norm_moment = draw_norm_moment(jax.random.fold_in(keys[28], 71), 0)
    norm_second = draw_norm_second(jax.random.fold_in(keys[28], 71), 0)
    queue_rows = normal_values(keys[24], (QUEUE, PROJ), (PROJ ** -0.5), 1.25, ((0, 8),))
    queue_valid = plant((jax.random.randint(keys[25], (QUEUE,), 0, 4) < 3).astype(jnp.int32), jax.random.fold_in(keys[25], 1), 0, 1)
    queue_fill = jax.random.randint(keys[26], (1,), QUEUE // 4, QUEUE).astype(jnp.int32)
    iteration = jax.random.randint(keys[27], (1,), 1, 5).astype(jnp.int32)
    return dict(images=images, crop_image=crop_image, slot_rows=slot_rows, squeeze_weight=squeeze_weight, squeeze_moment=squeeze_moment, squeeze_second=squeeze_second, spatial_weight=spatial_weight, spatial_moment=spatial_moment, spatial_second=spatial_second, expand_weight=expand_weight, expand_moment=expand_moment, expand_second=expand_second, hidden_weight=hidden_weight, hidden_moment=hidden_moment, hidden_second=hidden_second, project_weight=project_weight, project_moment=project_moment, project_second=project_second, prototypes=prototypes, proto_moment=proto_moment, proto_second=proto_second, norm_params=norm_params, norm_moment=norm_moment, norm_second=norm_second, queue_rows=queue_rows, queue_valid=queue_valid, queue_fill=queue_fill, iteration=iteration)


PRECISE = lax.Precision.HIGHEST
EPS_SINK = 0.05
SOFTMAX_WARMTH = 0.1
LOSS_MULTIPLIER = 256.0
NORM_EPS = 1e-05
BETA_ONE = 0.5
BETA_TWO = 0.5
ADAM_EPS = 1e-08
DECAY_RATE = 1e-06

@jax.custom_vjp
def low(v):
    return lax.optimization_barrier(v.astype(jnp.bfloat16)).astype(jnp.float32)

@jax.custom_vjp
def low_back(v):
    return v

def low_keep(v):
    return (low(v), None)

def low_pass(kept, grad):
    return (grad,)

def back_keep(v):
    return (v, None)

def back_low(kept, grad):
    return (low(grad),)
low.defvjp(low_keep, low_pass)
low_back.defvjp(back_keep, back_low)

def matmul(left, right):
    return jnp.dot(left, right, precision=PRECISE)

def batch_norm(pre_act, gain_row, bias_row):
    row_count = pre_act.shape[0]
    average = lax.optimization_barrier(jnp.sum(pre_act, axis=0)) / row_count
    variance = lax.optimization_barrier(jnp.sum(pre_act * pre_act, axis=0)) / row_count - average * average
    return (pre_act - average) * lax.rsqrt(variance + NORM_EPS) * gain_row + bias_row

def unpack_norms(norm_params):
    mid_width = C_MID // N_CHAN
    out_width = C_IN // N_CHAN
    first_norm = norm_params[:, :, :mid_width].reshape(2, C_MID)
    second_norm = norm_params[:, :, mid_width:2 * mid_width].reshape(2, C_MID)
    third_norm = norm_params[:, :, 2 * mid_width:2 * mid_width + out_width].reshape(2, C_IN)
    head_norm = norm_params[:, :, 2 * mid_width + out_width:].reshape(2, HID)
    return (first_norm, second_norm, third_norm, head_norm)

def patches(inner):
    feature_maps = inner.reshape(CROPS, SIDE, SIDE, C_MID)
    padded = jnp.pad(feature_maps, ((0, 0), (1, 1), (1, 1), (0, 0)))
    tap_list = [padded[:, row_at:row_at + SIDE, col_at:col_at + SIDE, :] for row_at in range(3) for col_at in range(3)]
    return jnp.concatenate(tap_list, axis=3).reshape(CROPS * HW, 9 * C_MID)

def network(params, pictures, slot_rows):
    squeeze_weight, spatial_weight, expand_weight, hidden_weight, project_weight, prototypes, norm_params = params
    row_place = jnp.zeros((C_IN + 1,), jnp.int32).at[slot_rows].set(jnp.arange(SLOTS, dtype=jnp.int32))[:C_IN]
    squeeze_rows = low(squeeze_weight)[row_place]
    expand_rows = low(expand_weight)[row_place]
    hidden_rows = low(hidden_weight)[row_place]
    project_rows = low(project_weight)[row_place]
    first_norm, second_norm, third_norm, head_norm = unpack_norms(norm_params)
    pixels = pictures.reshape(CROPS * HW, C_IN)
    pre_one = low_back(matmul(pixels, squeeze_rows))
    inner_one = low(jax.nn.silu(batch_norm(pre_one, first_norm[0], first_norm[1])))
    pre_two = low_back(matmul(patches(inner_one), low(spatial_weight)))
    inner_two = low(jax.nn.silu(batch_norm(pre_two, second_norm[0], second_norm[1])))
    pre_three = low_back(matmul(inner_two, expand_rows.T))
    summed = batch_norm(pre_three, third_norm[0], third_norm[1]) + pixels
    block_rows = jax.nn.silu(summed)
    pooled = low(lax.optimization_barrier(jnp.mean(block_rows.reshape(CROPS, HW, C_IN), axis=1)))
    hidden_pre = low_back(matmul(pooled, hidden_rows))
    hidden_act = low(jax.nn.silu(batch_norm(hidden_pre, head_norm[0], head_norm[1])))
    project_out = low_back(matmul(hidden_act, project_rows))
    normed = project_out * lax.rsqrt(lax.optimization_barrier(jnp.sum(project_out * project_out, axis=1, keepdims=True)) + 1e-06)
    prototype_scores = low_back(matmul(low(normed), low(prototypes)))
    return (block_rows, prototype_scores)

def transport_codes(prototype_scores, queue_similarity, queue_active):
    batch_codes = jnp.exp(prototype_scores / EPS_SINK)
    queue_codes = jnp.exp(queue_similarity / EPS_SINK) * queue_active[:, None]
    for turn_index in range(SINK_ITERS):
        proto_totals = lax.optimization_barrier(jnp.sum(batch_codes, axis=0)) + lax.optimization_barrier(jnp.sum(queue_codes, axis=0))
        batch_codes = batch_codes / proto_totals
        queue_codes = queue_codes / proto_totals
        batch_codes = batch_codes / lax.optimization_barrier(jnp.sum(batch_codes, axis=1, keepdims=True))
        queue_sums = lax.optimization_barrier(jnp.sum(queue_codes, axis=1, keepdims=True))
        queue_codes = queue_codes / jnp.where(queue_active[:, None] > 0, queue_sums, 1.0)
    return batch_codes

def crop_targets(balanced_codes, crop_image):
    labels = crop_image.reshape(N_DP, CROPS_DEV)
    same_image = (labels[:, :, None] == labels[:, None, :]) & ~jnp.eye(CROPS_DEV, dtype=bool)[None]
    pair_weights = same_image.astype(jnp.float32)
    others = lax.optimization_barrier(jnp.sum(pair_weights, axis=2, keepdims=True))
    blocks = balanced_codes.reshape(N_DP, CROPS_DEV, PROTO)
    shared = jnp.einsum('nij,njk->nik', pair_weights, blocks, precision=PRECISE)
    return (shared / jnp.maximum(others, 1.0)).reshape(CROPS, PROTO)

def adamw_step(weight, moment_one, moment_two, gradient, learn_rate, weight_decay, step_count):
    moment_new = BETA_ONE * moment_one + (1.0 - BETA_ONE) * gradient
    second_new = BETA_TWO * moment_two + (1.0 - BETA_TWO) * gradient * gradient
    fix_one = 1.0 - jnp.power(BETA_ONE, step_count)
    fix_two = 1.0 - jnp.power(BETA_TWO, step_count)
    update = moment_new / fix_one / (jnp.sqrt(second_new / fix_two) + ADAM_EPS)
    return (weight - learn_rate * (update + weight_decay * weight), moment_new, second_new)

def reference(images, crop_image, slot_rows, squeeze_weight, squeeze_moment, squeeze_second, spatial_weight, spatial_moment, spatial_second, expand_weight, expand_moment, expand_second, hidden_weight, hidden_moment, hidden_second, project_weight, project_moment, project_second, prototypes, proto_moment, proto_second, norm_params, norm_moment, norm_second, queue_rows, queue_valid, queue_fill, iteration):
    params = (squeeze_weight, spatial_weight, expand_weight, hidden_weight, project_weight, prototypes, norm_params)
    pictures = images.astype(jnp.float32)
    block_first, leading_scores = network(params, pictures, slot_rows)
    queue_similarity = jnp.dot(queue_rows.astype(jnp.float32), low(prototypes), precision=PRECISE)
    slot_index = jnp.arange(QUEUE, dtype=jnp.int32)
    queue_active = ((queue_valid > 0) & (slot_index < queue_fill[0])).astype(jnp.float32)
    balanced_codes = transport_codes(leading_scores, queue_similarity, queue_active)
    target_rows = crop_targets(balanced_codes, crop_image)

    def objective(param_tuple, picture_in):
        block_rows, prototype_scores = network(param_tuple, picture_in, slot_rows)
        raw_scores = prototype_scores / SOFTMAX_WARMTH
        log_likelihoods = raw_scores - jax.nn.logsumexp(raw_scores, axis=1, keepdims=True)
        per_crop = -lax.optimization_barrier(jnp.sum(target_rows * log_likelihoods, axis=1))
        return (LOSS_MULTIPLIER * jnp.sum(per_crop), (block_rows, per_crop))
    total_value, pullback, aux_values = jax.vjp(objective, params, pictures, has_aux=True)
    block_rows, per_crop = aux_values
    param_grads, picture_grad = pullback(jnp.ones_like(total_value))
    grad_squeeze, grad_spatial, grad_expand, grad_hidden, grad_project, grad_proto, grad_norm = param_grads
    step_count = iteration[0].astype(jnp.float32)
    squeeze_out = adamw_step(squeeze_weight, squeeze_moment, squeeze_second, grad_squeeze, C_IN ** (-0.5), DECAY_RATE, step_count)
    spatial_out = adamw_step(spatial_weight, spatial_moment, spatial_second, grad_spatial, (9 * C_MID) ** (-0.5), DECAY_RATE, step_count)
    expand_out = adamw_step(expand_weight, expand_moment, expand_second, grad_expand, C_MID ** (-0.5), DECAY_RATE, step_count)
    hidden_out = adamw_step(hidden_weight, hidden_moment, hidden_second, grad_hidden, C_IN ** (-0.5), DECAY_RATE, step_count)
    project_out = adamw_step(project_weight, project_moment, project_second, grad_project, HID ** (-0.5), DECAY_RATE, step_count)
    proto_out = adamw_step(prototypes, proto_moment, proto_second, grad_proto, 0.1, DECAY_RATE, step_count)
    norm_out = adamw_step(norm_params, norm_moment, norm_second, grad_norm, 0.5, 0.0, step_count)
    block_out = block_rows.astype(jnp.bfloat16).reshape(CROPS, SIDE, SIDE, C_IN)
    loss = (jnp.sum(per_crop) / CROPS).reshape(1)
    return (block_out, loss, picture_grad, squeeze_out[0], squeeze_out[1], squeeze_out[2], spatial_out[0], spatial_out[1], spatial_out[2], expand_out[0], expand_out[1], expand_out[2], hidden_out[0], hidden_out[1], hidden_out[2], project_out[0], project_out[1], project_out[2], proto_out[0], proto_out[1], proto_out[2], norm_out[0], norm_out[1], norm_out[2])
```

```python
import jax
import jax.numpy as jnp
from jax import lax
from jax.sharding import PartitionSpec as P

SINK_ITERS = 3
PRECISE = lax.Precision.HIGHEST
EPS_SINK = 0.05
SOFTMAX_WARMTH = 0.1
LOSS_MULTIPLIER = 256.0
NORM_EPS = 1e-05
BETA_ONE = 0.5
BETA_TWO = 0.5
ADAM_EPS = 1e-08
DECAY_RATE = 1e-06
LOW = jnp.bfloat16
WIDE = jnp.float32


def contract(left, right, left_dim, right_dim):
    return lax.dot_general(
        left, right, (((left_dim,), (right_dim,)), ((), ())), preferred_element_type=WIDE
    )


def silu_slope(value):
    sigma = jax.nn.sigmoid(value)
    return sigma * (1.0 + value * (1.0 - sigma))


def spread(value, axis):
    count = lax.axis_size(axis)
    return lax.all_to_all(jnp.broadcast_to(value[None], (count,) + value.shape), axis, 0, 0)


def total(value, axis):
    return jnp.sum(spread(value, axis).astype(WIDE), axis=0)


def swap(value, axis, bit):
    return lax.ppermute(value, axis, [(at, at ^ bit) for at in range(lax.axis_size(axis))])


def gather_relative(value, axis):
    held = {0: value}
    bit = lax.axis_size(axis) // 2
    while bit:
        keys = sorted(held)
        came = swap(jnp.stack([held[k] for k in keys]), axis, bit)
        held.update({k ^ bit: came[n] for n, k in enumerate(keys)})
        bit //= 2
    return [held[k] for k in range(lax.axis_size(axis))]


def scatter_relative(parts, axis, sent=LOW):
    held = dict(enumerate(parts))
    bit = 1
    while bit < lax.axis_size(axis):
        keys = [k for k in sorted(held) if not k & bit]
        came = swap(jnp.stack([held[k | bit].astype(sent) for k in keys]), axis, bit)
        held = {k: held[k] + came[n].astype(WIDE) for n, k in enumerate(keys)}
        bit *= 2
    return held[0]


def total_hyper(value, axis):
    bit = 1
    while bit < lax.axis_size(axis):
        value = value + swap(value, axis, bit)
        bit *= 2
    return value


def block_at(value, index, size, dim):
    return lax.dynamic_slice_in_dim(value, index * size, size, dim)


def statistics(sums, row_total):
    average = sums[0] / row_total
    variance = sums[1] / row_total - average * average
    return average, lax.rsqrt(variance + NORM_EPS)


def backward_of_norm(grad_out, centred, inv_std, gain_row, sums, row_total):
    return gain_row * inv_std * (grad_out - (sums[0] + centred * sums[1]) / row_total)


def adamw_step(weight, moment_one, moment_two, gradient, learn_rate, weight_decay, step_count):
    moment_new = BETA_ONE * moment_one + (1.0 - BETA_ONE) * gradient
    second_new = BETA_TWO * moment_two + (1.0 - BETA_TWO) * gradient * gradient
    fix_one = 1.0 - jnp.power(BETA_ONE, step_count)
    fix_two = 1.0 - jnp.power(BETA_TWO, step_count)
    update = moment_new / fix_one / (jnp.sqrt(second_new / fix_two) + ADAM_EPS)
    return (weight - learn_rate * (update + weight_decay * weight), moment_new, second_new)


def local(
    images,
    crop_image,
    slot_rows,
    squeeze_weight,
    squeeze_moment,
    squeeze_second,
    spatial_weight,
    spatial_moment,
    spatial_second,
    expand_weight,
    expand_moment,
    expand_second,
    hidden_weight,
    hidden_moment,
    hidden_second,
    project_weight,
    project_moment,
    project_second,
    prototypes,
    proto_moment,
    proto_second,
    norm_params,
    norm_moment,
    norm_second,
    queue_rows,
    queue_valid,
    queue_fill,
    iteration,
):
    dp_count = lax.axis_size("dp")
    dp_at = lax.axis_index("dp")
    chan_count = lax.axis_size("chan")
    chan_at = lax.axis_index("chan")
    crops_dev, map_side, _, in_width = images.shape
    map_area = map_side * map_side
    pixel_rows = crops_dev * map_area
    pixel_total = pixel_rows * dp_count
    crop_total = crops_dev * dp_count
    mid_local = squeeze_weight.shape[1]
    hid_local = hidden_weight.shape[1]
    out_local = in_width // chan_count
    slot_local = squeeze_weight.shape[0]
    slot_total = slot_rows.shape[0]
    mid_width = mid_local * chan_count
    hid_width = hid_local * chan_count

    channels = jnp.arange(in_width, dtype=jnp.int32)
    place_hot = (slot_rows[None, :] == channels[:, None]).astype(LOW)
    own_slots = block_at(slot_rows, dp_at, slot_local, 0)
    own_hot = (own_slots[:, None] == channels[None, :]).astype(LOW)
    slot_hot = (slot_rows[:, None] == channels[None, :]).astype(LOW)
    slot_hot_rel = (
        (slot_rows ^ (chan_at * out_local))[:, None] == channels[None, :]
    ).astype(LOW)

    squeeze_all = spread(squeeze_weight.astype(LOW), "dp").reshape(slot_total, mid_local)
    spatial_all = lax.all_gather(spatial_weight.astype(LOW), "dp", axis=0, tiled=True)
    expand_all = lax.all_gather(expand_weight.astype(LOW), "dp", axis=0, tiled=True)
    head_all = lax.all_gather(
        jnp.concatenate([hidden_weight.astype(LOW), project_weight.astype(LOW)], axis=1),
        "dp",
        axis=0,
        tiled=True,
    )
    squeeze_rows = contract(place_hot, squeeze_all, 1, 0).astype(LOW)

    norm_rows = norm_params[:, 0, :]
    first_norm = norm_rows[:, :mid_local]
    second_norm = norm_rows[:, mid_local : 2 * mid_local]
    third_norm = norm_rows[:, 2 * mid_local : 2 * mid_local + out_local]
    head_norm = norm_rows[:, 2 * mid_local + out_local :]

    def inner_layer(pre_act, norm):
        sums = jnp.stack([jnp.sum(pre_act, axis=0), jnp.sum(pre_act * pre_act, axis=0)])
        raw_all = jnp.concatenate(gather_relative(pre_act.astype(LOW), "chan"), axis=1)
        average, inv_std = statistics(total(sums, "dp"), pixel_total)
        scale = inv_std * norm[0]
        affine = jnp.stack([scale, norm[1] - average * scale])
        affine_all = jnp.concatenate(gather_relative(affine, "chan"), axis=1)
        act_all = jax.nn.silu(raw_all.astype(WIDE) * affine_all[0] + affine_all[1]).astype(LOW)
        return act_all, average, inv_std

    pixels = images.transpose(1, 2, 0, 3).reshape(pixel_rows, in_width)
    pre_one = contract(pixels, squeeze_rows, 1, 0)
    inner_one, average_one, inv_one = inner_layer(pre_one, first_norm)

    def relative_blocks(value, size, dim):
        return [block_at(value, chan_at ^ r, size, dim) for r in range(chan_count)]

    spatial_rel = jnp.concatenate(
        relative_blocks(spatial_all.reshape(9, mid_width, mid_local), mid_local, 1), axis=1
    ).reshape(3, 3, mid_width, mid_local)
    maps_one = inner_one.reshape(map_side, map_side, crops_dev, mid_width)
    conv_dims = lax.ConvDimensionNumbers((2, 3, 0, 1), (3, 2, 0, 1), (2, 3, 0, 1))
    pre_two = lax.conv_general_dilated(
        maps_one,
        spatial_rel,
        (1, 1),
        ((1, 1), (1, 1)),
        dimension_numbers=conv_dims,
        preferred_element_type=WIDE,
    ).reshape(pixel_rows, mid_local)
    inner_two, average_two, inv_two = inner_layer(pre_two, second_norm)

    expand_rows = contract(place_hot, expand_all, 1, 0).astype(LOW)
    expand_sent = relative_blocks(expand_rows, out_local, 0)
    expand_rel = jnp.concatenate(
        [expand_sent[0]] + [swap(expand_sent[r], "chan", r) for r in range(1, chan_count)], axis=1
    )
    squeeze_sent = relative_blocks(squeeze_rows, out_local, 0)
    squeeze_rel = jnp.concatenate(
        [squeeze_sent[0]] + [swap(squeeze_sent[r], "chan", r) for r in range(1, chan_count)],
        axis=1,
    )
    pre_three = contract(inner_two, expand_rel, 1, 1)
    sums_three = total(
        jnp.stack([jnp.sum(pre_three, axis=0), jnp.sum(pre_three * pre_three, axis=0)]), "dp"
    )
    average_three, inv_three = statistics(sums_three, pixel_total)
    centred_three = (pre_three - average_three) * inv_three
    residual_in = block_at(pixels, chan_at, out_local, 1).astype(WIDE)
    summed = centred_three * third_norm[0] + third_norm[1] + residual_in
    block_rows = jax.nn.silu(summed)
    block_out = block_rows.astype(LOW).reshape(map_side, map_side, crops_dev, out_local)
    block_out = block_out.transpose(2, 0, 1, 3)
    pooled = jnp.mean(block_rows.reshape(map_area, crops_dev, out_local), axis=0).astype(LOW)
    pooled_dev = lax.all_gather(pooled, "chan", axis=1, tiled=True)
    pooled_all = lax.all_gather(pooled_dev, "dp", axis=0, tiled=True)

    hidden_rows = contract(place_hot, head_all[:, :hid_local], 1, 0).astype(LOW)
    project_rows = contract(
        block_at(place_hot, chan_at, hid_local, 0), head_all[:, hid_local:], 1, 0
    ).astype(LOW)
    hidden_dev = contract(pooled_dev, hidden_rows, 1, 0)
    hidden_pre = spread(hidden_dev.astype(LOW), "dp").reshape(crop_total, hid_local).astype(WIDE)
    head_sums = jnp.stack([jnp.sum(hidden_pre, axis=0), jnp.sum(hidden_pre * hidden_pre, axis=0)])
    average_head, inv_head = statistics(head_sums, crop_total)
    centred_head = (hidden_pre - average_head) * inv_head
    normed_head = centred_head * head_norm[0] + head_norm[1]
    hidden_act = jax.nn.silu(normed_head).astype(LOW)
    project_out = total_hyper(contract(hidden_act, project_rows, 1, 0), "chan")
    inv_len = lax.rsqrt(jnp.sum(project_out * project_out, axis=1, keepdims=True) + 1e-06)
    normed = project_out * inv_len
    normed_low = normed.astype(LOW)
    proto_low = prototypes.astype(LOW).T
    proto_count = proto_low.shape[0]
    prototype_scores = contract(normed_low, proto_low, 1, 1)
    queue_similarity = contract(queue_rows, proto_low, 1, 1)
    queue_len = queue_rows.shape[0]
    slot_index = dp_at * queue_len + jnp.arange(queue_len, dtype=jnp.int32)
    queue_live = (queue_valid > 0) & (slot_index < queue_fill[0])
    queue_codes = jnp.exp(queue_similarity / EPS_SINK) * queue_live[:, None].astype(WIDE)
    queue_first = spread(
        jnp.concatenate([jnp.sum(queue_codes, axis=0), crop_image.astype(WIDE)]), "dp"
    )
    labels = queue_first[:, proto_count:].reshape(crop_total)

    batch_codes = jnp.exp(prototype_scores / EPS_SINK)
    proto_totals = jnp.sum(batch_codes, axis=0) + jnp.sum(queue_first[:, :proto_count], axis=0)

    def live_inverse(row_sums):
        return 1.0 / jnp.where(queue_live[:, None], row_sums, 1.0)

    batch_codes = batch_codes / proto_totals
    queue_codes = queue_codes / proto_totals
    batch_codes = batch_codes / jnp.sum(batch_codes, axis=1, keepdims=True)
    queue_codes = queue_codes * live_inverse(jnp.sum(queue_codes, axis=1, keepdims=True))
    batch_scale = 1.0
    queue_scale = 1.0
    for turn_index in range(1, SINK_ITERS):
        column = 1.0 / (
            jnp.sum(batch_codes * batch_scale, axis=0)
            + total(jnp.sum(queue_codes * queue_scale, axis=0), "dp")
        )
        batch_scale = 1.0 / jnp.sum(batch_codes * column, axis=1, keepdims=True)
        queue_scale = live_inverse(jnp.sum(queue_codes * column, axis=1, keepdims=True))
    codes = batch_codes * column * batch_scale

    crop_index = jnp.arange(crop_total, dtype=jnp.int32)
    same_image = (
        (labels[:, None] == labels[None, :])
        & (crop_index[:, None] != crop_index[None, :])
        & (crop_index[:, None] // crops_dev == crop_index[None, :] // crops_dev)
    )
    others = jnp.sum(same_image.astype(WIDE), axis=1, keepdims=True)
    pair_low = same_image.astype(LOW)
    codes_high = codes.astype(LOW)
    codes_rest = (codes - codes_high.astype(WIDE)).astype(LOW)
    target_rows = (
        contract(pair_low, codes_high, 1, 0) + contract(pair_low, codes_rest, 1, 0)
    ) / jnp.maximum(others, 1.0)
    raw_scores = prototype_scores / SOFTMAX_WARMTH
    log_norm = jax.nn.logsumexp(raw_scores, axis=1, keepdims=True)
    log_likelihoods = raw_scores - log_norm
    per_crop = -jnp.sum(target_rows * log_likelihoods, axis=1)
    target_weight_total = jnp.sum(target_rows, axis=1, keepdims=True)
    score_gradient = (
        LOSS_MULTIPLIER
        / SOFTMAX_WARMTH
        * (jnp.exp(log_likelihoods) * target_weight_total - target_rows)
    ).astype(LOW)
    loss = (jnp.sum(per_crop) / crop_total).reshape(1)
    proto_grad = contract(score_gradient, normed_low, 0, 0).T
    normed_grad = contract(score_gradient, proto_low, 1, 0)
    project_low_grad = (
        inv_len * (normed_grad - normed * jnp.sum(normed * normed_grad, axis=1, keepdims=True))
    ).astype(LOW)
    project_grad = lax.all_gather(
        contract(hidden_act, project_low_grad, 0, 0).astype(LOW), "chan", axis=0, tiled=True
    )
    hidden_grad_act = contract(project_low_grad, project_rows, 1, 1) * silu_slope(normed_head)
    head_grads = jnp.stack(
        [jnp.sum(hidden_grad_act, axis=0), jnp.sum(hidden_grad_act * centred_head, axis=0)]
    )
    head_pre_low = backward_of_norm(
        hidden_grad_act, centred_head, inv_head, head_norm[0], head_grads, crop_total
    ).astype(LOW)
    pooled_terms = contract(block_at(head_pre_low, dp_at, crops_dev, 0), hidden_rows, 1, 1)
    pooled_grad = scatter_relative(relative_blocks(pooled_terms, out_local, 1), "chan", WIDE)

    spread_grad = jnp.broadcast_to(
        pooled_grad[None] / map_area, (map_area, crops_dev, out_local)
    ).reshape(pixel_rows, out_local)
    sum_grad = spread_grad * silu_slope(summed)
    third_grads = total(
        jnp.stack([jnp.sum(sum_grad, axis=0), jnp.sum(sum_grad * centred_three, axis=0)]), "dp"
    )
    third_low = backward_of_norm(
        sum_grad, centred_three, inv_three, third_norm[0], third_grads, pixel_total
    ).astype(LOW)

    def inner_backward(terms, pre_act, average, inv_std, norm):
        parts = [terms[:, r * mid_local : (r + 1) * mid_local] for r in range(chan_count)]
        centred = (pre_act - average) * inv_std
        grad = scatter_relative(parts, "chan") * silu_slope(centred * norm[0] + norm[1])
        sums = total(jnp.stack([jnp.sum(grad, axis=0), jnp.sum(grad * centred, axis=0)]), "dp")
        return backward_of_norm(grad, centred, inv_std, norm[0], sums, pixel_total).astype(LOW), sums

    second_low, second_grads = inner_backward(
        contract(third_low, expand_rel, 1, 0), pre_two, average_two, inv_two, second_norm
    )
    expand_terms = contract(third_low, inner_two, 0, 0).astype(LOW)
    expand_parts = [expand_terms[:, r * mid_local : (r + 1) * mid_local] for r in range(chan_count)]
    expand_grad = jnp.concatenate(
        [expand_parts[0]] + [swap(expand_parts[r], "chan", r) for r in range(1, chan_count)], axis=0
    )
    slot_expand = lax.psum_scatter(
        contract(slot_hot_rel, expand_grad, 1, 0).astype(LOW), "dp", scatter_dimension=0, tiled=True
    ).astype(WIDE)

    maps_two = second_low.reshape(map_side, map_side, crops_dev, mid_local)
    first_terms = lax.conv_general_dilated(
        maps_two,
        spatial_rel[::-1, ::-1].transpose(0, 1, 3, 2),
        (1, 1),
        ((1, 1), (1, 1)),
        dimension_numbers=conv_dims,
        preferred_element_type=WIDE,
    ).reshape(pixel_rows, mid_width)
    spatial_terms = lax.conv_general_dilated(
        maps_one,
        maps_two,
        (1, 1),
        ((1, 1), (1, 1)),
        dimension_numbers=lax.ConvDimensionNumbers((3, 2, 0, 1), (3, 2, 0, 1), (2, 3, 0, 1)),
        preferred_element_type=WIDE,
    ).reshape(9, mid_width, mid_local)
    spatial_grad = jnp.concatenate(relative_blocks(spatial_terms.astype(LOW), mid_local, 1), axis=1)
    slot_spatial = jnp.sum(
        lax.all_to_all(
            spatial_grad.reshape(dp_count, -1, mid_local), "dp", 0, 0
        ).astype(WIDE),
        axis=0,
    )
    first_low, first_grads = inner_backward(
        first_terms, pre_one, average_one, inv_one, first_norm
    )
    first_all = jnp.concatenate(gather_relative(first_low, "chan"), axis=1)
    images_grad = contract(first_all, squeeze_rel, 1, 1) + sum_grad
    images_grad = images_grad.reshape(map_side, map_side, crops_dev, out_local).transpose(2, 0, 1, 3)
    squeeze_grad = contract(pixels, first_low, 0, 0).astype(LOW)
    slot_squeeze = jnp.sum(
        lax.all_to_all(
            contract(slot_hot, squeeze_grad, 1, 0).astype(LOW).reshape(dp_count, slot_local, mid_local),
            "dp",
            0,
            0,
        ).astype(WIDE),
        axis=0,
    )
    slot_project = contract(own_hot, project_grad, 1, 0)
    slot_hidden = contract(contract(pooled_all, own_hot, 1, 1).astype(LOW), head_pre_low, 0, 0)

    norm_gradient = jnp.concatenate([first_grads, second_grads, third_grads, head_grads], axis=1)
    norm_gradient = norm_gradient[::-1].reshape(norm_params.shape)
    step_count = iteration[0].astype(WIDE)

    def step(weight, moment, second, gradient, rate, decay=DECAY_RATE):
        return adamw_step(weight, moment, second, gradient, rate, decay, step_count)

    return (
        block_out,
        loss,
        images_grad,
        *step(squeeze_weight, squeeze_moment, squeeze_second, slot_squeeze, in_width ** (-0.5)),
        *step(
            spatial_weight, spatial_moment, spatial_second, slot_spatial, (9 * mid_width) ** (-0.5)
        ),
        *step(expand_weight, expand_moment, expand_second, slot_expand, mid_width ** (-0.5)),
        *step(hidden_weight, hidden_moment, hidden_second, slot_hidden, in_width ** (-0.5)),
        *step(project_weight, project_moment, project_second, slot_project, hid_width ** (-0.5)),
        *step(prototypes, proto_moment, proto_second, proto_grad, 0.1),
        *step(norm_params, norm_moment, norm_second, norm_gradient, 0.5, 0.0),
    )


def solution(mesh):
    rows, both, whole = P("dp", None), P("dp", "chan"), P()
    maps = P("dp", None, None, "chan")
    norm = P(None, "chan", None)
    placed = (
        (P("dp", None, None, None), P("dp"), whole)
        + (both,) * 12
        + (rows,) * 3
        + (whole,) * 3
        + (norm,) * 3
        + (rows, P("dp"), whole, whole)
    )
    return jax.shard_map(
        local,
        mesh=mesh,
        in_specs=placed,
        out_specs=(maps, whole, maps) + (both,) * 12 + (rows,) * 3 + (whole,) * 3 + (norm,) * 3,
        check_vma=False,
    )
```

```python
import math

import jax
import jax.numpy as jnp
from jax import lax
from jax.experimental import pallas as pl
from jax.experimental.pallas import tpu as pltpu
from jax.sharding import PartitionSpec as P

SINK_ITERS = 3
PRECISE = lax.Precision.HIGHEST
EPS_SINK = 0.05
SOFTMAX_WARMTH = 0.1
LOSS_MULTIPLIER = 256.0
NORM_EPS = 1e-05
BETA_ONE = 0.5
BETA_TWO = 0.5
ADAM_EPS = 1e-08
DECAY_RATE = 1e-06
LOW = jnp.bfloat16
WIDE = jnp.float32


def contract(left, right, left_dim, right_dim):
    return lax.dot_general(
        left, right, (((left_dim,), (right_dim,)), ((), ())), preferred_element_type=WIDE
    )


def silu_slope(value):
    sigma = jax.nn.sigmoid(value)
    return sigma * (1.0 + value * (1.0 - sigma))


def spread(value, axis):
    count = lax.axis_size(axis)
    return lax.all_to_all(jnp.broadcast_to(value[None], (count,) + value.shape), axis, 0, 0)


def total(value, axis):
    return jnp.sum(spread(value, axis).astype(WIDE), axis=0)


def swap(value, axis, bit):
    return lax.ppermute(value, axis, [(at, at ^ bit) for at in range(lax.axis_size(axis))])


def gather_relative(value, axis):
    held = {0: value}
    bit = lax.axis_size(axis) // 2
    while bit:
        keys = sorted(held)
        came = swap(jnp.stack([held[k] for k in keys]), axis, bit)
        held.update({k ^ bit: came[n] for n, k in enumerate(keys)})
        bit //= 2
    return [held[k] for k in range(lax.axis_size(axis))]


def invert_kernel(slots_ref, place_ref, rank_ref):
    count = slots_ref.shape[0]
    channels = place_ref.shape[0] - 128

    def step(at, rank):
        for n in range(16):
            slot = at * 16 + n
            channel = slots_ref[slot]
            place_ref[channel] = slot
            rank_ref[channel] = rank
            rank = rank + jnp.where(channel < channels, 1, 0)
        return rank

    lax.fori_loop(0, count // 16, step, jnp.int32(0))


def slot_of_channel(slot_rows, channels):
    smem = pl.BlockSpec(memory_space=pltpu.SMEM)
    return pl.pallas_call(
        invert_kernel,
        out_shape=[jax.ShapeDtypeStruct((channels + 128,), jnp.int32)] * 2,
        in_specs=[smem],
        out_specs=[smem] * 2,
        name="slot_of_channel",
    )(slot_rows)


def pick_kernel(first, count, place_ref, *refs):
    *blocks, out_ref, wide, picked = refs
    at = 0
    for block in blocks:
        for part in [block.at[k] for k in range(block.shape[0])] if len(block.shape) == 3 else [block]:
            wide[at : at + count, :] = part[first : first + count, :].astype(WIDE)
            at += count

    def step(group, carry):
        for n in range(8):
            row = group * 8 + n
            picked[pl.ds(row, 1), :] = wide[pl.ds(place_ref[row], 1), :]
        return carry

    lax.fori_loop(0, out_ref.shape[0] // 8, step, 0)
    out_ref[...] = picked[...].astype(out_ref.dtype)


def pick_rows(place, blocks, rows, first, count):
    width = blocks[0].shape[-1]
    held = sum(block.size // (width * block.shape[-2]) for block in blocks) * count
    vmem = pl.BlockSpec(memory_space=pltpu.VMEM)
    return pl.pallas_call(
        lambda *refs: pick_kernel(first, count, *refs),
        out_shape=jax.ShapeDtypeStruct((rows, width), LOW),
        in_specs=[pl.BlockSpec(memory_space=pltpu.SMEM)] + [vmem] * len(blocks),
        out_specs=vmem,
        scratch_shapes=[pltpu.VMEM((held, width), WIDE), pltpu.VMEM((rows, width), WIDE)],
        compiler_params=pltpu.CompilerParams(vmem_limit_bytes=32 << 20),
        cost_estimate=pl.CostEstimate(
            flops=0, bytes_accessed=2 * (held + rows) * width, transcendentals=0
        ),
        name="pick_rows",
    )(place, *blocks)


def assemble_kernel(taps, chan_count, rows, at_ref, held_ref, out_ref):
    per_tap = out_ref.shape[0] // taps
    per_chan = per_tap // chan_count
    size = math.gcd(rows, per_chan)
    for row in range(0, out_ref.shape[0], size):
        tap, inner = divmod(row, per_tap)
        chan, rest = divmod(inner, per_chan)
        target = pl.multiple_of((chan ^ at_ref[0]) * per_chan + tap * per_tap + rest, size)
        owner, source = divmod(row, rows)
        out_ref[pl.ds(target, size), :] = held_ref[owner, source : source + size, :]


def assemble(held, at, rows, taps, chan_count):
    vmem = pl.BlockSpec(memory_space=pltpu.VMEM)
    return pl.pallas_call(
        lambda *refs: assemble_kernel(taps, chan_count, rows, *refs),
        out_shape=jax.ShapeDtypeStruct((rows * held.shape[0], held.shape[2]), LOW),
        in_specs=[pl.BlockSpec(memory_space=pltpu.SMEM), vmem],
        out_specs=vmem,
        compiler_params=pltpu.CompilerParams(vmem_limit_bytes=32 << 20),
        cost_estimate=pl.CostEstimate(
            flops=0, bytes_accessed=4 * rows * held.shape[0] * held.shape[2], transcendentals=0
        ),
        name="assemble",
    )(at, held)


def after(value, token):
    return lax.optimization_barrier((value, token))[0]


def scatter_relative(parts, axis, sent=LOW):
    held = dict(enumerate(parts))
    bit = 1
    while bit < lax.axis_size(axis):
        keys = [k for k in sorted(held) if not k & bit]
        came = swap(jnp.stack([held[k | bit].astype(sent) for k in keys]), axis, bit)
        held = {k: held[k] + came[n].astype(WIDE) for n, k in enumerate(keys)}
        bit *= 2
    return held[0]


def total_hyper(value, axis):
    bit = 1
    while bit < lax.axis_size(axis):
        value = value + swap(value, axis, bit)
        bit *= 2
    return value


def block_at(value, index, size, dim):
    return lax.dynamic_slice_in_dim(value, index * size, size, dim)


def statistics(sums, row_total):
    average = sums[0] / row_total
    variance = sums[1] / row_total - average * average
    return average, lax.rsqrt(variance + NORM_EPS)


def backward_of_norm(grad_out, centred, inv_std, gain_row, sums, row_total):
    return gain_row * inv_std * (grad_out - (sums[0] + centred * sums[1]) / row_total)


def adamw_step(weight, moment_one, moment_two, gradient, learn_rate, weight_decay, step_count):
    moment_new = BETA_ONE * moment_one + (1.0 - BETA_ONE) * gradient
    second_new = BETA_TWO * moment_two + (1.0 - BETA_TWO) * gradient * gradient
    fix_one = 1.0 - jnp.power(BETA_ONE, step_count)
    fix_two = 1.0 - jnp.power(BETA_TWO, step_count)
    update = moment_new / fix_one / (jnp.sqrt(second_new / fix_two) + ADAM_EPS)
    return (weight - learn_rate * (update + weight_decay * weight), moment_new, second_new)


def local(
    images,
    crop_image,
    slot_rows,
    squeeze_weight,
    squeeze_moment,
    squeeze_second,
    spatial_weight,
    spatial_moment,
    spatial_second,
    expand_weight,
    expand_moment,
    expand_second,
    hidden_weight,
    hidden_moment,
    hidden_second,
    project_weight,
    project_moment,
    project_second,
    prototypes,
    proto_moment,
    proto_second,
    norm_params,
    norm_moment,
    norm_second,
    queue_rows,
    queue_valid,
    queue_fill,
    iteration,
):
    dp_count = lax.axis_size("dp")
    dp_at = lax.axis_index("dp")
    chan_count = lax.axis_size("chan")
    chan_at = lax.axis_index("chan")
    crops_dev, map_side, _, in_width = images.shape
    map_area = map_side * map_side
    pixel_rows = crops_dev * map_area
    pixel_total = pixel_rows * dp_count
    crop_total = crops_dev * dp_count
    mid_local = squeeze_weight.shape[1]
    hid_local = hidden_weight.shape[1]
    out_local = in_width // chan_count
    slot_local = squeeze_weight.shape[0]
    slot_total = slot_rows.shape[0]
    mid_width = mid_local * chan_count
    hid_width = hid_local * chan_count

    squeeze_came = spread(squeeze_weight.astype(LOW), "dp")
    tap_local = spatial_weight.shape[0]
    convs_all = lax.all_gather(
        jnp.concatenate([spatial_weight.astype(LOW), expand_weight.astype(LOW)], axis=0), "dp"
    )

    channels = jnp.arange(in_width, dtype=jnp.int32)
    used = (slot_rows < in_width).astype(jnp.int32).reshape(dp_count, slot_local)
    loads = jnp.sum(used, axis=1)
    owners = jnp.arange(dp_count, dtype=jnp.int32)
    firsts = jnp.sum(jnp.where(owners[None, :] < owners[:, None], loads[None, :], 0), axis=1)
    own_used = block_at(used, dp_at, 1, 0)[0]
    own_first = block_at(firsts, dp_at, 1, 0)
    own_at = jnp.arange(slot_local, dtype=jnp.int32)
    own_rank = jnp.sum(jnp.where(own_at[None, :] < own_at[:, None], own_used[None, :], 0), axis=1)
    cell = slot_local // dp_count
    share = in_width // dp_count
    target = (own_first + own_rank) % dp_count * cell + own_rank // dp_count
    deal_hot = ((target[None, :] == own_at[:, None]) & (own_used[None, :] > 0)).astype(LOW)
    head_low = jnp.concatenate([hidden_weight.astype(LOW), project_weight.astype(LOW)], axis=1)
    dealt = contract(deal_hot, head_low, 1, 0).astype(LOW)
    dealt = lax.all_to_all(after(dealt, squeeze_came).reshape(dp_count, cell, -1), "dp", 0, 0)
    ranks = (
        jnp.arange(cell, dtype=jnp.int32)[None, :] * dp_count + (dp_at - firsts[:, None]) % dp_count
    )
    share_at = jnp.where(ranks < loads[:, None], (firsts[:, None] + ranks) // dp_count, -1)
    share_at = share_at.reshape(slot_local)
    share_hot = (share_at[None, :] == channels[:share, None]).astype(LOW)
    head_all = lax.all_gather(
        contract(share_hot, dealt.reshape(slot_local, -1), 1, 0).astype(LOW),
        "dp",
        axis=0,
        tiled=True,
    )
    place, rank = slot_of_channel(slot_rows, in_width)
    place_dealt = (rank % dp_count * share + rank // dp_count)[:in_width]

    proto_low = prototypes.astype(LOW).T
    proto_count = proto_low.shape[0]
    queue_similarity = contract(queue_rows, proto_low, 1, 1)
    queue_len = queue_rows.shape[0]
    slot_index = dp_at * queue_len + jnp.arange(queue_len, dtype=jnp.int32)
    queue_live = (queue_valid > 0) & (slot_index < queue_fill[0])
    queue_codes = jnp.exp(queue_similarity / EPS_SINK) * queue_live[:, None].astype(WIDE)
    squeeze_came, queue_codes = lax.optimization_barrier((squeeze_came, queue_codes))
    squeeze_rows = pick_rows(place, [squeeze_came], in_width, 0, slot_local)

    norm_rows = norm_params[:, 0, :]
    first_norm = norm_rows[:, :mid_local]
    second_norm = norm_rows[:, mid_local : 2 * mid_local]
    third_norm = norm_rows[:, 2 * mid_local : 2 * mid_local + out_local]
    head_norm = norm_rows[:, 2 * mid_local + out_local :]

    def inner_layer(pre_act, norm):
        sums = jnp.stack([jnp.sum(pre_act, axis=0), jnp.sum(pre_act * pre_act, axis=0)])
        near = sums[0] / pixel_rows
        raw_all = jnp.concatenate(gather_relative((pre_act - near).astype(LOW), "chan"), axis=1)
        average, inv_std = statistics(total(sums, "dp"), pixel_total)
        scale = inv_std * norm[0]
        affine = jnp.stack([scale, norm[1] - (average - near) * scale])
        affine_all = jnp.concatenate(gather_relative(affine, "chan"), axis=1)
        act_all = jax.nn.silu(raw_all.astype(WIDE) * affine_all[0] + affine_all[1]).astype(LOW)
        return act_all, average, inv_std

    pixels = images.transpose(1, 2, 0, 3).reshape(pixel_rows, in_width)
    pre_one = contract(pixels, squeeze_rows, 1, 0)
    inner_one, average_one, inv_one = inner_layer(pre_one, first_norm)

    def relative_blocks(value, size, dim):
        return [block_at(value, chan_at ^ r, size, dim) for r in range(chan_count)]

    spatial_rel = assemble(
        convs_all, chan_at.astype(jnp.int32).reshape(1), tap_local, 9, chan_count
    ).reshape(3, 3, mid_width, mid_local)
    maps_one = inner_one.reshape(map_side, map_side, crops_dev, mid_width)
    conv_dims = lax.ConvDimensionNumbers((2, 3, 0, 1), (3, 2, 0, 1), (2, 3, 0, 1))
    pre_two = lax.conv_general_dilated(
        maps_one,
        spatial_rel,
        (1, 1),
        ((1, 1), (1, 1)),
        dimension_numbers=conv_dims,
        preferred_element_type=WIDE,
    ).reshape(pixel_rows, mid_local)
    inner_two, average_two, inv_two = inner_layer(pre_two, second_norm)

    expand_rows = pick_rows(place, [convs_all], in_width, tap_local, slot_local)
    pair_sent = relative_blocks(jnp.concatenate([expand_rows, squeeze_rows], axis=1), out_local, 0)
    pair_came = [pair_sent[0]] + [swap(pair_sent[r], "chan", r) for r in range(1, chan_count)]
    expand_rel = jnp.concatenate([pair[:, :mid_local] for pair in pair_came], axis=1)
    squeeze_rel = jnp.concatenate([pair[:, mid_local:] for pair in pair_came], axis=1)
    pre_three = contract(inner_two, expand_rel, 1, 1)
    sent_three = [
        jnp.sum(pre_three, axis=0),
        jnp.sum(pre_three * pre_three, axis=0),
        jnp.sum(queue_codes, axis=0),
        crop_image.astype(WIDE),
    ]
    came_three = spread(jnp.concatenate(sent_three), "dp")
    sums_three = jnp.sum(came_three[:, : 2 * out_local], axis=0).reshape(2, out_local)
    queue_first = came_three[:, 2 * out_local :]
    average_three, inv_three = statistics(sums_three, pixel_total)
    centred_three = (pre_three - average_three) * inv_three
    residual_in = block_at(pixels, chan_at, out_local, 1).astype(WIDE)
    summed = centred_three * third_norm[0] + third_norm[1] + residual_in
    block_rows = jax.nn.silu(summed)
    block_out = block_rows.astype(LOW).reshape(map_side, map_side, crops_dev, out_local)
    block_out = block_out.transpose(2, 0, 1, 3)
    pooled = jnp.mean(block_rows.reshape(map_area, crops_dev, out_local), axis=0).astype(LOW)
    pooled_dev = lax.all_gather(pooled, "chan", axis=1, tiled=True)
    pooled_all = lax.all_gather(pooled_dev, "dp", axis=0, tiled=True)

    dealt_hot = (place_dealt[:, None] == channels[None, :]).astype(LOW)
    hidden_rows = contract(dealt_hot, head_all[:, :hid_local], 1, 0).astype(LOW)
    own_place = block_at(place_dealt, chan_at, hid_local, 0)
    own_dealt_hot = (own_place[:, None] == channels[None, :]).astype(LOW)
    project_rows = contract(own_dealt_hot, head_all[:, hid_local:], 1, 0).astype(LOW)
    hidden_dev = contract(pooled_dev, hidden_rows, 1, 0)
    near_head = jnp.mean(hidden_dev, axis=0, keepdims=True).astype(LOW)
    hidden_sent = (hidden_dev - near_head.astype(WIDE)).astype(LOW)
    hidden_came = spread(jnp.concatenate([hidden_sent, near_head], axis=0), "dp").astype(WIDE)
    hidden_pre = (hidden_came[:, :crops_dev] + hidden_came[:, crops_dev:]).reshape(
        crop_total, hid_local
    )
    head_sums = jnp.stack([jnp.sum(hidden_pre, axis=0), jnp.sum(hidden_pre * hidden_pre, axis=0)])
    average_head, inv_head = statistics(head_sums, crop_total)
    centred_head = (hidden_pre - average_head) * inv_head
    normed_head = centred_head * head_norm[0] + head_norm[1]
    hidden_act = jax.nn.silu(normed_head).astype(LOW)
    project_out = total_hyper(contract(hidden_act, project_rows, 1, 0), "chan")
    inv_len = lax.rsqrt(jnp.sum(project_out * project_out, axis=1, keepdims=True) + 1e-06)
    normed = project_out * inv_len
    normed_low = normed.astype(LOW)
    prototype_scores = contract(normed_low, proto_low, 1, 1)
    labels = queue_first[:, proto_count:].reshape(crop_total)

    batch_codes = jnp.exp(prototype_scores / EPS_SINK)
    proto_totals = jnp.sum(batch_codes, axis=0) + jnp.sum(queue_first[:, :proto_count], axis=0)

    def live_inverse(row_sums):
        return 1.0 / jnp.where(queue_live[:, None], row_sums, 1.0)

    batch_codes = batch_codes / proto_totals
    queue_codes = queue_codes / proto_totals
    batch_codes = batch_codes / jnp.sum(batch_codes, axis=1, keepdims=True)
    queue_codes = queue_codes * live_inverse(jnp.sum(queue_codes, axis=1, keepdims=True))
    batch_scale = 1.0
    queue_scale = 1.0
    for turn_index in range(1, SINK_ITERS):
        column = 1.0 / (
            jnp.sum(batch_codes * batch_scale, axis=0)
            + total(jnp.sum(queue_codes * queue_scale, axis=0), "dp")
        )
        batch_scale = 1.0 / jnp.sum(batch_codes * column, axis=1, keepdims=True)
        queue_scale = live_inverse(jnp.sum(queue_codes * column, axis=1, keepdims=True))
    codes = batch_codes * column * batch_scale

    crop_index = jnp.arange(crop_total, dtype=jnp.int32)
    same_image = (
        (labels[:, None] == labels[None, :])
        & (crop_index[:, None] != crop_index[None, :])
        & (crop_index[:, None] // crops_dev == crop_index[None, :] // crops_dev)
    )
    others = jnp.sum(same_image.astype(WIDE), axis=1, keepdims=True)
    pair_low = same_image.astype(LOW)
    codes_high = codes.astype(LOW)
    codes_rest = (codes - codes_high.astype(WIDE)).astype(LOW)
    target_rows = (
        contract(pair_low, codes_high, 1, 0) + contract(pair_low, codes_rest, 1, 0)
    ) / jnp.maximum(others, 1.0)
    raw_scores = prototype_scores / SOFTMAX_WARMTH
    log_norm = jax.nn.logsumexp(raw_scores, axis=1, keepdims=True)
    log_likelihoods = raw_scores - log_norm
    per_crop = -jnp.sum(target_rows * log_likelihoods, axis=1)
    target_weight_total = jnp.sum(target_rows, axis=1, keepdims=True)
    score_gradient = (
        LOSS_MULTIPLIER
        / SOFTMAX_WARMTH
        * (jnp.exp(log_likelihoods) * target_weight_total - target_rows)
    ).astype(LOW)
    loss = (jnp.sum(per_crop) / crop_total).reshape(1)
    normed_grad = contract(score_gradient, proto_low, 1, 0)
    project_low_grad = (
        inv_len * (normed_grad - normed * jnp.sum(normed * normed_grad, axis=1, keepdims=True))
    ).astype(LOW)
    hidden_grad_act = contract(project_low_grad, project_rows, 1, 1) * silu_slope(normed_head)
    head_grads = jnp.stack(
        [jnp.sum(hidden_grad_act, axis=0), jnp.sum(hidden_grad_act * centred_head, axis=0)]
    )
    head_pre_low = backward_of_norm(
        hidden_grad_act, centred_head, inv_head, head_norm[0], head_grads, crop_total
    ).astype(LOW)
    pooled_terms = contract(block_at(head_pre_low, dp_at, crops_dev, 0), hidden_rows, 1, 1)
    pooled_grad = scatter_relative(relative_blocks(pooled_terms, out_local, 1), "chan", WIDE)

    spread_grad = jnp.broadcast_to(
        pooled_grad[None] / map_area, (map_area, crops_dev, out_local)
    ).reshape(pixel_rows, out_local)
    sum_grad = spread_grad * silu_slope(summed)
    third_grads = total(
        jnp.stack([jnp.sum(sum_grad, axis=0), jnp.sum(sum_grad * centred_three, axis=0)]), "dp"
    )
    third_low = backward_of_norm(
        sum_grad, centred_three, inv_three, third_norm[0], third_grads, pixel_total
    ).astype(LOW)

    def inner_backward(terms, pre_act, average, inv_std, norm, total):
        parts = [terms[:, r * mid_local : (r + 1) * mid_local] for r in range(chan_count)]
        centred = (pre_act - average) * inv_std
        grad = scatter_relative(parts, "chan") * silu_slope(centred * norm[0] + norm[1])
        sums = total(jnp.stack([jnp.sum(grad, axis=0), jnp.sum(grad * centred, axis=0)]), "dp")
        return backward_of_norm(grad, centred, inv_std, norm[0], sums, pixel_total).astype(LOW), sums

    second_low, second_grads = inner_backward(
        contract(third_low, expand_rel, 1, 0), pre_two, average_two, inv_two, second_norm, total
    )
    expand_terms = contract(third_low, inner_two, 0, 0).astype(LOW)
    expand_parts = [expand_terms[:, r * mid_local : (r + 1) * mid_local] for r in range(chan_count)]
    expand_grad = jnp.concatenate(
        [expand_parts[0]] + [swap(expand_parts[r], "chan", r) for r in range(1, chan_count)], axis=0
    )

    def slot_terms(grad_rows, turned):
        slot_hot = ((slot_rows ^ (turned * out_local))[:, None] == channels[None, :]).astype(LOW)
        terms = contract(slot_hot, grad_rows, 1, 0).astype(LOW)
        return terms.reshape(dp_count, slot_local, mid_local)

    expand_came = lax.all_to_all(slot_terms(expand_grad, chan_at), "dp", 0, 0)

    maps_two = second_low.reshape(map_side, map_side, crops_dev, mid_local)
    first_terms = lax.conv_general_dilated(
        maps_two,
        spatial_rel[::-1, ::-1].transpose(0, 1, 3, 2),
        (1, 1),
        ((1, 1), (1, 1)),
        dimension_numbers=conv_dims,
        preferred_element_type=WIDE,
    ).reshape(pixel_rows, mid_width)
    spatial_terms = lax.conv_general_dilated(
        maps_one,
        maps_two,
        (1, 1),
        ((1, 1), (1, 1)),
        dimension_numbers=lax.ConvDimensionNumbers((3, 2, 0, 1), (3, 2, 0, 1), (2, 3, 0, 1)),
        preferred_element_type=WIDE,
    ).reshape(9, mid_width, mid_local)
    spatial_grad = jnp.concatenate(relative_blocks(spatial_terms.astype(LOW), mid_local, 1), axis=1)
    spatial_grad, first_terms = lax.optimization_barrier((spatial_grad, first_terms))
    spatial_came = lax.all_to_all(spatial_grad.reshape(dp_count, -1, mid_local), "dp", 0, 0)
    first_low, first_grads = inner_backward(
        first_terms, pre_one, average_one, inv_one, first_norm, total_hyper
    )
    first_all = jnp.concatenate(gather_relative(first_low, "chan"), axis=1)
    images_grad = contract(first_all, squeeze_rel, 1, 1) + sum_grad
    images_grad = images_grad.reshape(map_side, map_side, crops_dev, out_local).transpose(2, 0, 1, 3)
    squeeze_grad = contract(pixels, first_low, 0, 0).astype(LOW)
    squeeze_terms = slot_terms(squeeze_grad, 0)
    squeeze_sum = lax.all_to_all(squeeze_terms, "dp", 0, 0)

    score_late, hidden_late, head_late, spatial_late, expand_late = lax.optimization_barrier(
        (score_gradient, hidden_act, head_pre_low, spatial_came, expand_came, squeeze_terms)
    )[:5]
    slot_squeeze, slot_spatial, slot_expand = [
        jnp.sum(came.astype(WIDE), axis=0) for came in (squeeze_sum, spatial_late, expand_late)
    ]
    proto_grad = contract(score_late, normed_low, 0, 0).T
    project_grad = jnp.concatenate(
        gather_relative(contract(hidden_late, project_low_grad, 0, 0).astype(LOW), "chan")
    )
    own_slots = block_at(slot_rows, dp_at, slot_local, 0)
    own_hot = (own_slots[:, None] == channels[None, :]).astype(LOW)
    turned_hot = ((own_slots ^ (chan_at * hid_local))[:, None] == channels[None, :]).astype(LOW)
    slot_project = contract(turned_hot, project_grad, 1, 0)
    slot_hidden = contract(contract(pooled_all, own_hot, 1, 1).astype(LOW), head_late, 0, 0)

    norm_gradient = jnp.concatenate([first_grads, second_grads, third_grads, head_grads], axis=1)
    norm_gradient = norm_gradient[::-1].reshape(norm_params.shape)
    step_count = iteration[0].astype(WIDE)

    def step(weight, moment, second, gradient, rate, decay=DECAY_RATE):
        return adamw_step(weight, moment, second, gradient, rate, decay, step_count)

    return (
        block_out,
        loss,
        images_grad,
        *step(squeeze_weight, squeeze_moment, squeeze_second, slot_squeeze, in_width ** (-0.5)),
        *step(
            spatial_weight, spatial_moment, spatial_second, slot_spatial, (9 * mid_width) ** (-0.5)
        ),
        *step(expand_weight, expand_moment, expand_second, slot_expand, mid_width ** (-0.5)),
        *step(hidden_weight, hidden_moment, hidden_second, slot_hidden, in_width ** (-0.5)),
        *step(project_weight, project_moment, project_second, slot_project, hid_width ** (-0.5)),
        *step(prototypes, proto_moment, proto_second, proto_grad, 0.1),
        *step(norm_params, norm_moment, norm_second, norm_gradient, 0.5, 0.0),
    )


def solution(mesh):
    rows, both, whole = P("dp", None), P("dp", "chan"), P()
    maps = P("dp", None, None, "chan")
    norm = P(None, "chan", None)
    placed = (
        (P("dp", None, None, None), P("dp"), whole)
        + (both,) * 12
        + (rows,) * 3
        + (whole,) * 3
        + (norm,) * 3
        + (rows, P("dp"), whole, whole)
    )
    return jax.shard_map(
        local,
        mesh=mesh,
        in_specs=placed,
        out_specs=(maps, whole, maps) + (both,) * 12 + (rows,) * 3 + (whole,) * 3 + (norm,) * 3,
        check_vma=False,
    )
```

```python
import math

import jax
import jax.numpy as jnp
from jax import lax
from jax.experimental import pallas as pl
from jax.experimental.pallas import tpu as pltpu
from jax.sharding import PartitionSpec as P

SINK_ITERS = 3
PRECISE = lax.Precision.HIGHEST
EPS_SINK = 0.05
SOFTMAX_WARMTH = 0.1
LOSS_MULTIPLIER = 256.0
NORM_EPS = 1e-05
BETA_ONE = 0.5
BETA_TWO = 0.5
ADAM_EPS = 1e-08
DECAY_RATE = 1e-06
LOW = jnp.bfloat16
WIDE = jnp.float32


def contract(left, right, left_dim, right_dim):
    return lax.dot_general(
        left, right, (((left_dim,), (right_dim,)), ((), ())), preferred_element_type=WIDE
    )


def silu_slope(value):
    sigma = jax.nn.sigmoid(value)
    return sigma * (1.0 + value * (1.0 - sigma))


def spread(value, axis):
    count = lax.axis_size(axis)
    return lax.all_to_all(jnp.broadcast_to(value[None], (count,) + value.shape), axis, 0, 0)


def total(value, axis):
    return jnp.sum(spread(value, axis).astype(WIDE), axis=0)


def swap(value, axis, bit):
    return lax.ppermute(value, axis, [(at, at ^ bit) for at in range(lax.axis_size(axis))])


def gather_relative(value, axis):
    held = {0: value}
    bit = lax.axis_size(axis) // 2
    while bit:
        keys = sorted(held)
        came = swap(jnp.stack([held[k] for k in keys]), axis, bit)
        held.update({k ^ bit: came[n] for n, k in enumerate(keys)})
        bit //= 2
    return [held[k] for k in range(lax.axis_size(axis))]


def invert_kernel(slots_ref, place_ref, rank_ref):
    count = slots_ref.shape[0]
    channels = place_ref.shape[0] - 128

    def step(at, rank):
        for n in range(16):
            slot = at * 16 + n
            channel = slots_ref[slot]
            place_ref[channel] = slot
            rank_ref[channel] = rank
            rank = rank + jnp.where(channel < channels, 1, 0)
        return rank

    lax.fori_loop(0, count // 16, step, jnp.int32(0))


def slot_of_channel(slot_rows, channels):
    smem = pl.BlockSpec(memory_space=pltpu.SMEM)
    return pl.pallas_call(
        invert_kernel,
        out_shape=[jax.ShapeDtypeStruct((channels + 128,), jnp.int32)] * 2,
        in_specs=[smem],
        out_specs=[smem] * 2,
        name="slot_of_channel",
    )(slot_rows)


def pick_kernel(first, count, place_ref, turn_ref, *refs):
    *blocks, out_ref, wide, picked = refs
    at = 0
    for block in blocks:
        for part in [block.at[k] for k in range(block.shape[0])] if len(block.shape) == 3 else [block]:
            wide[at : at + count, :] = part[first : first + count, :].astype(WIDE)
            at += count

    def step(group, carry):
        for n in range(8):
            row = group * 8 + n
            picked[pl.ds(row, 1), :] = wide[pl.ds(place_ref[(group * 8 ^ turn_ref[0]) + n], 1), :]
        return carry

    lax.fori_loop(0, out_ref.shape[0] // 8, step, 0)
    out_ref[...] = picked[...].astype(out_ref.dtype)


def pick_rows(place, turn, blocks, rows, first, count):
    width = blocks[0].shape[-1]
    held = sum(block.size // (width * block.shape[-2]) for block in blocks) * count
    vmem = pl.BlockSpec(memory_space=pltpu.VMEM)
    return pl.pallas_call(
        lambda *refs: pick_kernel(first, count, *refs),
        out_shape=jax.ShapeDtypeStruct((rows, width), LOW),
        in_specs=[pl.BlockSpec(memory_space=pltpu.SMEM)] * 2 + [vmem] * len(blocks),
        out_specs=vmem,
        scratch_shapes=[pltpu.VMEM((held, width), WIDE), pltpu.VMEM((rows, width), WIDE)],
        compiler_params=pltpu.CompilerParams(vmem_limit_bytes=32 << 20),
        cost_estimate=pl.CostEstimate(
            flops=0, bytes_accessed=2 * (held + rows) * width, transcendentals=0
        ),
        name="pick_rows",
    )(place, turn, *blocks)


def assemble_kernel(taps, chan_count, rows, at_ref, held_ref, out_ref):
    per_tap = out_ref.shape[0] // taps
    per_chan = per_tap // chan_count
    size = math.gcd(rows, per_chan)
    for row in range(0, out_ref.shape[0], size):
        tap, inner = divmod(row, per_tap)
        chan, rest = divmod(inner, per_chan)
        target = pl.multiple_of((chan ^ at_ref[0]) * per_chan + tap * per_tap + rest, size)
        owner, source = divmod(row, rows)
        out_ref[pl.ds(target, size), :] = held_ref[owner, source : source + size, :]


def assemble(held, at, rows, taps, chan_count):
    vmem = pl.BlockSpec(memory_space=pltpu.VMEM)
    return pl.pallas_call(
        lambda *refs: assemble_kernel(taps, chan_count, rows, *refs),
        out_shape=jax.ShapeDtypeStruct((rows * held.shape[0], held.shape[2]), LOW),
        in_specs=[pl.BlockSpec(memory_space=pltpu.SMEM), vmem],
        out_specs=vmem,
        compiler_params=pltpu.CompilerParams(vmem_limit_bytes=32 << 20),
        cost_estimate=pl.CostEstimate(
            flops=0, bytes_accessed=4 * rows * held.shape[0] * held.shape[2], transcendentals=0
        ),
        name="assemble",
    )(at, held)


def deal_kernel(taps, chan_count, order, at_ref, terms_ref, out_ref):
    rows = out_ref.shape[1]
    per_tap = terms_ref.shape[0] // taps
    per_chan = per_tap // chan_count
    size = math.gcd(rows, per_chan)
    for n, r in enumerate(order):
        for start in range(0, rows, size):
            row = (at_ref[0] ^ r) * rows + start
            tap, inner = row // per_tap, row % per_tap
            chan, rest = inner // per_chan, inner % per_chan
            source = tap * per_tap + (chan ^ at_ref[1]) * per_chan + rest
            source = pl.multiple_of(source, size)
            out_ref[n, start : start + size, :] = terms_ref[pl.ds(source, size), :]


def deal_rows(terms, at, owners, taps, chan_count):
    order = send_order(owners)
    vmem = pl.BlockSpec(memory_space=pltpu.VMEM)
    return pl.pallas_call(
        lambda *refs: deal_kernel(taps, chan_count, order, *refs),
        out_shape=jax.ShapeDtypeStruct((owners, terms.shape[0] // owners, terms.shape[1]), LOW),
        in_specs=[pl.BlockSpec(memory_space=pltpu.SMEM), vmem],
        out_specs=vmem,
        compiler_params=pltpu.CompilerParams(vmem_limit_bytes=32 << 20),
        cost_estimate=pl.CostEstimate(flops=0, bytes_accessed=4 * terms.size, transcendentals=0),
        name="deal_rows",
    )(at, terms)


def after(value, token):
    return lax.optimization_barrier((value, token))[0]


def join(*values):
    return lax.optimization_barrier(values)


def scatter_relative(parts, axis, sent=LOW):
    held = dict(enumerate(parts))
    bit = 1
    while bit < lax.axis_size(axis):
        keys = [k for k in sorted(held) if not k & bit]
        came = swap(jnp.stack([held[k | bit].astype(sent) for k in keys]), axis, bit)
        held = {k: held[k] + came[n].astype(WIDE) for n, k in enumerate(keys)}
        bit *= 2
    return held[0]


def send_order(count):
    low = max(count // 4, 1)
    order = list(range(0, count, low))
    bit = low // 2
    while bit:
        order = order + [r | bit for r in order]
        bit //= 2
    return order


def scatter_staged(blocks, axis):
    count = lax.axis_size(axis)
    low = max(count // 4, 1)
    held = blocks
    bit = 1
    while bit < low:
        half = held.shape[0] // 2
        came = swap(held[half:], axis, bit)
        held = (held[:half].astype(WIDE) + came.astype(WIDE)).astype(LOW)
        bit *= 2
    came = [swap(held[n], axis, n * low) for n in range(1, held.shape[0])]
    return held[0], came


def wide_sum(terms):
    kept, came = terms
    result = kept.astype(WIDE)
    for value in came:
        result = result + value.astype(WIDE)
    return result


def total_hyper(value, axis):
    bit = 1
    while bit < lax.axis_size(axis):
        value = value + swap(value, axis, bit)
        bit *= 2
    return value


def block_at(value, index, size, dim):
    return lax.dynamic_slice_in_dim(value, index * size, size, dim)


def statistics(sums, row_total):
    average = sums[0] / row_total
    variance = sums[1] / row_total - average * average
    return average, lax.rsqrt(variance + NORM_EPS)


def backward_of_norm(grad_out, centred, inv_std, gain_row, sums, row_total):
    return gain_row * inv_std * (grad_out - (sums[0] + centred * sums[1]) / row_total)


def adamw_step(weight, moment_one, moment_two, gradient, learn_rate, weight_decay, step_count):
    moment_new = BETA_ONE * moment_one + (1.0 - BETA_ONE) * gradient
    second_new = BETA_TWO * moment_two + (1.0 - BETA_TWO) * gradient * gradient
    fix_one = 1.0 - jnp.power(BETA_ONE, step_count)
    fix_two = 1.0 - jnp.power(BETA_TWO, step_count)
    update = moment_new / fix_one / (jnp.sqrt(second_new / fix_two) + ADAM_EPS)
    return (weight - learn_rate * (update + weight_decay * weight), moment_new, second_new)


def local(
    images,
    crop_image,
    slot_rows,
    squeeze_weight,
    squeeze_moment,
    squeeze_second,
    spatial_weight,
    spatial_moment,
    spatial_second,
    expand_weight,
    expand_moment,
    expand_second,
    hidden_weight,
    hidden_moment,
    hidden_second,
    project_weight,
    project_moment,
    project_second,
    prototypes,
    proto_moment,
    proto_second,
    norm_params,
    norm_moment,
    norm_second,
    queue_rows,
    queue_valid,
    queue_fill,
    iteration,
):
    dp_count = lax.axis_size("dp")
    dp_at = lax.axis_index("dp")
    chan_count = lax.axis_size("chan")
    chan_at = lax.axis_index("chan")
    crops_dev, map_side, _, in_width = images.shape
    map_area = map_side * map_side
    pixel_rows = crops_dev * map_area
    pixel_total = pixel_rows * dp_count
    crop_total = crops_dev * dp_count
    mid_local = squeeze_weight.shape[1]
    hid_local = hidden_weight.shape[1]
    out_local = in_width // chan_count
    slot_local = squeeze_weight.shape[0]
    slot_total = slot_rows.shape[0]
    mid_width = mid_local * chan_count
    hid_width = hid_local * chan_count

    squeeze_came = spread(squeeze_weight.astype(LOW), "dp")
    tap_local = spatial_weight.shape[0]
    convs_all = lax.all_gather(
        jnp.concatenate([spatial_weight.astype(LOW), expand_weight.astype(LOW)], axis=0), "dp"
    )

    channels = jnp.arange(in_width, dtype=jnp.int32)
    used = (slot_rows < in_width).astype(jnp.int32).reshape(dp_count, slot_local)
    loads = jnp.sum(used, axis=1)
    owners = jnp.arange(dp_count, dtype=jnp.int32)
    firsts = jnp.sum(jnp.where(owners[None, :] < owners[:, None], loads[None, :], 0), axis=1)
    own_used = block_at(used, dp_at, 1, 0)[0]
    own_first = block_at(firsts, dp_at, 1, 0)
    own_at = jnp.arange(slot_local, dtype=jnp.int32)
    own_rank = jnp.sum(jnp.where(own_at[None, :] < own_at[:, None], own_used[None, :], 0), axis=1)
    cell = slot_local // dp_count
    share = in_width // dp_count
    target = (own_first + own_rank) % dp_count * cell + own_rank // dp_count
    deal_hot = ((target[None, :] == own_at[:, None]) & (own_used[None, :] > 0)).astype(LOW)
    head_low = jnp.concatenate([hidden_weight.astype(LOW), project_weight.astype(LOW)], axis=1)
    dealt = contract(deal_hot, head_low, 1, 0).astype(LOW)
    ranks = (
        jnp.arange(cell, dtype=jnp.int32)[None, :] * dp_count + (dp_at - firsts[:, None]) % dp_count
    )
    share_at = jnp.where(ranks < loads[:, None], (firsts[:, None] + ranks) // dp_count, -1)
    share_at = share_at.reshape(slot_local)
    place, rank = slot_of_channel(slot_rows, in_width)
    slot_blocks = slot_rows.reshape(dp_count, slot_local)
    slot_sent = jnp.concatenate(
        [lax.dynamic_index_in_dim(slot_blocks, dp_at ^ r, 0, False) for r in send_order(dp_count)]
    )
    own_slots = slot_sent[:slot_local]
    place_dealt = (rank % dp_count * share + rank // dp_count)[:in_width]

    proto_low = prototypes.astype(LOW).T
    proto_count = proto_low.shape[0]
    queue_similarity = contract(queue_rows, proto_low, 1, 1)
    queue_len = queue_rows.shape[0]
    slot_index = dp_at * queue_len + jnp.arange(queue_len, dtype=jnp.int32)
    queue_live = (queue_valid > 0) & (slot_index < queue_fill[0])
    queue_codes = jnp.exp(queue_similarity / EPS_SINK) * queue_live[:, None].astype(WIDE)
    squeeze_came, queue_codes, slot_sent = join(squeeze_came, queue_codes, slot_sent)
    straight = jnp.zeros((1,), jnp.int32)
    turned = (chan_at * out_local).astype(jnp.int32).reshape(1)
    squeeze_rows = pick_rows(place, straight, [squeeze_came], in_width, 0, slot_local)

    norm_rows = norm_params[:, 0, :]
    first_norm = norm_rows[:, :mid_local]
    second_norm = norm_rows[:, mid_local : 2 * mid_local]
    third_norm = norm_rows[:, 2 * mid_local : 2 * mid_local + out_local]
    head_norm = norm_rows[:, 2 * mid_local + out_local :]

    def inner_layer(pre_act, norm, token=None):
        sums = jnp.stack([jnp.sum(pre_act, axis=0), jnp.sum(pre_act * pre_act, axis=0)])
        if token is not None:
            sums = after(sums, token)
        near = sums[0] / pixel_rows
        raw_all = jnp.concatenate(gather_relative((pre_act - near).astype(LOW), "chan"), axis=1)
        average, inv_std = statistics(total(sums, "dp"), pixel_total)
        scale = inv_std * norm[0]
        affine = jnp.stack([scale, norm[1] - (average - near) * scale])
        affine_all = jnp.concatenate(gather_relative(affine, "chan"), axis=1)
        act_all = jax.nn.silu(raw_all.astype(WIDE) * affine_all[0] + affine_all[1]).astype(LOW)
        return act_all, average, inv_std

    step_count = iteration[0].astype(WIDE)

    def step(weight, moment, second, gradient, rate, decay=DECAY_RATE):
        return adamw_step(weight, moment, second, gradient, rate, decay, step_count)

    pixels = images.transpose(1, 2, 0, 3).reshape(pixel_rows, in_width)
    pre_one = contract(pixels, squeeze_rows, 1, 0)
    inner_one, average_one, inv_one = inner_layer(pre_one, first_norm)
    dealt = lax.all_to_all(after(dealt, average_one).reshape(dp_count, cell, -1), "dp", 0, 0)
    def relative_blocks(value, size, dim):
        return [block_at(value, chan_at ^ r, size, dim) for r in range(chan_count)]

    spatial_rel = assemble(
        convs_all, chan_at.astype(jnp.int32).reshape(1), tap_local, 9, chan_count
    ).reshape(3, 3, mid_width, mid_local)
    maps_one = inner_one.reshape(map_side, map_side, crops_dev, mid_width)
    conv_dims = lax.ConvDimensionNumbers((2, 3, 0, 1), (3, 2, 0, 1), (2, 3, 0, 1))
    pre_two = lax.conv_general_dilated(
        maps_one,
        spatial_rel,
        (1, 1),
        ((1, 1), (1, 1)),
        dimension_numbers=conv_dims,
        preferred_element_type=WIDE,
    ).reshape(pixel_rows, mid_local)
    pre_two, dealt = join(pre_two, dealt)
    share_hot = (share_at[None, :] == channels[:share, None]).astype(LOW)
    head_all = lax.all_gather(
        contract(share_hot, dealt.reshape(slot_local, -1), 1, 0).astype(LOW),
        "dp",
        axis=0,
        tiled=True,
    )

    inner_two, average_two, inv_two = inner_layer(pre_two, second_norm)

    expand_rows = pick_rows(place, turned, [convs_all], in_width, tap_local, slot_local)

    def swap_blocks(blocks):
        return jnp.concatenate(
            [blocks[0]] + [swap(blocks[r], "chan", r) for r in range(1, chan_count)], axis=1
        )

    expand_rel = swap_blocks(
        [expand_rows[r * out_local : (r + 1) * out_local] for r in range(chan_count)]
    )
    squeeze_rel = swap_blocks(relative_blocks(squeeze_rows, out_local, 0))
    pre_three = contract(inner_two, expand_rel, 1, 1)
    sent_three = [
        jnp.sum(pre_three, axis=0),
        jnp.sum(pre_three * pre_three, axis=0),
        jnp.sum(queue_codes, axis=0),
        crop_image.astype(WIDE),
    ]
    came_three = spread(jnp.concatenate(sent_three), "dp")
    sums_three = jnp.sum(came_three[:, : 2 * out_local], axis=0).reshape(2, out_local)
    queue_first = came_three[:, 2 * out_local :]
    average_three, inv_three = statistics(sums_three, pixel_total)
    centred_three = (pre_three - average_three) * inv_three
    residual_in = block_at(pixels, chan_at, out_local, 1).astype(WIDE)
    summed = centred_three * third_norm[0] + third_norm[1] + residual_in
    block_rows = jax.nn.silu(summed)
    block_out = block_rows.astype(LOW).reshape(map_side, map_side, crops_dev, out_local)
    block_out = block_out.transpose(2, 0, 1, 3)
    pooled = jnp.mean(block_rows.reshape(map_area, crops_dev, out_local), axis=0).astype(LOW)
    pooled_dev = lax.all_gather(pooled, "chan", axis=1, tiled=True)
    pooled_all = lax.all_gather(pooled_dev, "dp", axis=0, tiled=True)

    dealt_hot = (place_dealt[:, None] == channels[None, :]).astype(LOW)
    pooled_dealt = contract(pooled_dev, dealt_hot, 1, 0).astype(LOW)
    pooled_dealt, head_all = join(pooled_dealt, head_all)
    hidden_dev = contract(pooled_dealt, head_all[:, :hid_local], 1, 0)
    own_place = block_at(place_dealt, chan_at, hid_local, 0)
    own_dealt_hot = (own_place[:, None] == channels[None, :]).astype(LOW)
    project_rows = contract(own_dealt_hot, head_all[:, hid_local:], 1, 0).astype(LOW)
    near_head = jnp.mean(hidden_dev, axis=0, keepdims=True).astype(LOW)
    hidden_sent = (hidden_dev - near_head.astype(WIDE)).astype(LOW)
    hidden_came = spread(jnp.concatenate([hidden_sent, near_head], axis=0), "dp")
    hidden_rows = contract(
        (after(place_dealt, hidden_dev)[:, None] == channels[None, :]).astype(LOW),
        head_all[:, :hid_local],
        1,
        0,
    ).astype(LOW)
    hidden_came, hidden_rows = join(hidden_came, hidden_rows)
    hidden_pre = (
        hidden_came[:, :crops_dev].astype(WIDE) + hidden_came[:, crops_dev:].astype(WIDE)
    ).reshape(
        crop_total, hid_local
    )
    head_sums = jnp.stack([jnp.sum(hidden_pre, axis=0), jnp.sum(hidden_pre * hidden_pre, axis=0)])
    average_head, inv_head = statistics(head_sums, crop_total)
    centred_head = (hidden_pre - average_head) * inv_head
    normed_head = centred_head * head_norm[0] + head_norm[1]
    hidden_act = jax.nn.silu(normed_head).astype(LOW)
    project_out = total_hyper(contract(hidden_act, project_rows, 1, 0), "chan")
    inv_len = lax.rsqrt(jnp.sum(project_out * project_out, axis=1, keepdims=True) + 1e-06)
    normed = project_out * inv_len
    normed_low = normed.astype(LOW)
    prototype_scores = contract(normed_low, proto_low, 1, 1)
    labels = queue_first[:, proto_count:].reshape(crop_total)

    batch_codes = jnp.exp(prototype_scores / EPS_SINK)
    proto_totals = jnp.sum(batch_codes, axis=0) + jnp.sum(queue_first[:, :proto_count], axis=0)

    def live_inverse(row_sums):
        return 1.0 / jnp.where(queue_live[:, None], row_sums, 1.0)

    batch_codes = batch_codes / proto_totals
    queue_codes = queue_codes / proto_totals
    batch_codes = batch_codes / jnp.sum(batch_codes, axis=1, keepdims=True)
    queue_codes = queue_codes * live_inverse(jnp.sum(queue_codes, axis=1, keepdims=True))
    batch_scale = 1.0
    queue_scale = 1.0
    for turn_index in range(1, SINK_ITERS):
        column = 1.0 / (
            jnp.sum(batch_codes * batch_scale, axis=0)
            + total(jnp.sum(queue_codes * queue_scale, axis=0), "dp")
        )
        batch_scale = 1.0 / jnp.sum(batch_codes * column, axis=1, keepdims=True)
        queue_scale = live_inverse(jnp.sum(queue_codes * column, axis=1, keepdims=True))
    codes, pooled_all = lax.optimization_barrier(
        (batch_codes * column * batch_scale, pooled_all)
    )

    crop_index = jnp.arange(crop_total, dtype=jnp.int32)
    same_image = (
        (labels[:, None] == labels[None, :])
        & (crop_index[:, None] != crop_index[None, :])
        & (crop_index[:, None] // crops_dev == crop_index[None, :] // crops_dev)
    )
    others = jnp.sum(same_image.astype(WIDE), axis=1, keepdims=True)
    pair_low = same_image.astype(LOW)
    codes_high = codes.astype(LOW)
    codes_rest = (codes - codes_high.astype(WIDE)).astype(LOW)
    target_rows = (
        contract(pair_low, codes_high, 1, 0) + contract(pair_low, codes_rest, 1, 0)
    ) / jnp.maximum(others, 1.0)
    raw_scores = prototype_scores / SOFTMAX_WARMTH
    log_norm = jax.nn.logsumexp(raw_scores, axis=1, keepdims=True)
    log_likelihoods = raw_scores - log_norm
    per_crop = -jnp.sum(target_rows * log_likelihoods, axis=1)
    target_weight_total = jnp.sum(target_rows, axis=1, keepdims=True)
    score_gradient = (
        LOSS_MULTIPLIER
        / SOFTMAX_WARMTH
        * (jnp.exp(log_likelihoods) * target_weight_total - target_rows)
    ).astype(LOW)
    loss = (jnp.sum(per_crop) / crop_total).reshape(1)
    normed_grad = contract(score_gradient, proto_low, 1, 0)
    project_low_grad = (
        inv_len * (normed_grad - normed * jnp.sum(normed * normed_grad, axis=1, keepdims=True))
    ).astype(LOW)
    hidden_grad_act = contract(project_low_grad, project_rows, 1, 1) * silu_slope(normed_head)
    head_grads = jnp.stack(
        [jnp.sum(hidden_grad_act, axis=0), jnp.sum(hidden_grad_act * centred_head, axis=0)]
    )
    head_pre_low = backward_of_norm(
        hidden_grad_act, centred_head, inv_head, head_norm[0], head_grads, crop_total
    ).astype(LOW)
    pooled_terms = contract(block_at(head_pre_low, dp_at, crops_dev, 0), hidden_rows, 1, 1)
    pooled_grad = scatter_relative(relative_blocks(pooled_terms, out_local, 1), "chan", WIDE)

    spread_grad = jnp.broadcast_to(
        pooled_grad[None] / map_area, (map_area, crops_dev, out_local)
    ).reshape(pixel_rows, out_local)
    sum_grad = spread_grad * silu_slope(summed)
    third_grads = total(
        jnp.stack([jnp.sum(sum_grad, axis=0), jnp.sum(sum_grad * centred_three, axis=0)]), "dp"
    )
    third_low = backward_of_norm(
        sum_grad, centred_three, inv_three, third_norm[0], third_grads, pixel_total
    ).astype(LOW)

    def column_parts(terms):
        return [terms[:, r * mid_local : (r + 1) * mid_local] for r in range(chan_count)]

    def inner_sums(summed_terms, pre_act, average, inv_std, norm):
        centred = (pre_act - average) * inv_std
        grad = summed_terms * silu_slope(centred * norm[0] + norm[1])
        sums = jnp.stack([jnp.sum(grad, axis=0), jnp.sum(grad * centred, axis=0)])
        return grad, centred, sums

    def slot_terms(grad_rows, turned):
        slot_hot = ((slot_sent ^ (turned * out_local))[:, None] == channels[None, :]).astype(LOW)
        terms = contract(slot_hot, grad_rows, 1, 0).astype(LOW)
        return terms.reshape(dp_count, slot_local, mid_local)

    second_sum = scatter_relative(column_parts(contract(third_low, expand_rel, 1, 0)), "chan")
    expand_terms = contract(third_low, inner_two, 0, 0).astype(LOW)
    proto_grad = contract(score_gradient, normed_low, 0, 0).T
    proto_new = step(prototypes, proto_moment, proto_second, proto_grad, 0.1)
    second_sum, expand_terms, *proto_new = join(second_sum, expand_terms, *proto_new)
    grad_two, centred_two, second_sums = inner_sums(
        second_sum, pre_two, average_two, inv_two, second_norm
    )
    expand_parts = column_parts(expand_terms)
    expand_grad = jnp.concatenate(
        [expand_parts[0]] + [swap(expand_parts[r], "chan", r) for r in range(1, chan_count)], axis=0
    )
    slot_expand = slot_terms(expand_grad, chan_at)
    second_grads, slot_expand = join(total(second_sums, "dp"), slot_expand)
    expand_came = scatter_staged(slot_expand, "dp")
    second_low = backward_of_norm(
        grad_two, centred_two, inv_two, second_norm[0], second_grads, pixel_total
    ).astype(LOW)
    maps_two = second_low.reshape(map_side, map_side, crops_dev, mid_local)
    first_terms = lax.conv_general_dilated(
        maps_two,
        spatial_rel[::-1, ::-1].transpose(0, 1, 3, 2),
        (1, 1),
        ((1, 1), (1, 1)),
        dimension_numbers=conv_dims,
        preferred_element_type=WIDE,
    ).reshape(pixel_rows, mid_width)
    first_sum = scatter_relative(column_parts(first_terms), "chan")
    spatial_terms = lax.conv_general_dilated(
        maps_one,
        maps_two,
        (1, 1),
        ((1, 1), (1, 1)),
        dimension_numbers=lax.ConvDimensionNumbers((3, 2, 0, 1), (3, 2, 0, 1), (2, 3, 0, 1)),
        preferred_element_type=WIDE,
    ).reshape(9, mid_width, mid_local)
    spatial_sent = deal_rows(
        spatial_terms.astype(LOW).reshape(9 * mid_width, mid_local),
        jnp.stack([dp_at, chan_at]).astype(jnp.int32),
        dp_count,
        9,
        chan_count,
    )
    first_sum, spatial_sent = join(first_sum, spatial_sent)
    spatial_came = scatter_staged(spatial_sent, "dp")
    own_hot = (own_slots[:, None] == channels[None, :]).astype(LOW)
    slot_hidden = contract(contract(pooled_all, own_hot, 1, 1).astype(LOW), head_pre_low, 0, 0)
    hidden_new = step(hidden_weight, hidden_moment, hidden_second, slot_hidden, in_width ** (-0.5))
    grad_one, centred_one, first_sums = inner_sums(
        first_sum, pre_one, average_one, inv_one, first_norm
    )
    first_grads, *hidden_new = join(total_hyper(first_sums, "dp"), *hidden_new)
    first_low = backward_of_norm(
        grad_one, centred_one, inv_one, first_norm[0], first_grads, pixel_total
    ).astype(LOW)
    squeeze_grad = contract(pixels, first_low, 0, 0).astype(LOW)
    squeeze_terms = slot_terms(squeeze_grad, 0)
    squeeze_came = scatter_staged(squeeze_terms, "dp")
    first_all = jnp.concatenate(gather_relative(after(first_low, squeeze_terms), "chan"), axis=1)
    images_grad = contract(first_all, squeeze_rel, 1, 1) + sum_grad
    images_grad = images_grad.reshape(map_side, map_side, crops_dev, out_local).transpose(2, 0, 1, 3)
    hidden_late, spatial_came, expand_came, _ = join(
        hidden_act, spatial_came, expand_came, squeeze_terms
    )
    slot_squeeze, slot_spatial, slot_expand = [
        wide_sum(came) for came in (squeeze_came, spatial_came, expand_came)
    ]
    project_grad = jnp.concatenate(
        gather_relative(contract(hidden_late, project_low_grad, 0, 0).astype(LOW), "chan")
    )
    turned_hot = ((own_slots ^ (chan_at * hid_local))[:, None] == channels[None, :]).astype(LOW)
    slot_project = contract(turned_hot, project_grad, 1, 0)

    norm_gradient = jnp.concatenate([first_grads, second_grads, third_grads, head_grads], axis=1)
    norm_gradient = norm_gradient[::-1].reshape(norm_params.shape)
    return (
        block_out,
        loss,
        images_grad,
        *step(squeeze_weight, squeeze_moment, squeeze_second, slot_squeeze, in_width ** (-0.5)),
        *step(
            spatial_weight, spatial_moment, spatial_second, slot_spatial, (9 * mid_width) ** (-0.5)
        ),
        *step(expand_weight, expand_moment, expand_second, slot_expand, mid_width ** (-0.5)),
        *hidden_new,
        *step(project_weight, project_moment, project_second, slot_project, hid_width ** (-0.5)),
        *proto_new,
        *step(norm_params, norm_moment, norm_second, norm_gradient, 0.5, 0.0),
    )


def solution(mesh):
    rows, both, whole = P("dp", None), P("dp", "chan"), P()
    maps = P("dp", None, None, "chan")
    norm = P(None, "chan", None)
    placed = (
        (P("dp", None, None, None), P("dp"), whole)
        + (both,) * 12
        + (rows,) * 3
        + (whole,) * 3
        + (norm,) * 3
        + (rows, P("dp"), whole, whole)
    )
    return jax.shard_map(
        local,
        mesh=mesh,
        in_specs=placed,
        out_specs=(maps, whole, maps) + (both,) * 12 + (rows,) * 3 + (whole,) * 3 + (norm,) * 3,
        check_vma=False,
    )
```

```python
import math

import jax
import jax.numpy as jnp
from jax import lax
from jax.experimental import pallas as pl
from jax.experimental.pallas import tpu as pltpu
from jax.sharding import PartitionSpec as P

SINK_ITERS = 3
PRECISE = lax.Precision.HIGHEST
EPS_SINK = 0.05
SOFTMAX_WARMTH = 0.1
LOSS_MULTIPLIER = 256.0
NORM_EPS = 1e-05
BETA_ONE = 0.5
BETA_TWO = 0.5
ADAM_EPS = 1e-08
DECAY_RATE = 1e-06
LOW = jnp.bfloat16
WIDE = jnp.float32


def contract(left, right, left_dim, right_dim):
    return lax.dot_general(
        left, right, (((left_dim,), (right_dim,)), ((), ())), preferred_element_type=WIDE
    )


def silu_slope(value):
    sigma = jax.nn.sigmoid(value)
    return sigma * (1.0 + value * (1.0 - sigma))


def spread(value, axis):
    count = lax.axis_size(axis)
    return lax.all_to_all(jnp.broadcast_to(value[None], (count,) + value.shape), axis, 0, 0)


def total(value, axis):
    return jnp.sum(spread(value, axis).astype(WIDE), axis=0)


def swap(value, axis, bit):
    return lax.ppermute(value, axis, [(at, at ^ bit) for at in range(lax.axis_size(axis))])


def gather_relative(value, axis):
    held = {0: value}
    bit = lax.axis_size(axis) // 2
    while bit:
        keys = sorted(held)
        came = swap(jnp.stack([held[k] for k in keys]), axis, bit)
        held.update({k ^ bit: came[n] for n, k in enumerate(keys)})
        bit //= 2
    return [held[k] for k in range(lax.axis_size(axis))]


def invert_kernel(slots_ref, place_ref, rank_ref):
    count = slots_ref.shape[0]
    channels = place_ref.shape[0] - 128

    def step(at, rank):
        for n in range(16):
            slot = at * 16 + n
            channel = slots_ref[slot]
            place_ref[channel] = slot
            rank_ref[channel] = rank
            rank = rank + jnp.where(channel < channels, 1, 0)
        return rank

    lax.fori_loop(0, count // 16, step, jnp.int32(0))


def slot_of_channel(slot_rows, channels):
    smem = pl.BlockSpec(memory_space=pltpu.SMEM)
    return pl.pallas_call(
        invert_kernel,
        out_shape=[jax.ShapeDtypeStruct((channels + 128,), jnp.int32)] * 2,
        in_specs=[smem],
        out_specs=[smem] * 2,
        name="slot_of_channel",
    )(slot_rows)


def pick_kernel(first, count, place_ref, turn_ref, *refs):
    *blocks, out_ref, wide, picked = refs
    at = 0
    for block in blocks:
        for part in [block.at[k] for k in range(block.shape[0])] if len(block.shape) == 3 else [block]:
            wide[at : at + count, :] = part[first : first + count, :].astype(WIDE)
            at += count

    def step(group, carry):
        for n in range(8):
            row = group * 8 + n
            picked[pl.ds(row, 1), :] = wide[pl.ds(place_ref[(group * 8 ^ turn_ref[0]) + n], 1), :]
        return carry

    lax.fori_loop(0, out_ref.shape[0] // 8, step, 0)
    out_ref[...] = picked[...].astype(out_ref.dtype)


def pick_rows(place, turn, blocks, rows, first, count):
    width = blocks[0].shape[-1]
    held = sum(block.size // (width * block.shape[-2]) for block in blocks) * count
    vmem = pl.BlockSpec()
    return pl.pallas_call(
        lambda *refs: pick_kernel(first, count, *refs),
        out_shape=jax.ShapeDtypeStruct((rows, width), LOW),
        in_specs=[pl.BlockSpec(memory_space=pltpu.SMEM)] * 2 + [vmem] * len(blocks),
        out_specs=vmem,
        scratch_shapes=[pltpu.VMEM((held, width), WIDE), pltpu.VMEM((rows, width), WIDE)],
        compiler_params=pltpu.CompilerParams(vmem_limit_bytes=12 << 20),
        cost_estimate=pl.CostEstimate(
            flops=0, bytes_accessed=2 * (held + rows) * width, transcendentals=0
        ),
        name="pick_rows",
    )(place, turn, *blocks)


def assemble_kernel(taps, chan_count, rows, at_ref, held_ref, out_ref):
    per_tap = out_ref.shape[0] // taps
    per_chan = per_tap // chan_count
    size = math.gcd(rows, per_chan)
    for row in range(0, out_ref.shape[0], size):
        tap, inner = divmod(row, per_tap)
        chan, rest = divmod(inner, per_chan)
        target = pl.multiple_of((chan ^ at_ref[0]) * per_chan + tap * per_tap + rest, size)
        owner, source = divmod(row, rows)
        out_ref[pl.ds(target, size), :] = held_ref[owner, source : source + size, :]


def assemble(held, at, rows, taps, chan_count):
    vmem = pl.BlockSpec()
    return pl.pallas_call(
        lambda *refs: assemble_kernel(taps, chan_count, rows, *refs),
        out_shape=jax.ShapeDtypeStruct((rows * held.shape[0], held.shape[2]), LOW),
        in_specs=[pl.BlockSpec(memory_space=pltpu.SMEM), vmem],
        out_specs=vmem,
        compiler_params=pltpu.CompilerParams(vmem_limit_bytes=12 << 20),
        cost_estimate=pl.CostEstimate(
            flops=0, bytes_accessed=4 * rows * held.shape[0] * held.shape[2], transcendentals=0
        ),
        name="assemble",
    )(at, held)


def deal_kernel(taps, chan_count, order, at_ref, terms_ref, out_ref):
    rows = out_ref.shape[1]
    per_tap = terms_ref.shape[0] // taps
    per_chan = per_tap // chan_count
    size = math.gcd(rows, per_chan)
    for n, r in enumerate(order):
        for start in range(0, rows, size):
            row = (at_ref[0] ^ r) * rows + start
            tap, inner = row // per_tap, row % per_tap
            chan, rest = inner // per_chan, inner % per_chan
            source = tap * per_tap + (chan ^ at_ref[1]) * per_chan + rest
            source = pl.multiple_of(source, size)
            out_ref[n, start : start + size, :] = terms_ref[pl.ds(source, size), :]


def deal_rows(terms, at, owners, taps, chan_count):
    order = send_order(owners)
    vmem = pl.BlockSpec()
    return pl.pallas_call(
        lambda *refs: deal_kernel(taps, chan_count, order, *refs),
        out_shape=jax.ShapeDtypeStruct((owners, terms.shape[0] // owners, terms.shape[1]), LOW),
        in_specs=[pl.BlockSpec(memory_space=pltpu.SMEM), vmem],
        out_specs=vmem,
        compiler_params=pltpu.CompilerParams(vmem_limit_bytes=12 << 20),
        cost_estimate=pl.CostEstimate(flops=0, bytes_accessed=4 * terms.size, transcendentals=0),
        name="deal_rows",
    )(at, terms)


ROWS = 32
BLOCK = 128


def whole(count):
    return [pl.BlockSpec()] * count


def over_rows(total_rows, body, size=ROWS):
    def step(at, carry):
        body(pl.ds(pl.multiple_of(at * size, size), size))
        return carry

    lax.fori_loop(0, total_rows // size, step, 0)


def sum_rows(total_rows, width, body, size):
    def step(at, held):
        value = body(pl.ds(pl.multiple_of(at * size, size), size))
        for first in range(0, size, 8):
            held = held + value[first : first + 8]
        return held

    held = lax.fori_loop(0, total_rows // size, step, jnp.zeros((8, width), WIDE))
    return jnp.sum(held, axis=0, keepdims=True)


def inverse_of(row_sums):
    return 1.0 / jnp.where(row_sums > 0.0, row_sums, 1.0)


def known_columns(width, known):
    return lax.broadcasted_iota(jnp.int32, (1, width), 1) < known


def fill(target, value):
    for at in range(target.shape[0]):
        target[at] = value


def low_of(z):
    return (z * lax.rsqrt(jnp.sum(z * z, axis=1, keepdims=True) + 1e-06)).astype(LOW)


def weigh_columns(matrix, factors):
    factors = jnp.broadcast_to(factors.astype(LOW), (128, factors.shape[1]))
    return contract(matrix.astype(LOW), factors, 1, 1)


def in_all_tiles(value, width):
    return jnp.concatenate([value] * (width // 128), axis=1)


def first_turn(
    known, z_ref, first_ref, proto_any, queue_any, b_ref, bq_any, sent_any, proto, bq, sent, inv, row_inv, sems
):
    proto_in = pltpu.make_async_copy(proto_any, proto, sems.at[0])
    queue_in = pltpu.make_async_copy(queue_any, bq, sems.at[1])
    queue_out = pltpu.make_async_copy(bq, bq_any, sems.at[2])
    sent_out = pltpu.make_async_copy(sent, sent_any, sems.at[3])
    proto_in.start()
    queue_in.start()
    low = low_of(z_ref[...])
    proto_in.wait()
    b_ref[...] = contract(low, proto[...], 1, 1)
    lines, width = bq.shape
    total_rows = b_ref.shape[0]
    mask = known_columns(width, known)

    def exponentials(rows):
        value = jnp.where(mask, jnp.exp(b_ref[rows, :] * (1.0 / EPS_SINK)), 0.0)
        b_ref[rows, :] = value
        return value

    totals = sum_rows(total_rows, width, exponentials, 8)
    totals = totals + jnp.sum(first_ref[...], axis=0, keepdims=True)
    factors = jnp.where(mask, 1.0 / jnp.where(mask, totals * 0.125, 1.0), 0.0)
    inv[...] = jnp.broadcast_to(factors, inv.shape)
    queue_in.wait()
    row_inv[pl.ds(0, lines), :] = inverse_of(weigh_columns(bq[...], factors))

    def queue(rows):
        factor = jnp.concatenate([inv[...]] * 2, axis=0)
        value = bq[rows, :].astype(WIDE) * factor * in_all_tiles(row_inv[rows, :], width)
        bq[rows, :] = value.astype(LOW)
        return value

    queue_sums = sum_rows(lines, width, queue, 16)
    queue_out.start()
    row_inv[pl.ds(0, total_rows), :] = inverse_of(weigh_columns(b_ref[...], factors))

    def batch(rows):
        value = b_ref[rows, :] * inv[...] * in_all_tiles(row_inv[rows, :], width)
        b_ref[rows, :] = value
        return value

    batch_sums = sum_rows(total_rows, width, batch, 8)
    fill(sent, queue_sums + batch_sums * (1.0 / sent.shape[0]))
    sent_out.start()
    queue_out.wait()
    sent_out.wait()


def column_factor(known, came_ref):
    totals = jnp.sum(came_ref[...], axis=0)
    mask = known_columns(totals.shape[1], known)
    return jnp.where(mask, 1.0 / jnp.where(mask, totals, 1.0), 0.0)


def next_turn(known, came_ref, b_ref, bq_any, sent_any, bq, sent, row_inv, sems):
    queue_in = pltpu.make_async_copy(bq_any, bq, sems.at[0])
    sent_out = pltpu.make_async_copy(sent, sent_any, sems.at[1])
    queue_in.start()
    factors = column_factor(known, came_ref)

    def weigh(source, size):
        total_rows, width = source.shape
        row_inv[pl.ds(0, total_rows), :] = inverse_of(weigh_columns(source[...], factors))

        def body(rows):
            return source[rows, :].astype(WIDE) * in_all_tiles(row_inv[rows, :], width)

        return sum_rows(total_rows, width, body, size)

    batch_sums = weigh(b_ref, 8)
    queue_in.wait()
    fill(sent, weigh(bq, 16) + batch_sums * (1.0 / sent.shape[0]))
    sent_out.start()
    sent_out.wait()


def norm_of_scores(known, z_ref, proto_any, norm_ref, proto, scores, sems):
    proto_in = pltpu.make_async_copy(proto_any, proto, sems.at[0])
    proto_in.start()
    low = low_of(z_ref[...])
    proto_in.wait()
    scores[...] = contract(low, proto[...], 1, 1)
    mask = known_columns(scores.shape[1], known)

    def body(rows):
        raw = scores[rows, :] * (1.0 / SOFTMAX_WARMTH)
        top = jnp.max(jnp.where(mask, raw, -jnp.inf), axis=1, keepdims=True)
        mass = jnp.sum(jnp.where(mask, jnp.exp(raw - top), 0.0), axis=1, keepdims=True)
        norm_ref[rows, :] = top + jnp.log(mass)

    over_rows(scores.shape[0], body)


def last_turn(
    known,
    came_ref,
    b_ref,
    z_ref,
    norm_ref,
    proto_any,
    pairs_any,
    grad_any,
    low_grad_ref,
    loss_ref,
    proto,
    pairs,
    grad,
    scores,
    high,
    rest,
    held,
    inv,
    sems,
):
    proto_in = pltpu.make_async_copy(proto_any, proto, sems.at[0])
    pairs_in = pltpu.make_async_copy(pairs_any, pairs, sems.at[1])
    grad_out = pltpu.make_async_copy(grad, grad_any, sems.at[2])
    proto_in.start()
    pairs_in.start()
    factors = column_factor(known, came_ref)
    inv[...] = factors
    mask = known_columns(factors.shape[1], known)
    size = pairs.shape[1]
    loss_ref[...] = jnp.zeros(loss_ref.shape, WIDE)
    proto_in.wait()
    pairs_in.wait()

    def block(at, carry):
        def here(rows):
            return pl.ds(pl.multiple_of(at * size + rows, 8), ROWS)

        place = pl.ds(pl.multiple_of(at * size, size), size)
        z = z_ref[place, :]
        inv_len = lax.rsqrt(jnp.sum(z * z, axis=1, keepdims=True) + 1e-06)
        scores[...] = contract((z * inv_len).astype(LOW), proto[...], 1, 1)
        for first in range(0, size, ROWS):
            value = b_ref[here(first), :] * inv[...]
            value = value * (1.0 / jnp.sum(value, axis=1, keepdims=True))
            top = value.astype(LOW)
            high[first : first + ROWS, :] = top
            rest[first : first + ROWS, :] = (value - top.astype(WIDE)).astype(LOW)
        pair = pairs[at]
        others = jnp.sum(pair.astype(WIDE), axis=1, keepdims=True)
        inv_others = 1.0 / jnp.maximum(others, 1.0)
        held[...] = contract(pair, high[...], 1, 0) + contract(pair, rest[...], 1, 0)
        for first in range(0, size, ROWS):
            rows = slice(first, first + ROWS)
            targets = held[rows, :] * inv_others[rows]
            logs = scores[rows, :] * (1.0 / SOFTMAX_WARMTH) - norm_ref[here(first), :]
            loss_ref[...] -= jnp.sum(jnp.where(mask, targets * logs, 0.0))
            weight = jnp.sum(targets, axis=1, keepdims=True)
            value = (LOSS_MULTIPLIER / SOFTMAX_WARMTH) * (jnp.exp(logs) * weight - targets)
            grad[here(first), :] = jnp.where(mask, value, 0.0).astype(LOW)
        normed_grad = contract(grad[place, :], proto[...], 1, 0)
        normed = z * inv_len
        along = jnp.sum(normed * normed_grad, axis=1, keepdims=True)
        low_grad_ref[place, :] = (inv_len * (normed_grad - normed * along)).astype(LOW)
        return carry

    lax.fori_loop(0, pairs.shape[0], block, 0)
    grad_out.start()
    grad_out.wait()


def shape(dims, kind=WIDE):
    return jax.ShapeDtypeStruct(dims, kind)


def turn_call(kernel, known, outs, anywhere_out, close, anywhere, scratch, copies):
    near, far = pl.BlockSpec(memory_space=pltpu.VMEM), pl.BlockSpec(memory_space=pltpu.HBM)
    held = sum(value.size * value.dtype.itemsize for value in (*scratch, *close, *outs))
    return pl.pallas_call(
        lambda *refs: kernel(known, *refs),
        out_shape=outs,
        in_specs=[near] * len(close) + [far] * len(anywhere),
        out_specs=[far if at in anywhere_out else near for at in range(len(outs))],
        scratch_shapes=[pltpu.VMEM(value.shape, value.dtype) for value in scratch]
        + [pltpu.SemaphoreType.DMA((copies,))],
        compiler_params=pltpu.CompilerParams(vmem_limit_bytes=min(held + (8 << 20), 60 << 20)),
        name=kernel.__name__,
    )(*close, *anywhere)


def call_first(known, z, proto, queue, first):
    rows, width, lines, owners = z.shape[0], proto.shape[0], queue.shape[0], first.shape[0]
    sent = shape((owners, 1, width))
    return turn_call(
        first_turn,
        known,
        [shape((rows, width)), shape(queue.shape, LOW), sent],
        (1, 2),
        (z, first),
        (proto, queue),
        [
            shape(proto.shape, LOW),
            shape(queue.shape, LOW),
            sent,
            shape((8, width)),
            shape((max(rows, lines), 128)),
        ],
        4,
    )


def call_next(known, came, b, bq):
    return turn_call(
        next_turn,
        known,
        [shape(came.shape)],
        (0,),
        (came, b),
        (bq,),
        [shape(bq.shape, LOW), shape(came.shape), shape((max(b.shape[0], bq.shape[0]), 128))],
        2,
    )[0]


def call_norm(known, z, proto):
    rows, width = z.shape[0], proto.shape[0]
    return turn_call(
        norm_of_scores,
        known,
        [shape((rows, 1))],
        (),
        (z,),
        (proto,),
        [shape(proto.shape, LOW), shape((rows, width))],
        1,
    )[0]


def call_last(known, came, b, z, norm, proto, pairs):
    width, size = b.shape[1], pairs.shape[1]
    part = (size, width)
    return turn_call(
        last_turn,
        known,
        [shape(b.shape, LOW), shape(z.shape, LOW), shape((8, 128))],
        (0,),
        (came, b, z, norm),
        (proto, pairs),
        [
            shape(proto.shape, LOW),
            shape(pairs.shape, LOW),
            shape(b.shape, LOW),
            shape(part),
            shape(part, LOW),
            shape(part, LOW),
            shape(part),
            shape((1, width)),
        ],
        3,
    )


def after(value, token):
    return lax.optimization_barrier((value, token))[0]


def join(*values):
    return lax.optimization_barrier(values)


def scatter_relative(parts, axis, sent=LOW):
    held = dict(enumerate(parts))
    bit = 1
    while bit < lax.axis_size(axis):
        keys = [k for k in sorted(held) if not k & bit]
        came = swap(jnp.stack([held[k | bit].astype(sent) for k in keys]), axis, bit)
        held = {k: held[k] + came[n].astype(WIDE) for n, k in enumerate(keys)}
        bit *= 2
    return held[0]


def send_order(count):
    low = max(count // 4, 1)
    order = list(range(0, count, low))
    bit = low // 2
    while bit:
        order = order + [r | bit for r in order]
        bit //= 2
    return order


def scatter_staged(blocks, axis):
    count = lax.axis_size(axis)
    low = max(count // 4, 1)
    held = blocks
    bit = 1
    while bit < low:
        half = held.shape[0] // 2
        came = swap(held[half:], axis, bit)
        held = (held[:half].astype(WIDE) + came.astype(WIDE)).astype(LOW)
        bit *= 2
    came = [swap(held[n], axis, n * low) for n in range(1, held.shape[0])]
    return held[0], came


def wide_sum(terms):
    kept, came = terms
    result = kept.astype(WIDE)
    for value in came:
        result = result + value.astype(WIDE)
    return result


def total_hyper(value, axis):
    bit = 1
    while bit < lax.axis_size(axis):
        value = value + swap(value, axis, bit)
        bit *= 2
    return value


def block_at(value, index, size, dim):
    return lax.dynamic_slice_in_dim(value, index * size, size, dim)


def statistics(sums, row_total):
    average = sums[0] / row_total
    variance = sums[1] / row_total - average * average
    return average, lax.rsqrt(variance + NORM_EPS)


def backward_of_norm(grad_out, centred, inv_std, gain_row, sums, row_total):
    return gain_row * inv_std * (grad_out - (sums[0] + centred * sums[1]) / row_total)


def adamw_step(weight, moment_one, moment_two, gradient, learn_rate, weight_decay, step_count):
    moment_new = BETA_ONE * moment_one + (1.0 - BETA_ONE) * gradient
    second_new = BETA_TWO * moment_two + (1.0 - BETA_TWO) * gradient * gradient
    fix_one = 1.0 - jnp.power(BETA_ONE, step_count)
    fix_two = 1.0 - jnp.power(BETA_TWO, step_count)
    update = moment_new / fix_one / (jnp.sqrt(second_new / fix_two) + ADAM_EPS)
    return (weight - learn_rate * (update + weight_decay * weight), moment_new, second_new)


def local(
    images,
    crop_image,
    slot_rows,
    squeeze_weight,
    squeeze_moment,
    squeeze_second,
    spatial_weight,
    spatial_moment,
    spatial_second,
    expand_weight,
    expand_moment,
    expand_second,
    hidden_weight,
    hidden_moment,
    hidden_second,
    project_weight,
    project_moment,
    project_second,
    prototypes,
    proto_moment,
    proto_second,
    norm_params,
    norm_moment,
    norm_second,
    queue_rows,
    queue_valid,
    queue_fill,
    iteration,
):
    dp_count = lax.axis_size("dp")
    dp_at = lax.axis_index("dp")
    chan_count = lax.axis_size("chan")
    chan_at = lax.axis_index("chan")
    crops_dev, map_side, _, in_width = images.shape
    map_area = map_side * map_side
    pixel_rows = crops_dev * map_area
    pixel_total = pixel_rows * dp_count
    crop_total = crops_dev * dp_count
    mid_local = squeeze_weight.shape[1]
    hid_local = hidden_weight.shape[1]
    out_local = in_width // chan_count
    slot_local = squeeze_weight.shape[0]
    slot_total = slot_rows.shape[0]
    mid_width = mid_local * chan_count
    hid_width = hid_local * chan_count

    squeeze_came = spread(squeeze_weight.astype(LOW), "dp")
    tap_local = spatial_weight.shape[0]
    convs_all = lax.all_gather(
        jnp.concatenate([spatial_weight.astype(LOW), expand_weight.astype(LOW)], axis=0), "dp"
    )

    channels = jnp.arange(in_width, dtype=jnp.int32)
    used = (slot_rows < in_width).astype(jnp.int32).reshape(dp_count, slot_local)
    loads = jnp.sum(used, axis=1)
    owners = jnp.arange(dp_count, dtype=jnp.int32)
    firsts = jnp.sum(jnp.where(owners[None, :] < owners[:, None], loads[None, :], 0), axis=1)
    own_used = block_at(used, dp_at, 1, 0)[0]
    own_first = block_at(firsts, dp_at, 1, 0)
    own_at = jnp.arange(slot_local, dtype=jnp.int32)
    own_rank = jnp.sum(jnp.where(own_at[None, :] < own_at[:, None], own_used[None, :], 0), axis=1)
    cell = slot_local // dp_count
    share = in_width // dp_count
    target = (own_first + own_rank) % dp_count * cell + own_rank // dp_count
    deal_hot = ((target[None, :] == own_at[:, None]) & (own_used[None, :] > 0)).astype(LOW)
    head_low = jnp.concatenate([hidden_weight.astype(LOW), project_weight.astype(LOW)], axis=1)
    dealt = contract(deal_hot, head_low, 1, 0).astype(LOW)
    ranks = (
        jnp.arange(cell, dtype=jnp.int32)[None, :] * dp_count + (dp_at - firsts[:, None]) % dp_count
    )
    share_at = jnp.where(ranks < loads[:, None], (firsts[:, None] + ranks) // dp_count, -1)
    share_at = share_at.reshape(slot_local)
    place, rank = slot_of_channel(slot_rows, in_width)
    slot_blocks = slot_rows.reshape(dp_count, slot_local)
    slot_sent = jnp.concatenate(
        [lax.dynamic_index_in_dim(slot_blocks, dp_at ^ r, 0, False) for r in send_order(dp_count)]
    )
    own_slots = slot_sent[:slot_local]
    place_dealt = (rank % dp_count * share + rank // dp_count)[:in_width]

    proto_count = prototypes.shape[1]
    proto_low = jnp.pad(prototypes.astype(LOW).T, ((0, -proto_count % 256), (0, 0)))
    proto_width = proto_low.shape[0]
    queue_len = queue_rows.shape[0]
    slot_index = dp_at * queue_len + jnp.arange(queue_len, dtype=jnp.int32)
    queue_live = ((queue_valid > 0) & (slot_index < queue_fill[0])).astype(WIDE)
    queue_live = jnp.pad(queue_live, (0, -queue_len % ROWS))
    queue_similarity = contract(
        jnp.pad(queue_rows, ((0, -queue_len % ROWS), (0, 0))), proto_low, 1, 1
    )
    queue_codes = jnp.where(
        (jnp.arange(proto_width) < proto_count)[None, :],
        jnp.exp(queue_similarity / EPS_SINK) * queue_live[:, None],
        0.0,
    )
    queue_mass = jnp.sum(queue_codes, axis=0)
    queue_codes = queue_codes.astype(LOW)
    squeeze_came, queue_codes, queue_mass, slot_sent, proto_low = join(
        squeeze_came, queue_codes, queue_mass, slot_sent, proto_low
    )
    straight = jnp.zeros((1,), jnp.int32)
    turned = (chan_at * out_local).astype(jnp.int32).reshape(1)
    squeeze_rows = pick_rows(place, straight, [squeeze_came], in_width, 0, slot_local)

    norm_rows = norm_params[:, 0, :]
    first_norm = norm_rows[:, :mid_local]
    second_norm = norm_rows[:, mid_local : 2 * mid_local]
    third_norm = norm_rows[:, 2 * mid_local : 2 * mid_local + out_local]
    head_norm = norm_rows[:, 2 * mid_local + out_local :]

    def inner_layer(pre_act, norm, token=None):
        sums = jnp.stack([jnp.sum(pre_act, axis=0), jnp.sum(pre_act * pre_act, axis=0)])
        if token is not None:
            sums = after(sums, token)
        near = sums[0] / pixel_rows
        raw_all = jnp.concatenate(gather_relative((pre_act - near).astype(LOW), "chan"), axis=1)
        average, inv_std = statistics(total(sums, "dp"), pixel_total)
        scale = inv_std * norm[0]
        affine = jnp.stack([scale, norm[1] - (average - near) * scale])
        affine_all = jnp.concatenate(gather_relative(affine, "chan"), axis=1)
        act_all = jax.nn.silu(raw_all.astype(WIDE) * affine_all[0] + affine_all[1]).astype(LOW)
        return act_all, average, inv_std

    step_count = iteration[0].astype(WIDE)

    def step(weight, moment, second, gradient, rate, decay=DECAY_RATE):
        return adamw_step(weight, moment, second, gradient, rate, decay, step_count)

    pixels = images.transpose(1, 2, 0, 3).reshape(pixel_rows, in_width)
    pre_one = contract(pixels, squeeze_rows, 1, 0)
    inner_one, average_one, inv_one = inner_layer(pre_one, first_norm)
    dealt = lax.all_to_all(after(dealt, average_one).reshape(dp_count, cell, -1), "dp", 0, 0)
    def relative_blocks(value, size, dim):
        return [block_at(value, chan_at ^ r, size, dim) for r in range(chan_count)]

    spatial_rel = assemble(
        convs_all, chan_at.astype(jnp.int32).reshape(1), tap_local, 9, chan_count
    ).reshape(3, 3, mid_width, mid_local)
    maps_one = inner_one.reshape(map_side, map_side, crops_dev, mid_width)
    conv_dims = lax.ConvDimensionNumbers((2, 3, 0, 1), (3, 2, 0, 1), (2, 3, 0, 1))
    pre_two = lax.conv_general_dilated(
        maps_one,
        spatial_rel,
        (1, 1),
        ((1, 1), (1, 1)),
        dimension_numbers=conv_dims,
        preferred_element_type=WIDE,
    ).reshape(pixel_rows, mid_local)
    pre_two, dealt = join(pre_two, dealt)
    share_hot = (share_at[None, :] == channels[:share, None]).astype(LOW)
    head_all = lax.all_gather(
        contract(share_hot, dealt.reshape(slot_local, -1), 1, 0).astype(LOW),
        "dp",
        axis=0,
        tiled=True,
    )

    inner_two, average_two, inv_two = inner_layer(pre_two, second_norm)

    expand_rows = pick_rows(place, turned, [convs_all], in_width, tap_local, slot_local)

    def swap_blocks(blocks):
        return jnp.concatenate(
            [blocks[0]] + [swap(blocks[r], "chan", r) for r in range(1, chan_count)], axis=1
        )

    expand_rel = swap_blocks(
        [expand_rows[r * out_local : (r + 1) * out_local] for r in range(chan_count)]
    )
    squeeze_rel = swap_blocks(relative_blocks(squeeze_rows, out_local, 0))
    pre_three = contract(inner_two, expand_rel, 1, 1)
    sent_three = [
        jnp.sum(pre_three, axis=0),
        jnp.sum(pre_three * pre_three, axis=0),
        queue_mass,
        crop_image.astype(WIDE),
    ]
    came_three = spread(jnp.concatenate(sent_three), "dp")
    sums_three = jnp.sum(came_three[:, : 2 * out_local], axis=0).reshape(2, out_local)
    queue_first = came_three[:, 2 * out_local :]
    average_three, inv_three = statistics(sums_three, pixel_total)
    centred_three = (pre_three - average_three) * inv_three
    residual_in = block_at(pixels, chan_at, out_local, 1).astype(WIDE)
    summed = centred_three * third_norm[0] + third_norm[1] + residual_in
    block_rows = jax.nn.silu(summed)
    block_out = block_rows.astype(LOW).reshape(map_side, map_side, crops_dev, out_local)
    block_out = block_out.transpose(2, 0, 1, 3)
    pooled = jnp.mean(block_rows.reshape(map_area, crops_dev, out_local), axis=0).astype(LOW)
    pooled_dev = lax.all_gather(pooled, "chan", axis=1, tiled=True)
    pooled_all = lax.all_gather(pooled_dev, "dp", axis=0, tiled=True)

    dealt_hot = (place_dealt[:, None] == channels[None, :]).astype(LOW)
    pooled_dealt = contract(pooled_dev, dealt_hot, 1, 0).astype(LOW)
    pooled_dealt, head_all = join(pooled_dealt, head_all)
    hidden_dev = contract(pooled_dealt, head_all[:, :hid_local], 1, 0)
    own_place = block_at(place_dealt, chan_at, hid_local, 0)
    own_dealt_hot = (own_place[:, None] == channels[None, :]).astype(LOW)
    project_rows = contract(own_dealt_hot, head_all[:, hid_local:], 1, 0).astype(LOW)
    near_head = jnp.mean(hidden_dev, axis=0, keepdims=True).astype(LOW)
    hidden_sent = (hidden_dev - near_head.astype(WIDE)).astype(LOW)
    hidden_came = spread(jnp.concatenate([hidden_sent, near_head], axis=0), "dp")
    hidden_rows = contract(
        (after(place_dealt, hidden_dev)[:, None] == channels[None, :]).astype(LOW),
        head_all[:, :hid_local],
        1,
        0,
    ).astype(LOW)
    hidden_came, hidden_rows = join(hidden_came, hidden_rows)
    hidden_pre = (
        hidden_came[:, :crops_dev].astype(WIDE) + hidden_came[:, crops_dev:].astype(WIDE)
    ).reshape(
        crop_total, hid_local
    )
    head_sums = jnp.stack([jnp.sum(hidden_pre, axis=0), jnp.sum(hidden_pre * hidden_pre, axis=0)])
    average_head, inv_head = statistics(head_sums, crop_total)
    centred_head = (hidden_pre - average_head) * inv_head
    normed_head = centred_head * head_norm[0] + head_norm[1]
    hidden_act = jax.nn.silu(normed_head).astype(LOW)
    project_out = total_hyper(contract(hidden_act, project_rows, 1, 0), "chan")
    block_rows_of = min(crop_total, max(BLOCK, crops_dev))
    labels = queue_first[:, proto_width:].reshape(-1, block_rows_of)
    crop_index = jnp.arange(block_rows_of, dtype=jnp.int32)
    same_image = (
        (labels[:, :, None] == labels[:, None, :])
        & (crop_index[:, None] != crop_index[None, :])
        & (crop_index[:, None] // crops_dev == crop_index[None, :] // crops_dev)
    )
    pairs = same_image.astype(LOW)

    codes, queue_codes, sent = call_first(
        proto_count, project_out, proto_low, queue_codes, queue_first[:, :proto_width]
    )
    came = lax.all_to_all(sent, "dp", 0, 0)
    log_norm = call_norm(proto_count, project_out, proto_low)
    for turn_index in range(2, SINK_ITERS):
        came = lax.all_to_all(call_next(proto_count, came, codes, queue_codes), "dp", 0, 0)
    came, pooled_all = join(came, pooled_all)
    score_gradient, project_low_grad, loss_total = call_last(
        proto_count, came, codes, project_out, log_norm, proto_low, pairs
    )
    loss = loss_total[0, :1] / crop_total
    normed_low = low_of(project_out)
    hidden_grad_act = contract(project_low_grad, project_rows, 1, 1) * silu_slope(normed_head)
    head_grads = jnp.stack(
        [jnp.sum(hidden_grad_act, axis=0), jnp.sum(hidden_grad_act * centred_head, axis=0)]
    )
    head_pre_low = backward_of_norm(
        hidden_grad_act, centred_head, inv_head, head_norm[0], head_grads, crop_total
    ).astype(LOW)
    pooled_terms = contract(block_at(head_pre_low, dp_at, crops_dev, 0), hidden_rows, 1, 1)
    pooled_grad = scatter_relative(relative_blocks(pooled_terms, out_local, 1), "chan", WIDE)

    spread_grad = jnp.broadcast_to(
        pooled_grad[None] / map_area, (map_area, crops_dev, out_local)
    ).reshape(pixel_rows, out_local)
    sum_grad = spread_grad * silu_slope(summed)
    third_grads = total(
        jnp.stack([jnp.sum(sum_grad, axis=0), jnp.sum(sum_grad * centred_three, axis=0)]), "dp"
    )
    third_low = backward_of_norm(
        sum_grad, centred_three, inv_three, third_norm[0], third_grads, pixel_total
    ).astype(LOW)

    def column_parts(terms):
        return [terms[:, r * mid_local : (r + 1) * mid_local] for r in range(chan_count)]

    def inner_sums(summed_terms, pre_act, average, inv_std, norm):
        centred = (pre_act - average) * inv_std
        grad = summed_terms * silu_slope(centred * norm[0] + norm[1])
        sums = jnp.stack([jnp.sum(grad, axis=0), jnp.sum(grad * centred, axis=0)])
        return grad, centred, sums

    def slot_terms(grad_rows, turned):
        slot_hot = ((slot_sent ^ (turned * out_local))[:, None] == channels[None, :]).astype(LOW)
        terms = contract(slot_hot, grad_rows, 1, 0).astype(LOW)
        return terms.reshape(dp_count, slot_local, mid_local)

    second_sum = scatter_relative(column_parts(contract(third_low, expand_rel, 1, 0)), "chan")
    expand_terms = contract(third_low, inner_two, 0, 0).astype(LOW)
    proto_grad = contract(score_gradient, normed_low, 0, 0)[:proto_count].T
    proto_new = step(prototypes, proto_moment, proto_second, proto_grad, 0.1)
    second_sum, expand_terms, *proto_new = join(second_sum, expand_terms, *proto_new)
    grad_two, centred_two, second_sums = inner_sums(
        second_sum, pre_two, average_two, inv_two, second_norm
    )
    expand_parts = column_parts(expand_terms)
    expand_grad = jnp.concatenate(
        [expand_parts[0]] + [swap(expand_parts[r], "chan", r) for r in range(1, chan_count)], axis=0
    )
    slot_expand = slot_terms(expand_grad, chan_at)
    second_grads, slot_expand = join(total(second_sums, "dp"), slot_expand)
    expand_came = scatter_staged(slot_expand, "dp")
    second_low = backward_of_norm(
        grad_two, centred_two, inv_two, second_norm[0], second_grads, pixel_total
    ).astype(LOW)
    maps_two = second_low.reshape(map_side, map_side, crops_dev, mid_local)
    first_terms = lax.conv_general_dilated(
        maps_two,
        spatial_rel[::-1, ::-1].transpose(0, 1, 3, 2),
        (1, 1),
        ((1, 1), (1, 1)),
        dimension_numbers=conv_dims,
        preferred_element_type=WIDE,
    ).reshape(pixel_rows, mid_width)
    first_sum = scatter_relative(column_parts(first_terms), "chan")
    spatial_terms = lax.conv_general_dilated(
        maps_one,
        maps_two,
        (1, 1),
        ((1, 1), (1, 1)),
        dimension_numbers=lax.ConvDimensionNumbers((3, 2, 0, 1), (3, 2, 0, 1), (2, 3, 0, 1)),
        preferred_element_type=WIDE,
    ).reshape(9, mid_width, mid_local)
    spatial_sent = deal_rows(
        spatial_terms.astype(LOW).reshape(9 * mid_width, mid_local),
        jnp.stack([dp_at, chan_at]).astype(jnp.int32),
        dp_count,
        9,
        chan_count,
    )
    first_sum, spatial_sent = join(first_sum, spatial_sent)
    spatial_came = scatter_staged(spatial_sent, "dp")
    own_hot = (own_slots[:, None] == channels[None, :]).astype(LOW)
    slot_hidden = contract(contract(pooled_all, own_hot, 1, 1).astype(LOW), head_pre_low, 0, 0)
    hidden_new = step(hidden_weight, hidden_moment, hidden_second, slot_hidden, in_width ** (-0.5))
    grad_one, centred_one, first_sums = inner_sums(
        first_sum, pre_one, average_one, inv_one, first_norm
    )
    first_grads, *hidden_new = join(total_hyper(first_sums, "dp"), *hidden_new)
    first_low = backward_of_norm(
        grad_one, centred_one, inv_one, first_norm[0], first_grads, pixel_total
    ).astype(LOW)
    squeeze_grad = contract(pixels, first_low, 0, 0).astype(LOW)
    squeeze_terms = slot_terms(squeeze_grad, 0)
    squeeze_came = scatter_staged(squeeze_terms, "dp")
    first_all = jnp.concatenate(gather_relative(after(first_low, squeeze_terms), "chan"), axis=1)
    images_grad = contract(first_all, squeeze_rel, 1, 1) + sum_grad
    images_grad = images_grad.reshape(map_side, map_side, crops_dev, out_local).transpose(2, 0, 1, 3)
    hidden_late, spatial_came, expand_came, _ = join(
        hidden_act, spatial_came, expand_came, squeeze_terms
    )
    slot_squeeze, slot_spatial, slot_expand = [
        wide_sum(came) for came in (squeeze_came, spatial_came, expand_came)
    ]
    project_grad = jnp.concatenate(
        gather_relative(contract(hidden_late, project_low_grad, 0, 0).astype(LOW), "chan")
    )
    turned_hot = ((own_slots ^ (chan_at * hid_local))[:, None] == channels[None, :]).astype(LOW)
    slot_project = contract(turned_hot, project_grad, 1, 0)

    norm_gradient = jnp.concatenate([first_grads, second_grads, third_grads, head_grads], axis=1)
    norm_gradient = norm_gradient[::-1].reshape(norm_params.shape)
    return (
        block_out,
        loss,
        images_grad,
        *step(squeeze_weight, squeeze_moment, squeeze_second, slot_squeeze, in_width ** (-0.5)),
        *step(
            spatial_weight, spatial_moment, spatial_second, slot_spatial, (9 * mid_width) ** (-0.5)
        ),
        *step(expand_weight, expand_moment, expand_second, slot_expand, mid_width ** (-0.5)),
        *hidden_new,
        *step(project_weight, project_moment, project_second, slot_project, hid_width ** (-0.5)),
        *proto_new,
        *step(norm_params, norm_moment, norm_second, norm_gradient, 0.5, 0.0),
    )


def solution(mesh):
    rows, both, whole = P("dp", None), P("dp", "chan"), P()
    maps = P("dp", None, None, "chan")
    norm = P(None, "chan", None)
    placed = (
        (P("dp", None, None, None), P("dp"), whole)
        + (both,) * 12
        + (rows,) * 3
        + (whole,) * 3
        + (norm,) * 3
        + (rows, P("dp"), whole, whole)
    )
    return jax.shard_map(
        local,
        mesh=mesh,
        in_specs=placed,
        out_specs=(maps, whole, maps) + (both,) * 12 + (rows,) * 3 + (whole,) * 3 + (norm,) * 3,
        check_vma=False,
    )
```

```python
import math

import jax
import jax.numpy as jnp
from jax import lax
from jax.experimental import pallas as pl
from jax.experimental.pallas import tpu as pltpu
from jax.sharding import PartitionSpec as P

SINK_ITERS = 3
PRECISE = lax.Precision.HIGHEST
EPS_SINK = 0.05
SOFTMAX_WARMTH = 0.1
LOSS_MULTIPLIER = 256.0
NORM_EPS = 1e-05
BETA_ONE = 0.5
BETA_TWO = 0.5
ADAM_EPS = 1e-08
DECAY_RATE = 1e-06
LOW = jnp.bfloat16
WIDE = jnp.float32


def contract(left, right, left_dim, right_dim):
    return lax.dot_general(
        left, right, (((left_dim,), (right_dim,)), ((), ())), preferred_element_type=WIDE
    )


def silu_slope(value):
    sigma = jax.nn.sigmoid(value)
    return sigma * (1.0 + value * (1.0 - sigma))


def spread(value, axis):
    count = lax.axis_size(axis)
    return lax.all_to_all(jnp.broadcast_to(value[None], (count,) + value.shape), axis, 0, 0)


def total(value, axis):
    return jnp.sum(spread(value, axis).astype(WIDE), axis=0)


def swap(value, axis, bit):
    return lax.ppermute(value, axis, [(at, at ^ bit) for at in range(lax.axis_size(axis))])


def gather_relative(value, axis):
    held = {0: value}
    bit = lax.axis_size(axis) // 2
    while bit:
        keys = sorted(held)
        came = swap(jnp.stack([held[k] for k in keys]), axis, bit)
        held.update({k ^ bit: came[n] for n, k in enumerate(keys)})
        bit //= 2
    return [held[k] for k in range(lax.axis_size(axis))]


def invert_kernel(slots_ref, place_ref, rank_ref):
    count = slots_ref.shape[0]
    channels = place_ref.shape[0] - 128

    def step(at, rank):
        for n in range(16):
            slot = at * 16 + n
            channel = slots_ref[slot]
            place_ref[channel] = slot
            rank_ref[channel] = rank
            rank = rank + jnp.where(channel < channels, 1, 0)
        return rank

    lax.fori_loop(0, count // 16, step, jnp.int32(0))


def slot_of_channel(slot_rows, channels):
    smem = pl.BlockSpec(memory_space=pltpu.SMEM)
    return pl.pallas_call(
        invert_kernel,
        out_shape=[jax.ShapeDtypeStruct((channels + 128,), jnp.int32)] * 2,
        in_specs=[smem],
        out_specs=[smem] * 2,
        name="slot_of_channel",
    )(slot_rows)


def pick_kernel(first, count, place_ref, turn_ref, *refs):
    *blocks, out_ref, wide, picked = refs
    at = 0
    for block in blocks:
        for part in [block.at[k] for k in range(block.shape[0])] if len(block.shape) == 3 else [block]:
            wide[at : at + count, :] = part[first : first + count, :].astype(WIDE)
            at += count

    def step(group, carry):
        for n in range(8):
            row = group * 8 + n
            picked[pl.ds(row, 1), :] = wide[pl.ds(place_ref[(group * 8 ^ turn_ref[0]) + n], 1), :]
        return carry

    lax.fori_loop(0, out_ref.shape[0] // 8, step, 0)
    out_ref[...] = picked[...].astype(out_ref.dtype)


def pick_rows(place, turn, blocks, rows, first, count):
    width = blocks[0].shape[-1]
    held = sum(block.size // (width * block.shape[-2]) for block in blocks) * count
    vmem = pl.BlockSpec()
    return pl.pallas_call(
        lambda *refs: pick_kernel(first, count, *refs),
        out_shape=jax.ShapeDtypeStruct((rows, width), LOW),
        in_specs=[pl.BlockSpec(memory_space=pltpu.SMEM)] * 2 + [vmem] * len(blocks),
        out_specs=vmem,
        scratch_shapes=[pltpu.VMEM((held, width), WIDE), pltpu.VMEM((rows, width), WIDE)],
        compiler_params=pltpu.CompilerParams(vmem_limit_bytes=12 << 20),
        cost_estimate=pl.CostEstimate(
            flops=0, bytes_accessed=2 * (held + rows) * width, transcendentals=0
        ),
        name="pick_rows",
    )(place, turn, *blocks)


def assemble_kernel(taps, chan_count, rows, at_ref, held_ref, out_ref):
    per_tap = out_ref.shape[0] // taps
    per_chan = per_tap // chan_count
    size = math.gcd(rows, per_chan)
    for row in range(0, out_ref.shape[0], size):
        tap, inner = divmod(row, per_tap)
        chan, rest = divmod(inner, per_chan)
        target = pl.multiple_of((chan ^ at_ref[0]) * per_chan + tap * per_tap + rest, size)
        owner, source = divmod(row, rows)
        out_ref[pl.ds(target, size), :] = held_ref[owner, source : source + size, :]


def assemble(held, at, rows, taps, chan_count):
    vmem = pl.BlockSpec()
    return pl.pallas_call(
        lambda *refs: assemble_kernel(taps, chan_count, rows, *refs),
        out_shape=jax.ShapeDtypeStruct((rows * held.shape[0], held.shape[2]), LOW),
        in_specs=[pl.BlockSpec(memory_space=pltpu.SMEM), vmem],
        out_specs=vmem,
        compiler_params=pltpu.CompilerParams(vmem_limit_bytes=12 << 20),
        cost_estimate=pl.CostEstimate(
            flops=0, bytes_accessed=4 * rows * held.shape[0] * held.shape[2], transcendentals=0
        ),
        name="assemble",
    )(at, held)


def deal_kernel(taps, chan_count, order, at_ref, terms_ref, out_ref):
    rows = out_ref.shape[1]
    per_tap = terms_ref.shape[0] // taps
    per_chan = per_tap // chan_count
    size = math.gcd(rows, per_chan)
    for n, r in enumerate(order):
        for start in range(0, rows, size):
            row = (at_ref[0] ^ r) * rows + start
            tap, inner = row // per_tap, row % per_tap
            chan, rest = inner // per_chan, inner % per_chan
            source = tap * per_tap + (chan ^ at_ref[1]) * per_chan + rest
            source = pl.multiple_of(source, size)
            out_ref[n, start : start + size, :] = terms_ref[pl.ds(source, size), :]


def deal_rows(terms, at, owners, taps, chan_count):
    order = send_order(owners)
    vmem = pl.BlockSpec()
    return pl.pallas_call(
        lambda *refs: deal_kernel(taps, chan_count, order, *refs),
        out_shape=jax.ShapeDtypeStruct((owners, terms.shape[0] // owners, terms.shape[1]), LOW),
        in_specs=[pl.BlockSpec(memory_space=pltpu.SMEM), vmem],
        out_specs=vmem,
        compiler_params=pltpu.CompilerParams(vmem_limit_bytes=12 << 20),
        cost_estimate=pl.CostEstimate(flops=0, bytes_accessed=4 * terms.size, transcendentals=0),
        name="deal_rows",
    )(at, terms)


ROWS = 32
BLOCK = 128


def whole(count):
    return [pl.BlockSpec()] * count


def over_rows(total_rows, body, size=ROWS):
    def step(at, carry):
        body(pl.ds(pl.multiple_of(at * size, size), size))
        return carry

    lax.fori_loop(0, total_rows // size, step, 0)


def sum_rows(total_rows, width, body, size):
    def step(at, held):
        value = body(pl.ds(pl.multiple_of(at * size, size), size))
        for first in range(0, size, 8):
            held = held + value[first : first + 8]
        return held

    held = lax.fori_loop(0, total_rows // size, step, jnp.zeros((8, width), WIDE))
    return jnp.sum(held, axis=0, keepdims=True)


def inverse_of(row_sums):
    return 1.0 / jnp.where(row_sums > 0.0, row_sums, 1.0)


def known_columns(width, known):
    return lax.broadcasted_iota(jnp.int32, (1, width), 1) < known


def fill(target, value):
    for at in range(target.shape[0]):
        target[at] = value


def low_of(z):
    return (z * lax.rsqrt(jnp.sum(z * z, axis=1, keepdims=True) + 1e-06)).astype(LOW)


def weigh_columns(matrix, factors):
    factors = jnp.broadcast_to(factors.astype(LOW), (128, factors.shape[1]))
    return contract(matrix.astype(LOW), factors, 1, 1)


def in_all_tiles(value, width):
    return jnp.concatenate([value] * (width // 128), axis=1)


def first_turn(
    known, z_ref, first_ref, proto_any, queue_any, b_ref, bq_any, sent_any, proto, bq, sent, inv, row_inv, sems
):
    proto_in = pltpu.make_async_copy(proto_any, proto, sems.at[0])
    queue_in = pltpu.make_async_copy(queue_any, bq, sems.at[1])
    queue_out = pltpu.make_async_copy(bq, bq_any, sems.at[2])
    sent_out = pltpu.make_async_copy(sent, sent_any, sems.at[3])
    proto_in.start()
    queue_in.start()
    low = low_of(z_ref[...])
    proto_in.wait()
    b_ref[...] = contract(low, proto[...], 1, 1)
    lines, width = bq.shape
    total_rows = b_ref.shape[0]
    mask = known_columns(width, known)

    def exponentials(rows):
        value = jnp.where(mask, jnp.exp(b_ref[rows, :] * (1.0 / EPS_SINK)), 0.0)
        b_ref[rows, :] = value
        return value

    totals = sum_rows(total_rows, width, exponentials, 8)
    totals = totals + jnp.sum(first_ref[...], axis=0, keepdims=True)
    factors = jnp.where(mask, 1.0 / jnp.where(mask, totals * 0.125, 1.0), 0.0)
    inv[...] = jnp.broadcast_to(factors, inv.shape)
    queue_in.wait()
    row_inv[pl.ds(0, lines), :] = inverse_of(weigh_columns(bq[...], factors))

    def queue(rows):
        factor = jnp.concatenate([inv[...]] * 2, axis=0)
        value = bq[rows, :].astype(WIDE) * factor * in_all_tiles(row_inv[rows, :], width)
        bq[rows, :] = value.astype(LOW)
        return value

    queue_sums = sum_rows(lines, width, queue, 16)
    queue_out.start()
    row_inv[pl.ds(0, total_rows), :] = inverse_of(weigh_columns(b_ref[...], factors))

    def batch(rows):
        value = b_ref[rows, :] * inv[...] * in_all_tiles(row_inv[rows, :], width)
        b_ref[rows, :] = value
        return value

    batch_sums = sum_rows(total_rows, width, batch, 8)
    fill(sent, queue_sums + batch_sums * (1.0 / sent.shape[0]))
    sent_out.start()
    queue_out.wait()
    sent_out.wait()


def column_factor(known, came_ref):
    totals = jnp.sum(came_ref[...], axis=0)
    mask = known_columns(totals.shape[1], known)
    return jnp.where(mask, 1.0 / jnp.where(mask, totals, 1.0), 0.0)


def next_turn(known, came_ref, b_ref, bq_any, sent_any, bq, sent, row_inv, sems):
    queue_in = pltpu.make_async_copy(bq_any, bq, sems.at[0])
    sent_out = pltpu.make_async_copy(sent, sent_any, sems.at[1])
    queue_in.start()
    factors = column_factor(known, came_ref)

    def weigh(source, size):
        total_rows, width = source.shape
        row_inv[pl.ds(0, total_rows), :] = inverse_of(weigh_columns(source[...], factors))

        def body(rows):
            return source[rows, :].astype(WIDE) * in_all_tiles(row_inv[rows, :], width)

        return sum_rows(total_rows, width, body, size)

    batch_sums = weigh(b_ref, 8)
    queue_in.wait()
    fill(sent, weigh(bq, 16) + batch_sums * (1.0 / sent.shape[0]))
    sent_out.start()
    sent_out.wait()


def norm_of_scores(known, z_ref, proto_any, norm_ref, proto, scores, sems):
    proto_in = pltpu.make_async_copy(proto_any, proto, sems.at[0])
    proto_in.start()
    low = low_of(z_ref[...])
    proto_in.wait()
    scores[...] = contract(low, proto[...], 1, 1)
    mask = known_columns(scores.shape[1], known)

    def body(rows):
        raw = scores[rows, :] * (1.0 / SOFTMAX_WARMTH)
        top = jnp.max(jnp.where(mask, raw, -jnp.inf), axis=1, keepdims=True)
        mass = jnp.sum(jnp.where(mask, jnp.exp(raw - top), 0.0), axis=1, keepdims=True)
        norm_ref[rows, :] = top + jnp.log(mass)

    over_rows(scores.shape[0], body)


def last_turn(
    known,
    came_ref,
    b_ref,
    z_ref,
    norm_ref,
    proto_any,
    pairs_any,
    grad_any,
    low_grad_ref,
    loss_ref,
    proto,
    pairs,
    grad,
    scores,
    high,
    rest,
    held,
    inv,
    sems,
):
    proto_in = pltpu.make_async_copy(proto_any, proto, sems.at[0])
    pairs_in = pltpu.make_async_copy(pairs_any, pairs, sems.at[1])
    grad_out = pltpu.make_async_copy(grad, grad_any, sems.at[2])
    proto_in.start()
    pairs_in.start()
    factors = column_factor(known, came_ref)
    inv[...] = factors
    mask = known_columns(factors.shape[1], known)
    size = pairs.shape[1]
    loss_ref[...] = jnp.zeros(loss_ref.shape, WIDE)
    proto_in.wait()
    pairs_in.wait()

    def block(at, carry):
        def here(rows):
            return pl.ds(pl.multiple_of(at * size + rows, 8), ROWS)

        place = pl.ds(pl.multiple_of(at * size, size), size)
        z = z_ref[place, :]
        inv_len = lax.rsqrt(jnp.sum(z * z, axis=1, keepdims=True) + 1e-06)
        scores[...] = contract((z * inv_len).astype(LOW), proto[...], 1, 1)
        for first in range(0, size, ROWS):
            value = b_ref[here(first), :] * inv[...]
            value = value * (1.0 / jnp.sum(value, axis=1, keepdims=True))
            top = value.astype(LOW)
            high[first : first + ROWS, :] = top
            rest[first : first + ROWS, :] = (value - top.astype(WIDE)).astype(LOW)
        pair = pairs[at]
        others = jnp.sum(pair.astype(WIDE), axis=1, keepdims=True)
        inv_others = 1.0 / jnp.maximum(others, 1.0)
        held[...] = contract(pair, high[...], 1, 0) + contract(pair, rest[...], 1, 0)
        for first in range(0, size, ROWS):
            rows = slice(first, first + ROWS)
            targets = held[rows, :] * inv_others[rows]
            logs = scores[rows, :] * (1.0 / SOFTMAX_WARMTH) - norm_ref[here(first), :]
            loss_ref[...] -= jnp.sum(jnp.where(mask, targets * logs, 0.0))
            weight = jnp.sum(targets, axis=1, keepdims=True)
            value = (LOSS_MULTIPLIER / SOFTMAX_WARMTH) * (jnp.exp(logs) * weight - targets)
            grad[here(first), :] = jnp.where(mask, value, 0.0).astype(LOW)
        normed_grad = contract(grad[place, :], proto[...], 1, 0)
        normed = z * inv_len
        along = jnp.sum(normed * normed_grad, axis=1, keepdims=True)
        low_grad_ref[place, :] = (inv_len * (normed_grad - normed * along)).astype(LOW)
        return carry

    lax.fori_loop(0, pairs.shape[0], block, 0)
    grad_out.start()
    grad_out.wait()


def shape(dims, kind=WIDE):
    return jax.ShapeDtypeStruct(dims, kind)


def turn_call(kernel, known, outs, anywhere_out, close, anywhere, scratch, copies):
    near, far = pl.BlockSpec(memory_space=pltpu.VMEM), pl.BlockSpec(memory_space=pltpu.HBM)
    held = sum(value.size * value.dtype.itemsize for value in (*scratch, *close, *outs))
    return pl.pallas_call(
        lambda *refs: kernel(known, *refs),
        out_shape=outs,
        in_specs=[near] * len(close) + [far] * len(anywhere),
        out_specs=[far if at in anywhere_out else near for at in range(len(outs))],
        scratch_shapes=[pltpu.VMEM(value.shape, value.dtype) for value in scratch]
        + [pltpu.SemaphoreType.DMA((copies,))],
        compiler_params=pltpu.CompilerParams(vmem_limit_bytes=min(held + (8 << 20), 60 << 20)),
        name=kernel.__name__,
    )(*close, *[pltpu.with_memory_space_constraint(value, pltpu.HBM) for value in anywhere])


def call_first(known, z, proto, queue, first):
    rows, width, lines, owners = z.shape[0], proto.shape[0], queue.shape[0], first.shape[0]
    sent = shape((owners, 1, width))
    return turn_call(
        first_turn,
        known,
        [shape((rows, width)), shape(queue.shape, LOW), sent],
        (1, 2),
        (z, first),
        (proto, queue),
        [
            shape(proto.shape, LOW),
            shape(queue.shape, LOW),
            sent,
            shape((8, width)),
            shape((max(rows, lines), 128)),
        ],
        4,
    )


def call_next(known, came, b, bq):
    return turn_call(
        next_turn,
        known,
        [shape(came.shape)],
        (0,),
        (came, b),
        (bq,),
        [shape(bq.shape, LOW), shape(came.shape), shape((max(b.shape[0], bq.shape[0]), 128))],
        2,
    )[0]


def call_norm(known, z, proto):
    rows, width = z.shape[0], proto.shape[0]
    return turn_call(
        norm_of_scores,
        known,
        [shape((rows, 1))],
        (),
        (z,),
        (proto,),
        [shape(proto.shape, LOW), shape((rows, width))],
        1,
    )[0]


def call_last(known, came, b, z, norm, proto, pairs):
    width, size = b.shape[1], pairs.shape[1]
    part = (size, width)
    return turn_call(
        last_turn,
        known,
        [shape(b.shape, LOW), shape(z.shape, LOW), shape((8, 128))],
        (0,),
        (came, b, z, norm),
        (proto, pairs),
        [
            shape(proto.shape, LOW),
            shape(pairs.shape, LOW),
            shape(b.shape, LOW),
            shape(part),
            shape(part, LOW),
            shape(part, LOW),
            shape(part),
            shape((1, width)),
        ],
        3,
    )


def after(value, token):
    return lax.optimization_barrier((value, token))[0]


def join(*values):
    return lax.optimization_barrier(values)


def scatter_relative(parts, axis, sent=LOW):
    held = dict(enumerate(parts))
    bit = 1
    while bit < lax.axis_size(axis):
        keys = [k for k in sorted(held) if not k & bit]
        came = swap(jnp.stack([held[k | bit].astype(sent) for k in keys]), axis, bit)
        held = {k: held[k] + came[n].astype(WIDE) for n, k in enumerate(keys)}
        bit *= 2
    return held[0]


def send_order(count):
    low = max(count // 4, 1)
    order = list(range(0, count, low))
    bit = low // 2
    while bit:
        order = order + [r | bit for r in order]
        bit //= 2
    return order


def scatter_staged(blocks, axis):
    count = lax.axis_size(axis)
    low = max(count // 4, 1)
    held = blocks
    bit = 1
    while bit < low:
        half = held.shape[0] // 2
        came = swap(held[half:], axis, bit)
        held = (held[:half].astype(WIDE) + came.astype(WIDE)).astype(LOW)
        bit *= 2
    came = [swap(held[n], axis, n * low) for n in range(1, held.shape[0])]
    return held[0], came


def wide_sum(terms):
    kept, came = terms
    result = kept.astype(WIDE)
    for value in came:
        result = result + value.astype(WIDE)
    return result


def total_hyper(value, axis):
    bit = 1
    while bit < lax.axis_size(axis):
        value = value + swap(value, axis, bit)
        bit *= 2
    return value


def block_at(value, index, size, dim):
    return lax.dynamic_slice_in_dim(value, index * size, size, dim)


def statistics(sums, row_total):
    average = sums[0] / row_total
    variance = sums[1] / row_total - average * average
    return average, lax.rsqrt(variance + NORM_EPS)


def backward_of_norm(grad_out, centred, inv_std, gain_row, sums, row_total):
    return gain_row * inv_std * (grad_out - (sums[0] + centred * sums[1]) / row_total)


def adamw_step(weight, moment_one, moment_two, gradient, learn_rate, weight_decay, step_count):
    moment_new = BETA_ONE * moment_one + (1.0 - BETA_ONE) * gradient
    second_new = BETA_TWO * moment_two + (1.0 - BETA_TWO) * gradient * gradient
    fix_one = 1.0 - jnp.power(BETA_ONE, step_count)
    fix_two = 1.0 - jnp.power(BETA_TWO, step_count)
    update = moment_new / fix_one / (jnp.sqrt(second_new / fix_two) + ADAM_EPS)
    return (weight - learn_rate * (update + weight_decay * weight), moment_new, second_new)


def local(
    images,
    crop_image,
    slot_rows,
    squeeze_weight,
    squeeze_moment,
    squeeze_second,
    spatial_weight,
    spatial_moment,
    spatial_second,
    expand_weight,
    expand_moment,
    expand_second,
    hidden_weight,
    hidden_moment,
    hidden_second,
    project_weight,
    project_moment,
    project_second,
    prototypes,
    proto_moment,
    proto_second,
    norm_params,
    norm_moment,
    norm_second,
    queue_rows,
    queue_valid,
    queue_fill,
    iteration,
):
    dp_count = lax.axis_size("dp")
    dp_at = lax.axis_index("dp")
    chan_count = lax.axis_size("chan")
    chan_at = lax.axis_index("chan")
    crops_dev, map_side, _, in_width = images.shape
    map_area = map_side * map_side
    pixel_rows = crops_dev * map_area
    pixel_total = pixel_rows * dp_count
    crop_total = crops_dev * dp_count
    mid_local = squeeze_weight.shape[1]
    hid_local = hidden_weight.shape[1]
    out_local = in_width // chan_count
    slot_local = squeeze_weight.shape[0]
    slot_total = slot_rows.shape[0]
    mid_width = mid_local * chan_count
    hid_width = hid_local * chan_count

    squeeze_came = spread(squeeze_weight.astype(LOW), "dp")
    tap_local = spatial_weight.shape[0]
    convs_all = lax.all_gather(
        jnp.concatenate([spatial_weight.astype(LOW), expand_weight.astype(LOW)], axis=0), "dp"
    )

    channels = jnp.arange(in_width, dtype=jnp.int32)
    used = (slot_rows < in_width).astype(jnp.int32).reshape(dp_count, slot_local)
    loads = jnp.sum(used, axis=1)
    owners = jnp.arange(dp_count, dtype=jnp.int32)
    firsts = jnp.sum(jnp.where(owners[None, :] < owners[:, None], loads[None, :], 0), axis=1)
    own_used = block_at(used, dp_at, 1, 0)[0]
    own_first = block_at(firsts, dp_at, 1, 0)
    own_at = jnp.arange(slot_local, dtype=jnp.int32)
    own_rank = jnp.sum(jnp.where(own_at[None, :] < own_at[:, None], own_used[None, :], 0), axis=1)
    cell = slot_local // dp_count
    share = in_width // dp_count
    target = (own_first + own_rank) % dp_count * cell + own_rank // dp_count
    deal_hot = ((target[None, :] == own_at[:, None]) & (own_used[None, :] > 0)).astype(LOW)
    head_low = jnp.concatenate([hidden_weight.astype(LOW), project_weight.astype(LOW)], axis=1)
    dealt = contract(deal_hot, head_low, 1, 0).astype(LOW)
    ranks = (
        jnp.arange(cell, dtype=jnp.int32)[None, :] * dp_count + (dp_at - firsts[:, None]) % dp_count
    )
    share_at = jnp.where(ranks < loads[:, None], (firsts[:, None] + ranks) // dp_count, -1)
    share_at = share_at.reshape(slot_local)
    place, rank = slot_of_channel(slot_rows, in_width)
    slot_blocks = slot_rows.reshape(dp_count, slot_local)
    slot_sent = jnp.concatenate(
        [lax.dynamic_index_in_dim(slot_blocks, dp_at ^ r, 0, False) for r in send_order(dp_count)]
    )
    own_slots = slot_sent[:slot_local]
    place_dealt = (rank % dp_count * share + rank // dp_count)[:in_width]

    proto_count = prototypes.shape[1]
    proto_low = jnp.pad(prototypes.astype(LOW).T, ((0, -proto_count % 256), (0, 0)))
    proto_width = proto_low.shape[0]
    queue_len = queue_rows.shape[0]
    slot_index = dp_at * queue_len + jnp.arange(queue_len, dtype=jnp.int32)
    queue_live = ((queue_valid > 0) & (slot_index < queue_fill[0])).astype(WIDE)
    queue_live = jnp.pad(queue_live, (0, -queue_len % ROWS))
    queue_similarity = contract(
        jnp.pad(queue_rows, ((0, -queue_len % ROWS), (0, 0))), proto_low, 1, 1
    )
    queue_codes = jnp.where(
        (jnp.arange(proto_width) < proto_count)[None, :],
        jnp.exp(queue_similarity / EPS_SINK) * queue_live[:, None],
        0.0,
    )
    queue_mass = jnp.sum(queue_codes, axis=0)
    queue_codes = queue_codes.astype(LOW)
    squeeze_came, queue_codes, queue_mass, slot_sent, proto_low = join(
        squeeze_came, queue_codes, queue_mass, slot_sent, proto_low
    )
    straight = jnp.zeros((1,), jnp.int32)
    turned = (chan_at * out_local).astype(jnp.int32).reshape(1)
    squeeze_rows = pick_rows(place, straight, [squeeze_came], in_width, 0, slot_local)

    norm_rows = norm_params[:, 0, :]
    first_norm = norm_rows[:, :mid_local]
    second_norm = norm_rows[:, mid_local : 2 * mid_local]
    third_norm = norm_rows[:, 2 * mid_local : 2 * mid_local + out_local]
    head_norm = norm_rows[:, 2 * mid_local + out_local :]

    def inner_layer(pre_act, norm, token=None):
        sums = jnp.stack([jnp.sum(pre_act, axis=0), jnp.sum(pre_act * pre_act, axis=0)])
        if token is not None:
            sums = after(sums, token)
        near = sums[0] / pixel_rows
        raw_all = jnp.concatenate(gather_relative((pre_act - near).astype(LOW), "chan"), axis=1)
        average, inv_std = statistics(total(sums, "dp"), pixel_total)
        scale = inv_std * norm[0]
        affine = jnp.stack([scale, norm[1] - (average - near) * scale])
        affine_all = jnp.concatenate(gather_relative(affine, "chan"), axis=1)
        act_all = jax.nn.silu(raw_all.astype(WIDE) * affine_all[0] + affine_all[1]).astype(LOW)
        return act_all, average, inv_std

    step_count = iteration[0].astype(WIDE)

    def step(weight, moment, second, gradient, rate, decay=DECAY_RATE):
        return adamw_step(weight, moment, second, gradient, rate, decay, step_count)

    pixels = images.transpose(1, 2, 0, 3).reshape(pixel_rows, in_width)
    pre_one = contract(pixels, squeeze_rows, 1, 0)
    inner_one, average_one, inv_one = inner_layer(pre_one, first_norm)
    dealt = lax.all_to_all(after(dealt, average_one).reshape(dp_count, cell, -1), "dp", 0, 0)
    def relative_blocks(value, size, dim):
        return [block_at(value, chan_at ^ r, size, dim) for r in range(chan_count)]

    spatial_rel = assemble(
        convs_all, chan_at.astype(jnp.int32).reshape(1), tap_local, 9, chan_count
    ).reshape(3, 3, mid_width, mid_local)
    maps_one = inner_one.reshape(map_side, map_side, crops_dev, mid_width)
    conv_dims = lax.ConvDimensionNumbers((2, 3, 0, 1), (3, 2, 0, 1), (2, 3, 0, 1))
    pre_two = lax.conv_general_dilated(
        maps_one,
        spatial_rel,
        (1, 1),
        ((1, 1), (1, 1)),
        dimension_numbers=conv_dims,
        preferred_element_type=WIDE,
    ).reshape(pixel_rows, mid_local)
    pre_two, dealt = join(pre_two, dealt)
    share_hot = (share_at[None, :] == channels[:share, None]).astype(LOW)
    head_all = lax.all_gather(
        contract(share_hot, dealt.reshape(slot_local, -1), 1, 0).astype(LOW),
        "dp",
        axis=0,
        tiled=True,
    )

    inner_two, average_two, inv_two = inner_layer(pre_two, second_norm)

    expand_rows = pick_rows(place, turned, [convs_all], in_width, tap_local, slot_local)

    def swap_blocks(blocks):
        return jnp.concatenate(
            [blocks[0]] + [swap(blocks[r], "chan", r) for r in range(1, chan_count)], axis=1
        )

    expand_rel = swap_blocks(
        [expand_rows[r * out_local : (r + 1) * out_local] for r in range(chan_count)]
    )
    squeeze_rel = swap_blocks(relative_blocks(squeeze_rows, out_local, 0))
    pre_three = contract(inner_two, expand_rel, 1, 1)
    sent_three = [
        jnp.sum(pre_three, axis=0),
        jnp.sum(pre_three * pre_three, axis=0),
        queue_mass,
        crop_image.astype(WIDE),
    ]
    came_three = spread(jnp.concatenate(sent_three), "dp")
    sums_three = jnp.sum(came_three[:, : 2 * out_local], axis=0).reshape(2, out_local)
    queue_first = came_three[:, 2 * out_local :]
    average_three, inv_three = statistics(sums_three, pixel_total)
    centred_three = (pre_three - average_three) * inv_three
    residual_in = block_at(pixels, chan_at, out_local, 1).astype(WIDE)
    summed = centred_three * third_norm[0] + third_norm[1] + residual_in
    block_rows = jax.nn.silu(summed)
    block_out = block_rows.astype(LOW).reshape(map_side, map_side, crops_dev, out_local)
    block_out = block_out.transpose(2, 0, 1, 3)
    pooled = jnp.mean(block_rows.reshape(map_area, crops_dev, out_local), axis=0).astype(LOW)
    pooled_dev = lax.all_gather(pooled, "chan", axis=1, tiled=True)
    pooled_all = lax.all_gather(pooled_dev, "dp", axis=0, tiled=True)

    dealt_hot = (place_dealt[:, None] == channels[None, :]).astype(LOW)
    pooled_dealt = contract(pooled_dev, dealt_hot, 1, 0).astype(LOW)
    pooled_dealt, head_all = join(pooled_dealt, head_all)
    hidden_dev = contract(pooled_dealt, head_all[:, :hid_local], 1, 0)
    own_place = block_at(place_dealt, chan_at, hid_local, 0)
    own_dealt_hot = (own_place[:, None] == channels[None, :]).astype(LOW)
    project_rows = contract(own_dealt_hot, head_all[:, hid_local:], 1, 0).astype(LOW)
    near_head = jnp.mean(hidden_dev, axis=0, keepdims=True).astype(LOW)
    hidden_sent = (hidden_dev - near_head.astype(WIDE)).astype(LOW)
    hidden_came = spread(jnp.concatenate([hidden_sent, near_head], axis=0), "dp")
    hidden_rows = contract(
        (after(place_dealt, hidden_dev)[:, None] == channels[None, :]).astype(LOW),
        head_all[:, :hid_local],
        1,
        0,
    ).astype(LOW)
    hidden_came, hidden_rows = join(hidden_came, hidden_rows)
    hidden_pre = (
        hidden_came[:, :crops_dev].astype(WIDE) + hidden_came[:, crops_dev:].astype(WIDE)
    ).reshape(
        crop_total, hid_local
    )
    head_sums = jnp.stack([jnp.sum(hidden_pre, axis=0), jnp.sum(hidden_pre * hidden_pre, axis=0)])
    average_head, inv_head = statistics(head_sums, crop_total)
    centred_head = (hidden_pre - average_head) * inv_head
    normed_head = centred_head * head_norm[0] + head_norm[1]
    hidden_act = jax.nn.silu(normed_head).astype(LOW)
    project_out = total_hyper(contract(hidden_act, project_rows, 1, 0), "chan")
    block_rows_of = min(crop_total, max(BLOCK, crops_dev))
    labels = queue_first[:, proto_width:].reshape(-1, block_rows_of)
    crop_index = jnp.arange(block_rows_of, dtype=jnp.int32)
    same_image = (
        (labels[:, :, None] == labels[:, None, :])
        & (crop_index[:, None] != crop_index[None, :])
        & (crop_index[:, None] // crops_dev == crop_index[None, :] // crops_dev)
    )
    pairs = same_image.astype(LOW)

    codes, queue_codes, sent = call_first(
        proto_count, project_out, proto_low, queue_codes, queue_first[:, :proto_width]
    )
    came = lax.all_to_all(sent, "dp", 0, 0)
    log_norm = call_norm(proto_count, project_out, proto_low)
    for turn_index in range(2, SINK_ITERS):
        came = lax.all_to_all(call_next(proto_count, came, codes, queue_codes), "dp", 0, 0)
    came, pooled_all = join(came, pooled_all)
    score_gradient, project_low_grad, loss_total = call_last(
        proto_count, came, codes, project_out, log_norm, proto_low, pairs
    )
    loss = loss_total[0, :1] / crop_total
    normed_low = low_of(project_out)
    hidden_grad_act = contract(project_low_grad, project_rows, 1, 1) * silu_slope(normed_head)
    head_grads = jnp.stack(
        [jnp.sum(hidden_grad_act, axis=0), jnp.sum(hidden_grad_act * centred_head, axis=0)]
    )
    head_pre_low = backward_of_norm(
        hidden_grad_act, centred_head, inv_head, head_norm[0], head_grads, crop_total
    ).astype(LOW)
    pooled_terms = contract(block_at(head_pre_low, dp_at, crops_dev, 0), hidden_rows, 1, 1)
    pooled_grad = scatter_relative(relative_blocks(pooled_terms, out_local, 1), "chan", WIDE)

    spread_grad = jnp.broadcast_to(
        pooled_grad[None] / map_area, (map_area, crops_dev, out_local)
    ).reshape(pixel_rows, out_local)
    sum_grad = spread_grad * silu_slope(summed)
    third_grads = total(
        jnp.stack([jnp.sum(sum_grad, axis=0), jnp.sum(sum_grad * centred_three, axis=0)]), "dp"
    )
    project_grad = jnp.concatenate(
        gather_relative(contract(hidden_act, project_low_grad, 0, 0).astype(LOW), "chan")
    )
    third_grads, project_grad = join(third_grads, project_grad)
    third_low = backward_of_norm(
        sum_grad, centred_three, inv_three, third_norm[0], third_grads, pixel_total
    ).astype(LOW)

    def column_parts(terms):
        return [terms[:, r * mid_local : (r + 1) * mid_local] for r in range(chan_count)]

    def inner_sums(summed_terms, pre_act, average, inv_std, norm):
        centred = (pre_act - average) * inv_std
        grad = summed_terms * silu_slope(centred * norm[0] + norm[1])
        sums = jnp.stack([jnp.sum(grad, axis=0), jnp.sum(grad * centred, axis=0)])
        return grad, centred, sums

    def slot_terms(grad_rows, turned):
        slot_hot = ((slot_sent ^ (turned * out_local))[:, None] == channels[None, :]).astype(LOW)
        terms = contract(slot_hot, grad_rows, 1, 0).astype(LOW)
        return terms.reshape(dp_count, slot_local, mid_local)

    second_sum = scatter_relative(column_parts(contract(third_low, expand_rel, 1, 0)), "chan")
    expand_terms = contract(third_low, inner_two, 0, 0).astype(LOW)
    proto_grad = contract(score_gradient, normed_low, 0, 0)[:proto_count].T
    proto_new = step(prototypes, proto_moment, proto_second, proto_grad, 0.1)
    turned_hot = ((own_slots ^ (chan_at * hid_local))[:, None] == channels[None, :]).astype(LOW)
    slot_project = contract(turned_hot, project_grad, 1, 0)
    project_new = step(
        project_weight, project_moment, project_second, slot_project, hid_width ** (-0.5)
    )
    second_sum, expand_terms, *others_new = join(
        second_sum, expand_terms, *proto_new, *project_new
    )
    grad_two, centred_two, second_sums = inner_sums(
        second_sum, pre_two, average_two, inv_two, second_norm
    )
    expand_parts = column_parts(expand_terms)
    expand_grad = jnp.concatenate(
        [expand_parts[0]] + [swap(expand_parts[r], "chan", r) for r in range(1, chan_count)], axis=0
    )
    slot_expand = slot_terms(expand_grad, chan_at)
    second_grads, slot_expand = join(total(second_sums, "dp"), slot_expand)
    expand_came = scatter_staged(slot_expand, "dp")
    second_low = backward_of_norm(
        grad_two, centred_two, inv_two, second_norm[0], second_grads, pixel_total
    ).astype(LOW)
    maps_two = second_low.reshape(map_side, map_side, crops_dev, mid_local)
    first_terms = lax.conv_general_dilated(
        maps_two,
        spatial_rel[::-1, ::-1].transpose(0, 1, 3, 2),
        (1, 1),
        ((1, 1), (1, 1)),
        dimension_numbers=conv_dims,
        preferred_element_type=WIDE,
    ).reshape(pixel_rows, mid_width)
    first_sum = scatter_relative(column_parts(first_terms), "chan")
    spatial_terms = lax.conv_general_dilated(
        maps_one,
        maps_two,
        (1, 1),
        ((1, 1), (1, 1)),
        dimension_numbers=lax.ConvDimensionNumbers((3, 2, 0, 1), (3, 2, 0, 1), (2, 3, 0, 1)),
        preferred_element_type=WIDE,
    ).reshape(9, mid_width, mid_local)
    spatial_sent = deal_rows(
        spatial_terms.astype(LOW).reshape(9 * mid_width, mid_local),
        jnp.stack([dp_at, chan_at]).astype(jnp.int32),
        dp_count,
        9,
        chan_count,
    )
    first_sum, spatial_sent = join(first_sum, spatial_sent)
    spatial_came = scatter_staged(spatial_sent, "dp")
    own_hot = (own_slots[:, None] == channels[None, :]).astype(LOW)
    slot_hidden = contract(contract(pooled_all, own_hot, 1, 1).astype(LOW), head_pre_low, 0, 0)
    hidden_new = step(hidden_weight, hidden_moment, hidden_second, slot_hidden, in_width ** (-0.5))
    grad_one, centred_one, first_sums = inner_sums(
        first_sum, pre_one, average_one, inv_one, first_norm
    )
    first_grads, *hidden_new = join(total_hyper(first_sums, "dp"), *hidden_new)
    first_low = backward_of_norm(
        grad_one, centred_one, inv_one, first_norm[0], first_grads, pixel_total
    ).astype(LOW)
    squeeze_grad = contract(pixels, first_low, 0, 0).astype(LOW)
    squeeze_terms = slot_terms(squeeze_grad, 0)
    squeeze_came = scatter_staged(squeeze_terms, "dp")
    first_all = jnp.concatenate(gather_relative(after(first_low, squeeze_terms), "chan"), axis=1)
    images_grad = contract(first_all, squeeze_rel, 1, 1) + sum_grad
    images_grad = images_grad.reshape(map_side, map_side, crops_dev, out_local).transpose(2, 0, 1, 3)
    spatial_came, expand_came, _ = join(spatial_came, expand_came, squeeze_terms)
    images_grad, squeeze_came = join(images_grad, squeeze_came)
    slot_squeeze, slot_spatial, slot_expand = [
        wide_sum(came) for came in (squeeze_came, spatial_came, expand_came)
    ]
    norm_gradient = jnp.concatenate([first_grads, second_grads, third_grads, head_grads], axis=1)
    norm_gradient = norm_gradient[::-1].reshape(norm_params.shape)
    return (
        block_out,
        loss,
        images_grad,
        *step(squeeze_weight, squeeze_moment, squeeze_second, slot_squeeze, in_width ** (-0.5)),
        *step(
            spatial_weight, spatial_moment, spatial_second, slot_spatial, (9 * mid_width) ** (-0.5)
        ),
        *step(expand_weight, expand_moment, expand_second, slot_expand, mid_width ** (-0.5)),
        *hidden_new,
        *others_new[3:],
        *others_new[:3],
        *step(norm_params, norm_moment, norm_second, norm_gradient, 0.5, 0.0),
    )


def solution(mesh):
    rows, both, whole = P("dp", None), P("dp", "chan"), P()
    maps = P("dp", None, None, "chan")
    norm = P(None, "chan", None)
    placed = (
        (P("dp", None, None, None), P("dp"), whole)
        + (both,) * 12
        + (rows,) * 3
        + (whole,) * 3
        + (norm,) * 3
        + (rows, P("dp"), whole, whole)
    )
    return jax.shard_map(
        local,
        mesh=mesh,
        in_specs=placed,
        out_specs=(maps, whole, maps) + (both,) * 12 + (rows,) * 3 + (whole,) * 3 + (norm,) * 3,
        check_vma=False,
    )
```

```python
import math

import jax
import jax.numpy as jnp
from jax import lax
from jax.experimental import pallas as pl
from jax.experimental.pallas import tpu as pltpu
from jax.sharding import PartitionSpec as P

SINK_ITERS = 3
PRECISE = lax.Precision.HIGHEST
EPS_SINK = 0.05
SOFTMAX_WARMTH = 0.1
LOSS_MULTIPLIER = 256.0
NORM_EPS = 1e-05
BETA_ONE = 0.5
BETA_TWO = 0.5
ADAM_EPS = 1e-08
DECAY_RATE = 1e-06
LOW = jnp.bfloat16
WIDE = jnp.float32


def contract(left, right, left_dim, right_dim):
    return lax.dot_general(
        left, right, (((left_dim,), (right_dim,)), ((), ())), preferred_element_type=WIDE
    )


def silu_slope(value):
    sigma = jax.nn.sigmoid(value)
    return sigma * (1.0 + value * (1.0 - sigma))


def spread(value, axis):
    count = lax.axis_size(axis)
    return lax.all_to_all(jnp.broadcast_to(value[None], (count,) + value.shape), axis, 0, 0)


def total(value, axis):
    return jnp.sum(spread(value, axis).astype(WIDE), axis=0)


def swap(value, axis, bit):
    return lax.ppermute(value, axis, [(at, at ^ bit) for at in range(lax.axis_size(axis))])


def gather_relative(value, axis):
    held = {0: value}
    bit = lax.axis_size(axis) // 2
    while bit:
        keys = sorted(held)
        came = swap(jnp.stack([held[k] for k in keys]), axis, bit)
        held.update({k ^ bit: came[n] for n, k in enumerate(keys)})
        bit //= 2
    return [held[k] for k in range(lax.axis_size(axis))]


def invert_kernel(slots_ref, place_ref, rank_ref):
    count = slots_ref.shape[0]
    channels = place_ref.shape[0] - 128

    def step(at, rank):
        for n in range(16):
            slot = at * 16 + n
            channel = slots_ref[slot]
            place_ref[channel] = slot
            rank_ref[channel] = rank
            rank = rank + jnp.where(channel < channels, 1, 0)
        return rank

    lax.fori_loop(0, count // 16, step, jnp.int32(0))


def slot_of_channel(slot_rows, channels):
    smem = pl.BlockSpec(memory_space=pltpu.SMEM)
    return pl.pallas_call(
        invert_kernel,
        out_shape=[jax.ShapeDtypeStruct((channels + 128,), jnp.int32)] * 2,
        in_specs=[smem],
        out_specs=[smem] * 2,
        name="slot_of_channel",
    )(slot_rows)


def pick_kernel(first, count, place_ref, turn_ref, *refs):
    *blocks, out_ref, wide, picked = refs
    at = 0
    for block in blocks:
        for part in [block.at[k] for k in range(block.shape[0])] if len(block.shape) == 3 else [block]:
            wide[at : at + count, :] = part[first : first + count, :].astype(WIDE)
            at += count

    def step(group, carry):
        for n in range(8):
            row = group * 8 + n
            picked[pl.ds(row, 1), :] = wide[pl.ds(place_ref[(group * 8 ^ turn_ref[0]) + n], 1), :]
        return carry

    lax.fori_loop(0, out_ref.shape[0] // 8, step, 0)
    out_ref[...] = picked[...].astype(out_ref.dtype)


def pick_rows(place, turn, blocks, rows, first, count):
    width = blocks[0].shape[-1]
    held = sum(block.size // (width * block.shape[-2]) for block in blocks) * count
    vmem = pl.BlockSpec()
    return pl.pallas_call(
        lambda *refs: pick_kernel(first, count, *refs),
        out_shape=jax.ShapeDtypeStruct((rows, width), LOW),
        in_specs=[pl.BlockSpec(memory_space=pltpu.SMEM)] * 2 + [vmem] * len(blocks),
        out_specs=vmem,
        scratch_shapes=[pltpu.VMEM((held, width), WIDE), pltpu.VMEM((rows, width), WIDE)],
        compiler_params=pltpu.CompilerParams(vmem_limit_bytes=12 << 20),
        cost_estimate=pl.CostEstimate(
            flops=0, bytes_accessed=2 * (held + rows) * width, transcendentals=0
        ),
        name="pick_rows",
    )(place, turn, *blocks)


def assemble_kernel(taps, chan_count, rows, at_ref, held_ref, out_ref):
    per_tap = out_ref.shape[0] // taps
    per_chan = per_tap // chan_count
    size = math.gcd(rows, per_chan)
    for row in range(0, out_ref.shape[0], size):
        tap, inner = divmod(row, per_tap)
        chan, rest = divmod(inner, per_chan)
        target = pl.multiple_of((chan ^ at_ref[0]) * per_chan + tap * per_tap + rest, size)
        owner, source = divmod(row, rows)
        out_ref[pl.ds(target, size), :] = held_ref[owner, source : source + size, :]


def assemble(held, at, rows, taps, chan_count):
    vmem = pl.BlockSpec()
    return pl.pallas_call(
        lambda *refs: assemble_kernel(taps, chan_count, rows, *refs),
        out_shape=jax.ShapeDtypeStruct((rows * held.shape[0], held.shape[2]), LOW),
        in_specs=[pl.BlockSpec(memory_space=pltpu.SMEM), vmem],
        out_specs=vmem,
        compiler_params=pltpu.CompilerParams(vmem_limit_bytes=12 << 20),
        cost_estimate=pl.CostEstimate(
            flops=0, bytes_accessed=4 * rows * held.shape[0] * held.shape[2], transcendentals=0
        ),
        name="assemble",
    )(at, held)


def deal_kernel(taps, chan_count, order, at_ref, terms_ref, out_ref):
    rows = out_ref.shape[1]
    per_tap = terms_ref.shape[0] // taps
    per_chan = per_tap // chan_count
    size = math.gcd(rows, per_chan)
    for n, r in enumerate(order):
        for start in range(0, rows, size):
            row = (at_ref[0] ^ r) * rows + start
            tap, inner = row // per_tap, row % per_tap
            chan, rest = inner // per_chan, inner % per_chan
            source = tap * per_tap + (chan ^ at_ref[1]) * per_chan + rest
            source = pl.multiple_of(source, size)
            out_ref[n, start : start + size, :] = terms_ref[pl.ds(source, size), :]


def deal_rows(terms, at, owners, taps, chan_count):
    order = send_order(owners)
    vmem = pl.BlockSpec()
    return pl.pallas_call(
        lambda *refs: deal_kernel(taps, chan_count, order, *refs),
        out_shape=jax.ShapeDtypeStruct((owners, terms.shape[0] // owners, terms.shape[1]), LOW),
        in_specs=[pl.BlockSpec(memory_space=pltpu.SMEM), vmem],
        out_specs=vmem,
        compiler_params=pltpu.CompilerParams(vmem_limit_bytes=12 << 20),
        cost_estimate=pl.CostEstimate(flops=0, bytes_accessed=4 * terms.size, transcendentals=0),
        name="deal_rows",
    )(at, terms)


ROWS = 32
BLOCK = 128


def whole(count):
    return [pl.BlockSpec()] * count


def over_rows(total_rows, body, size=ROWS):
    def step(at, carry):
        body(pl.ds(pl.multiple_of(at * size, size), size))
        return carry

    lax.fori_loop(0, total_rows // size, step, 0)


def sum_rows(total_rows, width, body, size):
    def step(at, held):
        value = body(pl.ds(pl.multiple_of(at * size, size), size))
        for first in range(0, size, 8):
            held = held + value[first : first + 8]
        return held

    held = lax.fori_loop(0, total_rows // size, step, jnp.zeros((8, width), WIDE))
    return jnp.sum(held, axis=0, keepdims=True)


def inverse_of(row_sums):
    return 1.0 / jnp.where(row_sums > 0.0, row_sums, 1.0)


def known_columns(width, known):
    return lax.broadcasted_iota(jnp.int32, (1, width), 1) < known


def fill(target, value):
    for at in range(target.shape[0]):
        target[at] = value


def low_of(z):
    return (z * lax.rsqrt(jnp.sum(z * z, axis=1, keepdims=True) + 1e-06)).astype(LOW)


def weigh_columns(matrix, factors):
    factors = jnp.broadcast_to(factors.astype(LOW), (128, factors.shape[1]))
    return contract(matrix.astype(LOW), factors, 1, 1)


def in_all_tiles(value, width):
    return jnp.concatenate([value] * (width // 128), axis=1)


def first_turn(
    known, z_ref, first_ref, proto_any, queue_any, b_ref, bq_any, sent_any, proto, bq, sent, inv, row_inv, sems
):
    proto_in = pltpu.make_async_copy(proto_any, proto, sems.at[0])
    queue_in = pltpu.make_async_copy(queue_any, bq, sems.at[1])
    queue_out = pltpu.make_async_copy(bq, bq_any, sems.at[2])
    sent_out = pltpu.make_async_copy(sent, sent_any, sems.at[3])
    proto_in.start()
    queue_in.start()
    low = low_of(z_ref[...])
    proto_in.wait()
    b_ref[...] = contract(low, proto[...], 1, 1)
    lines, width = bq.shape
    total_rows = b_ref.shape[0]
    mask = known_columns(width, known)

    def exponentials(rows):
        value = jnp.where(mask, jnp.exp(b_ref[rows, :] * (1.0 / EPS_SINK)), 0.0)
        b_ref[rows, :] = value
        return value

    totals = sum_rows(total_rows, width, exponentials, 8)
    totals = totals + jnp.sum(first_ref[...], axis=0, keepdims=True)
    factors = jnp.where(mask, 1.0 / jnp.where(mask, totals * 0.125, 1.0), 0.0)
    inv[...] = jnp.broadcast_to(factors, inv.shape)
    queue_in.wait()
    row_inv[pl.ds(0, lines), :] = inverse_of(weigh_columns(bq[...], factors))

    def queue(rows):
        factor = jnp.concatenate([inv[...]] * 2, axis=0)
        value = bq[rows, :].astype(WIDE) * factor * in_all_tiles(row_inv[rows, :], width)
        bq[rows, :] = value.astype(LOW)
        return value

    queue_sums = sum_rows(lines, width, queue, 16)
    queue_out.start()
    row_inv[pl.ds(0, total_rows), :] = inverse_of(weigh_columns(b_ref[...], factors))

    def batch(rows):
        value = b_ref[rows, :] * inv[...] * in_all_tiles(row_inv[rows, :], width)
        b_ref[rows, :] = value
        return value

    batch_sums = sum_rows(total_rows, width, batch, 8)
    fill(sent, queue_sums + batch_sums * (1.0 / sent.shape[0]))
    sent_out.start()
    queue_out.wait()
    sent_out.wait()


def column_factor(known, came_ref):
    totals = jnp.sum(came_ref[...], axis=0)
    mask = known_columns(totals.shape[1], known)
    return jnp.where(mask, 1.0 / jnp.where(mask, totals, 1.0), 0.0)


def next_turn(known, came_ref, b_ref, bq_any, sent_any, bq, sent, row_inv, sems):
    queue_in = pltpu.make_async_copy(bq_any, bq, sems.at[0])
    sent_out = pltpu.make_async_copy(sent, sent_any, sems.at[1])
    queue_in.start()
    factors = column_factor(known, came_ref)

    def weigh(source, size):
        total_rows, width = source.shape
        row_inv[pl.ds(0, total_rows), :] = inverse_of(weigh_columns(source[...], factors))

        def body(rows):
            return source[rows, :].astype(WIDE) * in_all_tiles(row_inv[rows, :], width)

        return sum_rows(total_rows, width, body, size)

    batch_sums = weigh(b_ref, 8)
    queue_in.wait()
    fill(sent, weigh(bq, 16) + batch_sums * (1.0 / sent.shape[0]))
    sent_out.start()
    sent_out.wait()


def norm_of_scores(known, z_ref, proto_any, norm_ref, proto, scores, sems):
    proto_in = pltpu.make_async_copy(proto_any, proto, sems.at[0])
    proto_in.start()
    low = low_of(z_ref[...])
    proto_in.wait()
    scores[...] = contract(low, proto[...], 1, 1)
    mask = known_columns(scores.shape[1], known)

    def body(rows):
        raw = scores[rows, :] * (1.0 / SOFTMAX_WARMTH)
        top = jnp.max(jnp.where(mask, raw, -jnp.inf), axis=1, keepdims=True)
        mass = jnp.sum(jnp.where(mask, jnp.exp(raw - top), 0.0), axis=1, keepdims=True)
        norm_ref[rows, :] = top + jnp.log(mass)

    over_rows(scores.shape[0], body)


def last_turn(
    known,
    came_ref,
    b_ref,
    z_ref,
    norm_ref,
    proto_any,
    pairs_any,
    grad_any,
    low_grad_ref,
    loss_ref,
    proto,
    pairs,
    grad,
    scores,
    high,
    rest,
    held,
    inv,
    sems,
):
    proto_in = pltpu.make_async_copy(proto_any, proto, sems.at[0])
    pairs_in = pltpu.make_async_copy(pairs_any, pairs, sems.at[1])
    grad_out = pltpu.make_async_copy(grad, grad_any, sems.at[2])
    proto_in.start()
    pairs_in.start()
    factors = column_factor(known, came_ref)
    inv[...] = factors
    mask = known_columns(factors.shape[1], known)
    size = pairs.shape[1]
    loss_ref[...] = jnp.zeros(loss_ref.shape, WIDE)
    proto_in.wait()
    pairs_in.wait()

    def block(at, carry):
        def here(rows):
            return pl.ds(pl.multiple_of(at * size + rows, 8), ROWS)

        place = pl.ds(pl.multiple_of(at * size, size), size)
        z = z_ref[place, :]
        inv_len = lax.rsqrt(jnp.sum(z * z, axis=1, keepdims=True) + 1e-06)
        scores[...] = contract((z * inv_len).astype(LOW), proto[...], 1, 1)
        for first in range(0, size, ROWS):
            value = b_ref[here(first), :] * inv[...]
            value = value * (1.0 / jnp.sum(value, axis=1, keepdims=True))
            top = value.astype(LOW)
            high[first : first + ROWS, :] = top
            rest[first : first + ROWS, :] = (value - top.astype(WIDE)).astype(LOW)
        pair = pairs[at]
        others = jnp.sum(pair.astype(WIDE), axis=1, keepdims=True)
        inv_others = 1.0 / jnp.maximum(others, 1.0)
        held[...] = contract(pair, high[...], 1, 0) + contract(pair, rest[...], 1, 0)
        for first in range(0, size, ROWS):
            rows = slice(first, first + ROWS)
            targets = held[rows, :] * inv_others[rows]
            logs = scores[rows, :] * (1.0 / SOFTMAX_WARMTH) - norm_ref[here(first), :]
            loss_ref[...] -= jnp.sum(jnp.where(mask, targets * logs, 0.0))
            weight = jnp.sum(targets, axis=1, keepdims=True)
            value = (LOSS_MULTIPLIER / SOFTMAX_WARMTH) * (jnp.exp(logs) * weight - targets)
            grad[here(first), :] = jnp.where(mask, value, 0.0).astype(LOW)
        normed_grad = contract(grad[place, :], proto[...], 1, 0)
        normed = z * inv_len
        along = jnp.sum(normed * normed_grad, axis=1, keepdims=True)
        low_grad_ref[place, :] = (inv_len * (normed_grad - normed * along)).astype(LOW)
        return carry

    lax.fori_loop(0, pairs.shape[0], block, 0)
    grad_out.start()
    grad_out.wait()


def shape(dims, kind=WIDE):
    return jax.ShapeDtypeStruct(dims, kind)


def turn_call(kernel, known, outs, anywhere_out, close, anywhere, scratch, copies):
    near, far = pl.BlockSpec(memory_space=pltpu.VMEM), pl.BlockSpec(memory_space=pltpu.HBM)
    held = sum(value.size * value.dtype.itemsize for value in (*scratch, *close, *outs))
    return pl.pallas_call(
        lambda *refs: kernel(known, *refs),
        out_shape=outs,
        in_specs=[near] * len(close) + [far] * len(anywhere),
        out_specs=[far if at in anywhere_out else near for at in range(len(outs))],
        scratch_shapes=[pltpu.VMEM(value.shape, value.dtype) for value in scratch]
        + [pltpu.SemaphoreType.DMA((copies,))],
        compiler_params=pltpu.CompilerParams(vmem_limit_bytes=min(held + (8 << 20), 60 << 20)),
        name=kernel.__name__,
    )(*close, *[pltpu.with_memory_space_constraint(value, pltpu.HBM) for value in anywhere])


def call_first(known, z, proto, queue, first):
    rows, width, lines, owners = z.shape[0], proto.shape[0], queue.shape[0], first.shape[0]
    sent = shape((owners, 1, width))
    return turn_call(
        first_turn,
        known,
        [shape((rows, width)), shape(queue.shape, LOW), sent],
        (1, 2),
        (z, first),
        (proto, queue),
        [
            shape(proto.shape, LOW),
            shape(queue.shape, LOW),
            sent,
            shape((8, width)),
            shape((max(rows, lines), 128)),
        ],
        4,
    )


def call_next(known, came, b, bq):
    return turn_call(
        next_turn,
        known,
        [shape(came.shape)],
        (0,),
        (came, b),
        (bq,),
        [shape(bq.shape, LOW), shape(came.shape), shape((max(b.shape[0], bq.shape[0]), 128))],
        2,
    )[0]


def call_norm(known, z, proto):
    rows, width = z.shape[0], proto.shape[0]
    return turn_call(
        norm_of_scores,
        known,
        [shape((rows, 1))],
        (),
        (z,),
        (proto,),
        [shape(proto.shape, LOW), shape((rows, width))],
        1,
    )[0]


def call_last(known, came, b, z, norm, proto, pairs):
    width, size = b.shape[1], pairs.shape[1]
    part = (size, width)
    return turn_call(
        last_turn,
        known,
        [shape(b.shape, LOW), shape(z.shape, LOW), shape((8, 128))],
        (0,),
        (came, b, z, norm),
        (proto, pairs),
        [
            shape(proto.shape, LOW),
            shape(pairs.shape, LOW),
            shape(b.shape, LOW),
            shape(part),
            shape(part, LOW),
            shape(part, LOW),
            shape(part),
            shape((1, width)),
        ],
        3,
    )


def after(value, token):
    return lax.optimization_barrier((value, token))[0]


def join(*values):
    return lax.optimization_barrier(values)


def scatter_relative(parts, axis, sent=LOW):
    held = dict(enumerate(parts))
    bit = 1
    while bit < lax.axis_size(axis):
        keys = [k for k in sorted(held) if not k & bit]
        came = swap(jnp.stack([held[k | bit].astype(sent) for k in keys]), axis, bit)
        held = {k: held[k] + came[n].astype(WIDE) for n, k in enumerate(keys)}
        bit *= 2
    return held[0]


def send_order(count):
    low = max(count // 4, 1)
    order = list(range(0, count, low))
    bit = low // 2
    while bit:
        order = order + [r | bit for r in order]
        bit //= 2
    return order


def scatter_staged(blocks, axis):
    count = lax.axis_size(axis)
    low = max(count // 4, 1)
    held = blocks
    bit = 1
    while bit < low:
        half = held.shape[0] // 2
        came = swap(held[half:], axis, bit)
        held = (held[:half].astype(WIDE) + came.astype(WIDE)).astype(LOW)
        bit *= 2
    came = [swap(held[n], axis, n * low) for n in range(1, held.shape[0])]
    return held[0], came


def wide_sum(terms):
    kept, came = terms
    result = kept.astype(WIDE)
    for value in came:
        result = result + value.astype(WIDE)
    return result


def total_hyper(value, axis):
    bit = 1
    while bit < lax.axis_size(axis):
        value = value + swap(value, axis, bit)
        bit *= 2
    return value


def block_at(value, index, size, dim):
    return lax.dynamic_slice_in_dim(value, index * size, size, dim)


def statistics(sums, row_total):
    average = sums[0] / row_total
    variance = sums[1] / row_total - average * average
    return average, lax.rsqrt(variance + NORM_EPS)


def backward_of_norm(grad_out, centred, inv_std, gain_row, sums, row_total):
    return gain_row * inv_std * (grad_out - (sums[0] + centred * sums[1]) / row_total)


def adamw_step(weight, moment_one, moment_two, gradient, learn_rate, weight_decay, step_count):
    moment_new = BETA_ONE * moment_one + (1.0 - BETA_ONE) * gradient
    second_new = BETA_TWO * moment_two + (1.0 - BETA_TWO) * gradient * gradient
    fix_one = 1.0 - jnp.power(BETA_ONE, step_count)
    fix_two = 1.0 - jnp.power(BETA_TWO, step_count)
    update = moment_new / fix_one / (jnp.sqrt(second_new / fix_two) + ADAM_EPS)
    return (weight - learn_rate * (update + weight_decay * weight), moment_new, second_new)


def local(
    images,
    crop_image,
    slot_rows,
    squeeze_weight,
    squeeze_moment,
    squeeze_second,
    spatial_weight,
    spatial_moment,
    spatial_second,
    expand_weight,
    expand_moment,
    expand_second,
    hidden_weight,
    hidden_moment,
    hidden_second,
    project_weight,
    project_moment,
    project_second,
    prototypes,
    proto_moment,
    proto_second,
    norm_params,
    norm_moment,
    norm_second,
    queue_rows,
    queue_valid,
    queue_fill,
    iteration,
):
    dp_count = lax.axis_size("dp")
    dp_at = lax.axis_index("dp")
    chan_count = lax.axis_size("chan")
    chan_at = lax.axis_index("chan")
    crops_dev, map_side, _, in_width = images.shape
    map_area = map_side * map_side
    pixel_rows = crops_dev * map_area
    pixel_total = pixel_rows * dp_count
    crop_total = crops_dev * dp_count
    mid_local = squeeze_weight.shape[1]
    hid_local = hidden_weight.shape[1]
    out_local = in_width // chan_count
    slot_local = squeeze_weight.shape[0]
    slot_total = slot_rows.shape[0]
    mid_width = mid_local * chan_count
    hid_width = hid_local * chan_count

    squeeze_came = spread(squeeze_weight.astype(LOW), "dp")
    tap_local = spatial_weight.shape[0]
    convs_all = lax.all_gather(
        jnp.concatenate([spatial_weight.astype(LOW), expand_weight.astype(LOW)], axis=0), "dp"
    )

    channels = jnp.arange(in_width, dtype=jnp.int32)
    used = (slot_rows < in_width).astype(jnp.int32).reshape(dp_count, slot_local)
    loads = jnp.sum(used, axis=1)
    owners = jnp.arange(dp_count, dtype=jnp.int32)
    firsts = jnp.sum(jnp.where(owners[None, :] < owners[:, None], loads[None, :], 0), axis=1)
    own_used = block_at(used, dp_at, 1, 0)[0]
    own_first = block_at(firsts, dp_at, 1, 0)
    own_at = jnp.arange(slot_local, dtype=jnp.int32)
    own_rank = jnp.sum(jnp.where(own_at[None, :] < own_at[:, None], own_used[None, :], 0), axis=1)
    cell = slot_local // dp_count
    share = in_width // dp_count
    target = (own_first + own_rank) % dp_count * cell + own_rank // dp_count
    deal_hot = ((target[None, :] == own_at[:, None]) & (own_used[None, :] > 0)).astype(LOW)
    head_low = jnp.concatenate([hidden_weight.astype(LOW), project_weight.astype(LOW)], axis=1)
    dealt = contract(deal_hot, head_low, 1, 0).astype(LOW)
    ranks = (
        jnp.arange(cell, dtype=jnp.int32)[None, :] * dp_count + (dp_at - firsts[:, None]) % dp_count
    )
    share_at = jnp.where(ranks < loads[:, None], (firsts[:, None] + ranks) // dp_count, -1)
    share_at = share_at.reshape(slot_local)
    place, rank = slot_of_channel(slot_rows, in_width)
    slot_blocks = slot_rows.reshape(dp_count, slot_local)
    slot_sent = jnp.concatenate(
        [lax.dynamic_index_in_dim(slot_blocks, dp_at ^ r, 0, False) for r in send_order(dp_count)]
    )
    own_slots = slot_sent[:slot_local]
    place_dealt = (rank % dp_count * share + rank // dp_count)[:in_width]

    proto_count = prototypes.shape[1]
    proto_low = jnp.pad(prototypes.astype(LOW).T, ((0, -proto_count % 256), (0, 0)))
    proto_width = proto_low.shape[0]
    queue_len = queue_rows.shape[0]
    slot_index = dp_at * queue_len + jnp.arange(queue_len, dtype=jnp.int32)
    queue_live = ((queue_valid > 0) & (slot_index < queue_fill[0])).astype(WIDE)
    queue_live = jnp.pad(queue_live, (0, -queue_len % ROWS))
    queue_similarity = contract(
        jnp.pad(queue_rows, ((0, -queue_len % ROWS), (0, 0))), proto_low, 1, 1
    )
    queue_codes = jnp.where(
        (jnp.arange(proto_width) < proto_count)[None, :],
        jnp.exp(queue_similarity / EPS_SINK) * queue_live[:, None],
        0.0,
    )
    queue_mass = jnp.sum(queue_codes, axis=0)
    queue_codes = queue_codes.astype(LOW)
    squeeze_came, queue_codes, queue_mass, slot_sent, proto_low = join(
        squeeze_came, queue_codes, queue_mass, slot_sent, proto_low
    )
    straight = jnp.zeros((1,), jnp.int32)
    turned = (chan_at * out_local).astype(jnp.int32).reshape(1)
    squeeze_rows = pick_rows(place, straight, [squeeze_came], in_width, 0, slot_local)

    norm_rows = norm_params[:, 0, :]
    first_norm = norm_rows[:, :mid_local]
    second_norm = norm_rows[:, mid_local : 2 * mid_local]
    third_norm = norm_rows[:, 2 * mid_local : 2 * mid_local + out_local]
    head_norm = norm_rows[:, 2 * mid_local + out_local :]

    def inner_layer(pre_act, norm, token=None):
        sums = jnp.stack([jnp.sum(pre_act, axis=0), jnp.sum(pre_act * pre_act, axis=0)])
        if token is not None:
            sums = after(sums, token)
        near = sums[0] / pixel_rows
        raw_all = jnp.concatenate(gather_relative((pre_act - near).astype(LOW), "chan"), axis=1)
        average, inv_std = statistics(total(sums, "dp"), pixel_total)
        scale = inv_std * norm[0]
        affine = jnp.stack([scale, norm[1] - (average - near) * scale])
        affine_all = jnp.concatenate(gather_relative(affine, "chan"), axis=1)
        act_all = jax.nn.silu(raw_all.astype(WIDE) * affine_all[0] + affine_all[1]).astype(LOW)
        return act_all, average, inv_std

    step_count = iteration[0].astype(WIDE)

    def step(weight, moment, second, gradient, rate, decay=DECAY_RATE):
        return adamw_step(weight, moment, second, gradient, rate, decay, step_count)

    pixels = images.transpose(1, 2, 0, 3).reshape(pixel_rows, in_width)
    pre_one = contract(pixels, squeeze_rows, 1, 0)
    inner_one, average_one, inv_one = inner_layer(pre_one, first_norm)
    dealt = lax.all_to_all(after(dealt, average_one).reshape(dp_count, cell, -1), "dp", 0, 0)
    def relative_blocks(value, size, dim):
        return [block_at(value, chan_at ^ r, size, dim) for r in range(chan_count)]

    spatial_rel = assemble(
        convs_all, chan_at.astype(jnp.int32).reshape(1), tap_local, 9, chan_count
    ).reshape(3, 3, mid_width, mid_local)
    maps_one = inner_one.reshape(map_side, map_side, crops_dev, mid_width)
    conv_dims = lax.ConvDimensionNumbers((2, 3, 0, 1), (3, 2, 0, 1), (2, 3, 0, 1))
    pre_two = lax.conv_general_dilated(
        maps_one,
        spatial_rel,
        (1, 1),
        ((1, 1), (1, 1)),
        dimension_numbers=conv_dims,
        preferred_element_type=WIDE,
    ).reshape(pixel_rows, mid_local)
    pre_two, dealt = join(pre_two, dealt)
    share_hot = (share_at[None, :] == channels[:share, None]).astype(LOW)
    head_all = lax.all_gather(
        contract(share_hot, dealt.reshape(slot_local, -1), 1, 0).astype(LOW),
        "dp",
        axis=0,
        tiled=True,
    )

    inner_two, average_two, inv_two = inner_layer(pre_two, second_norm)

    expand_rows = pick_rows(place, turned, [convs_all], in_width, tap_local, slot_local)

    def swap_blocks(blocks):
        return jnp.concatenate(
            [blocks[0]] + [swap(blocks[r], "chan", r) for r in range(1, chan_count)], axis=1
        )

    expand_rel = swap_blocks(
        [expand_rows[r * out_local : (r + 1) * out_local] for r in range(chan_count)]
    )
    squeeze_rel = swap_blocks(relative_blocks(squeeze_rows, out_local, 0))
    pre_three = contract(inner_two, expand_rel, 1, 1)
    sent_three = [
        jnp.sum(pre_three, axis=0),
        jnp.sum(pre_three * pre_three, axis=0),
        queue_mass,
        crop_image.astype(WIDE),
    ]
    came_three = spread(jnp.concatenate(sent_three), "dp")
    sums_three = jnp.sum(came_three[:, : 2 * out_local], axis=0).reshape(2, out_local)
    queue_first = came_three[:, 2 * out_local :]
    average_three, inv_three = statistics(sums_three, pixel_total)
    centred_three = (pre_three - average_three) * inv_three
    residual_in = block_at(pixels, chan_at, out_local, 1).astype(WIDE)
    summed = centred_three * third_norm[0] + third_norm[1] + residual_in
    block_rows = jax.nn.silu(summed)
    block_out = block_rows.astype(LOW).reshape(map_side, map_side, crops_dev, out_local)
    block_out = block_out.transpose(2, 0, 1, 3)
    pooled = jnp.mean(block_rows.reshape(map_area, crops_dev, out_local), axis=0).astype(LOW)
    pooled_dev = lax.all_gather(pooled, "chan", axis=1, tiled=True)
    pooled_all = lax.all_gather(pooled_dev, "dp", axis=0, tiled=True)

    dealt_hot = (place_dealt[:, None] == channels[None, :]).astype(LOW)
    pooled_dealt = contract(pooled_dev, dealt_hot, 1, 0).astype(LOW)
    pooled_dealt, head_all = join(pooled_dealt, head_all)
    hidden_dev = contract(pooled_dealt, head_all[:, :hid_local], 1, 0)
    own_place = block_at(place_dealt, chan_at, hid_local, 0)
    own_dealt_hot = (own_place[:, None] == channels[None, :]).astype(LOW)
    project_rows = contract(own_dealt_hot, head_all[:, hid_local:], 1, 0).astype(LOW)
    near_head = jnp.mean(hidden_dev, axis=0, keepdims=True).astype(LOW)
    hidden_sent = (hidden_dev - near_head.astype(WIDE)).astype(LOW)
    hidden_came = spread(jnp.concatenate([hidden_sent, near_head], axis=0), "dp")
    hidden_rows = contract(
        (after(place_dealt, hidden_dev)[:, None] == channels[None, :]).astype(LOW),
        head_all[:, :hid_local],
        1,
        0,
    ).astype(LOW)
    hidden_came, hidden_rows = join(hidden_came, hidden_rows)
    hidden_pre = (
        hidden_came[:, :crops_dev].astype(WIDE) + hidden_came[:, crops_dev:].astype(WIDE)
    ).reshape(
        crop_total, hid_local
    )
    head_sums = jnp.stack([jnp.sum(hidden_pre, axis=0), jnp.sum(hidden_pre * hidden_pre, axis=0)])
    average_head, inv_head = statistics(head_sums, crop_total)
    centred_head = (hidden_pre - average_head) * inv_head
    normed_head = centred_head * head_norm[0] + head_norm[1]
    hidden_act = jax.nn.silu(normed_head).astype(LOW)
    project_out = total_hyper(contract(hidden_act, project_rows, 1, 0), "chan")
    block_rows_of = min(crop_total, max(BLOCK, crops_dev))
    labels = queue_first[:, proto_width:].reshape(-1, block_rows_of)
    crop_index = jnp.arange(block_rows_of, dtype=jnp.int32)
    same_image = (
        (labels[:, :, None] == labels[:, None, :])
        & (crop_index[:, None] != crop_index[None, :])
        & (crop_index[:, None] // crops_dev == crop_index[None, :] // crops_dev)
    )
    pairs = same_image.astype(LOW)

    codes, queue_codes, sent = call_first(
        proto_count, project_out, proto_low, queue_codes, queue_first[:, :proto_width]
    )
    came = lax.all_to_all(sent, "dp", 0, 0)
    log_norm = call_norm(proto_count, project_out, proto_low)
    for turn_index in range(2, SINK_ITERS):
        came = lax.all_to_all(call_next(proto_count, came, codes, queue_codes), "dp", 0, 0)
    came, pooled_all = join(came, pooled_all)
    score_gradient, project_low_grad, loss_total = call_last(
        proto_count, came, codes, project_out, log_norm, proto_low, pairs
    )
    loss = loss_total[0, :1] / crop_total
    normed_low = low_of(project_out)
    hidden_grad_act = contract(project_low_grad, project_rows, 1, 1) * silu_slope(normed_head)
    head_grads = jnp.stack(
        [jnp.sum(hidden_grad_act, axis=0), jnp.sum(hidden_grad_act * centred_head, axis=0)]
    )
    head_pre_low = backward_of_norm(
        hidden_grad_act, centred_head, inv_head, head_norm[0], head_grads, crop_total
    ).astype(LOW)
    pooled_terms = contract(block_at(head_pre_low, dp_at, crops_dev, 0), hidden_rows, 1, 1)
    pooled_grad = scatter_relative(relative_blocks(pooled_terms, out_local, 1), "chan", WIDE)

    spread_grad = jnp.broadcast_to(
        pooled_grad[None] / map_area, (map_area, crops_dev, out_local)
    ).reshape(pixel_rows, out_local)
    sum_grad = spread_grad * silu_slope(summed)
    third_grads = total(
        jnp.stack([jnp.sum(sum_grad, axis=0), jnp.sum(sum_grad * centred_three, axis=0)]), "dp"
    )
    project_grad = jnp.concatenate(
        gather_relative(contract(hidden_act, project_low_grad, 0, 0).astype(LOW), "chan")
    )
    third_grads, project_grad = join(third_grads, project_grad)
    third_low = backward_of_norm(
        sum_grad, centred_three, inv_three, third_norm[0], third_grads, pixel_total
    ).astype(LOW)

    def column_parts(terms):
        return [terms[:, r * mid_local : (r + 1) * mid_local] for r in range(chan_count)]

    def inner_sums(summed_terms, pre_act, average, inv_std, norm):
        centred = (pre_act - average) * inv_std
        grad = summed_terms * silu_slope(centred * norm[0] + norm[1])
        sums = jnp.stack([jnp.sum(grad, axis=0), jnp.sum(grad * centred, axis=0)])
        return grad, centred, sums

    def slot_terms(grad_rows, turned):
        slot_hot = ((slot_sent ^ (turned * out_local))[:, None] == channels[None, :]).astype(LOW)
        terms = contract(slot_hot, grad_rows, 1, 0).astype(LOW)
        return terms.reshape(dp_count, slot_local, mid_local)

    second_sum = scatter_relative(column_parts(contract(third_low, expand_rel, 1, 0)), "chan")
    expand_terms = contract(third_low, inner_two, 0, 0).astype(LOW)
    turned_hot = ((own_slots ^ (chan_at * hid_local))[:, None] == channels[None, :]).astype(LOW)
    slot_project = contract(turned_hot, project_grad, 1, 0)
    project_new = step(
        project_weight, project_moment, project_second, slot_project, hid_width ** (-0.5)
    )
    second_sum, expand_terms, *project_new = join(second_sum, expand_terms, *project_new)
    grad_two, centred_two, second_sums = inner_sums(
        second_sum, pre_two, average_two, inv_two, second_norm
    )
    expand_parts = column_parts(expand_terms)
    expand_grad = jnp.concatenate(
        [expand_parts[0]] + [swap(expand_parts[r], "chan", r) for r in range(1, chan_count)], axis=0
    )
    slot_expand = slot_terms(expand_grad, chan_at)
    own_hot = (own_slots[:, None] == channels[None, :]).astype(LOW)
    slot_hidden = contract(contract(pooled_all, own_hot, 1, 1).astype(LOW), head_pre_low, 0, 0)
    hidden_new = step(hidden_weight, hidden_moment, hidden_second, slot_hidden, in_width ** (-0.5))
    second_grads, slot_expand, *hidden_new = join(
        total(second_sums, "dp"), slot_expand, *hidden_new
    )
    expand_came = scatter_staged(slot_expand, "dp")
    second_low = backward_of_norm(
        grad_two, centred_two, inv_two, second_norm[0], second_grads, pixel_total
    ).astype(LOW)
    maps_two = second_low.reshape(map_side, map_side, crops_dev, mid_local)
    first_terms = lax.conv_general_dilated(
        maps_two,
        spatial_rel[::-1, ::-1].transpose(0, 1, 3, 2),
        (1, 1),
        ((1, 1), (1, 1)),
        dimension_numbers=conv_dims,
        preferred_element_type=WIDE,
    ).reshape(pixel_rows, mid_width)
    first_sum = scatter_relative(column_parts(first_terms), "chan")
    spatial_terms = lax.conv_general_dilated(
        maps_one,
        maps_two,
        (1, 1),
        ((1, 1), (1, 1)),
        dimension_numbers=lax.ConvDimensionNumbers((3, 2, 0, 1), (3, 2, 0, 1), (2, 3, 0, 1)),
        preferred_element_type=WIDE,
    ).reshape(9, mid_width, mid_local)
    spatial_sent = deal_rows(
        spatial_terms.astype(LOW).reshape(9 * mid_width, mid_local),
        jnp.stack([dp_at, chan_at]).astype(jnp.int32),
        dp_count,
        9,
        chan_count,
    )
    first_sum, spatial_sent = join(first_sum, spatial_sent)
    spatial_came = scatter_staged(spatial_sent, "dp")
    grad_one, centred_one, first_sums = inner_sums(
        first_sum, pre_one, average_one, inv_one, first_norm
    )
    first_grads = total_hyper(first_sums, "dp")
    first_low = backward_of_norm(
        grad_one, centred_one, inv_one, first_norm[0], first_grads, pixel_total
    ).astype(LOW)
    squeeze_grad = contract(pixels, first_low, 0, 0).astype(LOW)
    squeeze_terms = slot_terms(squeeze_grad, 0)
    squeeze_came = scatter_staged(squeeze_terms, "dp")
    first_all = jnp.concatenate(gather_relative(after(first_low, squeeze_terms), "chan"), axis=1)
    proto_grad = contract(after(score_gradient, squeeze_terms), normed_low, 0, 0)[:proto_count].T
    proto_new = step(prototypes, proto_moment, proto_second, proto_grad, 0.1)
    first_all, *proto_new = join(first_all, *proto_new)
    images_grad = contract(first_all, squeeze_rel, 1, 1) + sum_grad
    images_grad = images_grad.reshape(map_side, map_side, crops_dev, out_local).transpose(2, 0, 1, 3)
    spatial_came, expand_came, _ = join(spatial_came, expand_came, squeeze_terms)
    images_grad, squeeze_came = join(images_grad, squeeze_came)
    slot_squeeze, slot_spatial, slot_expand = [
        wide_sum(came) for came in (squeeze_came, spatial_came, expand_came)
    ]
    norm_gradient = jnp.concatenate([first_grads, second_grads, third_grads, head_grads], axis=1)
    norm_gradient = norm_gradient[::-1].reshape(norm_params.shape)
    return (
        block_out,
        loss,
        images_grad,
        *step(squeeze_weight, squeeze_moment, squeeze_second, slot_squeeze, in_width ** (-0.5)),
        *step(
            spatial_weight, spatial_moment, spatial_second, slot_spatial, (9 * mid_width) ** (-0.5)
        ),
        *step(expand_weight, expand_moment, expand_second, slot_expand, mid_width ** (-0.5)),
        *hidden_new,
        *project_new,
        *proto_new,
        *step(norm_params, norm_moment, norm_second, norm_gradient, 0.5, 0.0),
    )


def solution(mesh):
    rows, both, whole = P("dp", None), P("dp", "chan"), P()
    maps = P("dp", None, None, "chan")
    norm = P(None, "chan", None)
    placed = (
        (P("dp", None, None, None), P("dp"), whole)
        + (both,) * 12
        + (rows,) * 3
        + (whole,) * 3
        + (norm,) * 3
        + (rows, P("dp"), whole, whole)
    )
    return jax.shard_map(
        local,
        mesh=mesh,
        in_specs=placed,
        out_specs=(maps, whole, maps) + (both,) * 12 + (rows,) * 3 + (whole,) * 3 + (norm,) * 3,
        check_vma=False,
    )
```

```python
import math

import jax
import jax.numpy as jnp
from jax import lax
from jax.experimental import pallas as pl
from jax.experimental.pallas import tpu as pltpu
from jax.sharding import PartitionSpec as P

SINK_ITERS = 3
PRECISE = lax.Precision.HIGHEST
EPS_SINK = 0.05
SOFTMAX_WARMTH = 0.1
LOSS_MULTIPLIER = 256.0
NORM_EPS = 1e-05
BETA_ONE = 0.5
BETA_TWO = 0.5
ADAM_EPS = 1e-08
DECAY_RATE = 1e-06
LOW = jnp.bfloat16
WIDE = jnp.float32


def contract(left, right, left_dim, right_dim):
    return lax.dot_general(
        left, right, (((left_dim,), (right_dim,)), ((), ())), preferred_element_type=WIDE
    )


def silu_slope(value):
    sigma = jax.nn.sigmoid(value)
    return sigma * (1.0 + value * (1.0 - sigma))


def spread(value, axis):
    count = lax.axis_size(axis)
    return lax.all_to_all(jnp.broadcast_to(value[None], (count,) + value.shape), axis, 0, 0)


def total(value, axis):
    return jnp.sum(spread(value, axis).astype(WIDE), axis=0)


def swap(value, axis, bit):
    return lax.ppermute(value, axis, [(at, at ^ bit) for at in range(lax.axis_size(axis))])


def gather_relative(value, axis):
    held = {0: value}
    bit = lax.axis_size(axis) // 2
    while bit:
        keys = sorted(held)
        came = swap(jnp.stack([held[k] for k in keys]), axis, bit)
        held.update({k ^ bit: came[n] for n, k in enumerate(keys)})
        bit //= 2
    return [held[k] for k in range(lax.axis_size(axis))]


def invert_kernel(slots_ref, place_ref, rank_ref):
    count = slots_ref.shape[0]
    channels = place_ref.shape[0] - 128

    def step(at, rank):
        for n in range(16):
            slot = at * 16 + n
            channel = slots_ref[slot]
            place_ref[channel] = slot
            rank_ref[channel] = rank
            rank = rank + jnp.where(channel < channels, 1, 0)
        return rank

    lax.fori_loop(0, count // 16, step, jnp.int32(0))


def slot_of_channel(slot_rows, channels):
    smem = pl.BlockSpec(memory_space=pltpu.SMEM)
    return pl.pallas_call(
        invert_kernel,
        out_shape=[jax.ShapeDtypeStruct((channels + 128,), jnp.int32)] * 2,
        in_specs=[smem],
        out_specs=[smem] * 2,
        name="slot_of_channel",
    )(slot_rows)


def pick_kernel(first, count, place_ref, turn_ref, *refs):
    *blocks, out_ref, wide, picked = refs
    at = 0
    for block in blocks:
        for part in [block.at[k] for k in range(block.shape[0])] if len(block.shape) == 3 else [block]:
            wide[at : at + count, :] = part[first : first + count, :].astype(WIDE)
            at += count

    def step(group, carry):
        for n in range(8):
            row = group * 8 + n
            picked[pl.ds(row, 1), :] = wide[pl.ds(place_ref[(group * 8 ^ turn_ref[0]) + n], 1), :]
        return carry

    lax.fori_loop(0, out_ref.shape[0] // 8, step, 0)
    out_ref[...] = picked[...].astype(out_ref.dtype)


def pick_rows(place, turn, blocks, rows, first, count):
    width = blocks[0].shape[-1]
    held = sum(block.size // (width * block.shape[-2]) for block in blocks) * count
    vmem = pl.BlockSpec()
    return pl.pallas_call(
        lambda *refs: pick_kernel(first, count, *refs),
        out_shape=jax.ShapeDtypeStruct((rows, width), LOW),
        in_specs=[pl.BlockSpec(memory_space=pltpu.SMEM)] * 2 + [vmem] * len(blocks),
        out_specs=vmem,
        scratch_shapes=[pltpu.VMEM((held, width), WIDE), pltpu.VMEM((rows, width), WIDE)],
        compiler_params=pltpu.CompilerParams(vmem_limit_bytes=12 << 20),
        cost_estimate=pl.CostEstimate(
            flops=0, bytes_accessed=2 * (held + rows) * width, transcendentals=0
        ),
        name="pick_rows",
    )(place, turn, *blocks)


def assemble_kernel(taps, chan_count, rows, at_ref, held_ref, out_ref):
    per_tap = out_ref.shape[0] // taps
    per_chan = per_tap // chan_count
    size = math.gcd(rows, per_chan)
    for row in range(0, out_ref.shape[0], size):
        tap, inner = divmod(row, per_tap)
        chan, rest = divmod(inner, per_chan)
        target = pl.multiple_of((chan ^ at_ref[0]) * per_chan + tap * per_tap + rest, size)
        owner, source = divmod(row, rows)
        out_ref[pl.ds(target, size), :] = held_ref[owner, source : source + size, :]


def assemble(held, at, rows, taps, chan_count):
    vmem = pl.BlockSpec()
    return pl.pallas_call(
        lambda *refs: assemble_kernel(taps, chan_count, rows, *refs),
        out_shape=jax.ShapeDtypeStruct((rows * held.shape[0], held.shape[2]), LOW),
        in_specs=[pl.BlockSpec(memory_space=pltpu.SMEM), vmem],
        out_specs=vmem,
        compiler_params=pltpu.CompilerParams(vmem_limit_bytes=12 << 20),
        cost_estimate=pl.CostEstimate(
            flops=0, bytes_accessed=4 * rows * held.shape[0] * held.shape[2], transcendentals=0
        ),
        name="assemble",
    )(at, held)


def deal_kernel(taps, chan_count, order, at_ref, terms_ref, out_ref):
    rows = out_ref.shape[1]
    per_tap = terms_ref.shape[0] // taps
    per_chan = per_tap // chan_count
    size = math.gcd(rows, per_chan)
    for n, r in enumerate(order):
        for start in range(0, rows, size):
            row = (at_ref[0] ^ r) * rows + start
            tap, inner = row // per_tap, row % per_tap
            chan, rest = inner // per_chan, inner % per_chan
            source = tap * per_tap + (chan ^ at_ref[1]) * per_chan + rest
            source = pl.multiple_of(source, size)
            out_ref[n, start : start + size, :] = terms_ref[pl.ds(source, size), :]


def deal_rows(terms, at, owners, taps, chan_count):
    order = send_order(owners)
    vmem = pl.BlockSpec()
    return pl.pallas_call(
        lambda *refs: deal_kernel(taps, chan_count, order, *refs),
        out_shape=jax.ShapeDtypeStruct((owners, terms.shape[0] // owners, terms.shape[1]), LOW),
        in_specs=[pl.BlockSpec(memory_space=pltpu.SMEM), vmem],
        out_specs=vmem,
        compiler_params=pltpu.CompilerParams(vmem_limit_bytes=12 << 20),
        cost_estimate=pl.CostEstimate(flops=0, bytes_accessed=4 * terms.size, transcendentals=0),
        name="deal_rows",
    )(at, terms)


ROWS = 32
BLOCK = 128


def whole(count):
    return [pl.BlockSpec()] * count


def over_rows(total_rows, body, size=ROWS):
    def step(at, carry):
        body(pl.ds(pl.multiple_of(at * size, size), size))
        return carry

    lax.fori_loop(0, total_rows // size, step, 0)


def sum_rows(total_rows, width, body, size):
    def step(at, held):
        value = body(pl.ds(pl.multiple_of(at * size, size), size))
        for first in range(0, size, 8):
            held = held + value[first : first + 8]
        return held

    held = lax.fori_loop(0, total_rows // size, step, jnp.zeros((8, width), WIDE))
    return jnp.sum(held, axis=0, keepdims=True)


def inverse_of(row_sums):
    return 1.0 / jnp.where(row_sums > 0.0, row_sums, 1.0)


def known_columns(width, known):
    return lax.broadcasted_iota(jnp.int32, (1, width), 1) < known


def fill(target, value):
    for at in range(target.shape[0]):
        target[at] = value


def low_of(z):
    return (z * lax.rsqrt(jnp.sum(z * z, axis=1, keepdims=True) + 1e-06)).astype(LOW)


def weigh_columns(matrix, factors):
    factors = jnp.broadcast_to(factors.astype(LOW), (128, factors.shape[1]))
    return contract(matrix.astype(LOW), factors, 1, 1)


def in_all_tiles(value, width):
    return jnp.concatenate([value] * (width // 128), axis=1)


def first_turn(
    known, z_ref, first_ref, proto_any, queue_any, b_ref, bq_any, sent_any, proto, bq, sent, inv, row_inv, sems
):
    proto_in = pltpu.make_async_copy(proto_any, proto, sems.at[0])
    queue_in = pltpu.make_async_copy(queue_any, bq, sems.at[1])
    queue_out = pltpu.make_async_copy(bq, bq_any, sems.at[2])
    sent_out = pltpu.make_async_copy(sent, sent_any, sems.at[3])
    proto_in.start()
    queue_in.start()
    low = low_of(z_ref[...])
    proto_in.wait()
    b_ref[...] = contract(low, proto[...], 1, 1)
    lines, width = bq.shape
    total_rows = b_ref.shape[0]
    mask = known_columns(width, known)

    def exponentials(rows):
        value = jnp.where(mask, jnp.exp(b_ref[rows, :] * (1.0 / EPS_SINK)), 0.0)
        b_ref[rows, :] = value
        return value

    totals = sum_rows(total_rows, width, exponentials, 8)
    totals = totals + jnp.sum(first_ref[...], axis=0, keepdims=True)
    factors = jnp.where(mask, 1.0 / jnp.where(mask, totals * 0.125, 1.0), 0.0)
    inv[...] = jnp.broadcast_to(factors, inv.shape)
    queue_in.wait()
    row_inv[pl.ds(0, lines), :] = inverse_of(weigh_columns(bq[...], factors))

    def queue(rows):
        factor = jnp.concatenate([inv[...]] * 2, axis=0)
        value = bq[rows, :].astype(WIDE) * factor * in_all_tiles(row_inv[rows, :], width)
        bq[rows, :] = value.astype(LOW)
        return value

    queue_sums = sum_rows(lines, width, queue, 16)
    queue_out.start()
    row_inv[pl.ds(0, total_rows), :] = inverse_of(weigh_columns(b_ref[...], factors))

    def batch(rows):
        value = b_ref[rows, :] * inv[...] * in_all_tiles(row_inv[rows, :], width)
        b_ref[rows, :] = value
        return value

    batch_sums = sum_rows(total_rows, width, batch, 8)
    fill(sent, queue_sums + batch_sums * (1.0 / sent.shape[0]))
    sent_out.start()
    queue_out.wait()
    sent_out.wait()


def column_factor(known, came_ref):
    totals = jnp.sum(came_ref[...], axis=0)
    mask = known_columns(totals.shape[1], known)
    return jnp.where(mask, 1.0 / jnp.where(mask, totals, 1.0), 0.0)


def next_turn(known, came_ref, b_ref, bq_any, sent_any, bq, sent, row_inv, sems):
    queue_in = pltpu.make_async_copy(bq_any, bq, sems.at[0])
    sent_out = pltpu.make_async_copy(sent, sent_any, sems.at[1])
    queue_in.start()
    factors = column_factor(known, came_ref)

    def weigh(source, size):
        total_rows, width = source.shape
        row_inv[pl.ds(0, total_rows), :] = inverse_of(weigh_columns(source[...], factors))

        def body(rows):
            return source[rows, :].astype(WIDE) * in_all_tiles(row_inv[rows, :], width)

        return sum_rows(total_rows, width, body, size)

    batch_sums = weigh(b_ref, 8)
    queue_in.wait()
    fill(sent, weigh(bq, 16) + batch_sums * (1.0 / sent.shape[0]))
    sent_out.start()
    sent_out.wait()


def norm_of_scores(known, z_ref, proto_any, norm_ref, proto, scores, sems):
    proto_in = pltpu.make_async_copy(proto_any, proto, sems.at[0])
    proto_in.start()
    low = low_of(z_ref[...])
    proto_in.wait()
    scores[...] = contract(low, proto[...], 1, 1)
    mask = known_columns(scores.shape[1], known)

    def body(rows):
        raw = scores[rows, :] * (1.0 / SOFTMAX_WARMTH)
        top = jnp.max(jnp.where(mask, raw, -jnp.inf), axis=1, keepdims=True)
        mass = jnp.sum(jnp.where(mask, jnp.exp(raw - top), 0.0), axis=1, keepdims=True)
        norm_ref[rows, :] = top + jnp.log(mass)

    over_rows(scores.shape[0], body)


def last_turn(
    known,
    came_ref,
    b_ref,
    z_ref,
    norm_ref,
    proto_any,
    pairs_any,
    grad_any,
    low_grad_ref,
    loss_ref,
    proto,
    pairs,
    grad,
    scores,
    high,
    rest,
    held,
    inv,
    sems,
):
    proto_in = pltpu.make_async_copy(proto_any, proto, sems.at[0])
    pairs_in = pltpu.make_async_copy(pairs_any, pairs, sems.at[1])
    grad_out = pltpu.make_async_copy(grad, grad_any, sems.at[2])
    proto_in.start()
    pairs_in.start()
    factors = column_factor(known, came_ref)
    inv[...] = factors
    mask = known_columns(factors.shape[1], known)
    size = pairs.shape[1]
    loss_ref[...] = jnp.zeros(loss_ref.shape, WIDE)
    proto_in.wait()
    pairs_in.wait()

    def block(at, carry):
        def here(rows):
            return pl.ds(pl.multiple_of(at * size + rows, 8), ROWS)

        place = pl.ds(pl.multiple_of(at * size, size), size)
        z = z_ref[place, :]
        inv_len = lax.rsqrt(jnp.sum(z * z, axis=1, keepdims=True) + 1e-06)
        scores[...] = contract((z * inv_len).astype(LOW), proto[...], 1, 1)
        for first in range(0, size, ROWS):
            value = b_ref[here(first), :] * inv[...]
            value = value * (1.0 / jnp.sum(value, axis=1, keepdims=True))
            top = value.astype(LOW)
            high[first : first + ROWS, :] = top
            rest[first : first + ROWS, :] = (value - top.astype(WIDE)).astype(LOW)
        pair = pairs[at]
        others = jnp.sum(pair.astype(WIDE), axis=1, keepdims=True)
        inv_others = 1.0 / jnp.maximum(others, 1.0)
        held[...] = contract(pair, high[...], 1, 0) + contract(pair, rest[...], 1, 0)
        for first in range(0, size, ROWS):
            rows = slice(first, first + ROWS)
            targets = held[rows, :] * inv_others[rows]
            logs = scores[rows, :] * (1.0 / SOFTMAX_WARMTH) - norm_ref[here(first), :]
            loss_ref[...] -= jnp.sum(jnp.where(mask, targets * logs, 0.0))
            weight = jnp.sum(targets, axis=1, keepdims=True)
            value = (LOSS_MULTIPLIER / SOFTMAX_WARMTH) * (jnp.exp(logs) * weight - targets)
            grad[here(first), :] = jnp.where(mask, value, 0.0).astype(LOW)
        normed_grad = contract(grad[place, :], proto[...], 1, 0)
        normed = z * inv_len
        along = jnp.sum(normed * normed_grad, axis=1, keepdims=True)
        low_grad_ref[place, :] = (inv_len * (normed_grad - normed * along)).astype(LOW)
        return carry

    lax.fori_loop(0, pairs.shape[0], block, 0)
    grad_out.start()
    grad_out.wait()


def shape(dims, kind=WIDE):
    return jax.ShapeDtypeStruct(dims, kind)


def turn_call(kernel, known, outs, anywhere_out, close, anywhere, scratch, copies, aliases={}):
    near, far = pl.BlockSpec(memory_space=pltpu.VMEM), pl.BlockSpec(memory_space=pltpu.HBM)
    held = sum(value.size * value.dtype.itemsize for value in (*scratch, *close, *outs))
    return pl.pallas_call(
        lambda *refs: kernel(known, *refs),
        out_shape=outs,
        in_specs=[near] * len(close) + [far] * len(anywhere),
        out_specs=[far if at in anywhere_out else near for at in range(len(outs))],
        scratch_shapes=[pltpu.VMEM(value.shape, value.dtype) for value in scratch]
        + [pltpu.SemaphoreType.DMA((copies,))],
        compiler_params=pltpu.CompilerParams(vmem_limit_bytes=min(held + (8 << 20), 60 << 20)),
        input_output_aliases=aliases,
        name=kernel.__name__,
    )(*close, *[pltpu.with_memory_space_constraint(value, pltpu.HBM) for value in anywhere])


def call_first(known, z, proto, queue, first):
    rows, width, lines, owners = z.shape[0], proto.shape[0], queue.shape[0], first.shape[0]
    sent = shape((owners, 1, width))
    return turn_call(
        first_turn,
        known,
        [shape((rows, width)), shape(queue.shape, LOW), sent],
        (1, 2),
        (z, first),
        (proto, queue),
        [
            shape(proto.shape, LOW),
            shape(queue.shape, LOW),
            sent,
            shape((8, width)),
            shape((max(rows, lines), 128)),
        ],
        4,
        {3: 1},
    )


def call_next(known, came, b, bq):
    return turn_call(
        next_turn,
        known,
        [shape(came.shape)],
        (0,),
        (came, b),
        (bq,),
        [shape(bq.shape, LOW), shape(came.shape), shape((max(b.shape[0], bq.shape[0]), 128))],
        2,
    )[0]


def call_norm(known, z, proto):
    rows, width = z.shape[0], proto.shape[0]
    return turn_call(
        norm_of_scores,
        known,
        [shape((rows, 1))],
        (),
        (z,),
        (proto,),
        [shape(proto.shape, LOW), shape((rows, width))],
        1,
    )[0]


def call_last(known, came, b, z, norm, proto, pairs):
    width, size = b.shape[1], pairs.shape[1]
    part = (size, width)
    return turn_call(
        last_turn,
        known,
        [shape(b.shape, LOW), shape(z.shape, LOW), shape((8, 128))],
        (0,),
        (came, b, z, norm),
        (proto, pairs),
        [
            shape(proto.shape, LOW),
            shape(pairs.shape, LOW),
            shape(b.shape, LOW),
            shape(part),
            shape(part, LOW),
            shape(part, LOW),
            shape(part),
            shape((1, width)),
        ],
        3,
    )


def after(value, token):
    return lax.optimization_barrier((value, token))[0]


def join(*values):
    return lax.optimization_barrier(values)


def scatter_relative(parts, axis, sent=LOW):
    held = dict(enumerate(parts))
    bit = 1
    while bit < lax.axis_size(axis):
        keys = [k for k in sorted(held) if not k & bit]
        came = swap(jnp.stack([held[k | bit].astype(sent) for k in keys]), axis, bit)
        held = {k: held[k] + came[n].astype(WIDE) for n, k in enumerate(keys)}
        bit *= 2
    return held[0]


def send_order(count):
    low = max(count // 4, 1)
    order = list(range(0, count, low))
    bit = low // 2
    while bit:
        order = order + [r | bit for r in order]
        bit //= 2
    return order


def scatter_staged(blocks, axis):
    count = lax.axis_size(axis)
    low = max(count // 4, 1)
    held = blocks
    bit = 1
    while bit < low:
        half = held.shape[0] // 2
        came = swap(held[half:], axis, bit)
        held = (held[:half].astype(WIDE) + came.astype(WIDE)).astype(LOW)
        bit *= 2
    came = [swap(held[n], axis, n * low) for n in range(1, held.shape[0])]
    return held[0], came


def wide_sum(terms):
    kept, came = terms
    result = kept.astype(WIDE)
    for value in came:
        result = result + value.astype(WIDE)
    return result


def total_hyper(value, axis):
    bit = 1
    while bit < lax.axis_size(axis):
        value = value + swap(value, axis, bit)
        bit *= 2
    return value


def block_at(value, index, size, dim):
    return lax.dynamic_slice_in_dim(value, index * size, size, dim)


def statistics(sums, row_total):
    average = sums[0] / row_total
    variance = sums[1] / row_total - average * average
    return average, lax.rsqrt(variance + NORM_EPS)


def backward_of_norm(grad_out, centred, inv_std, gain_row, sums, row_total):
    return gain_row * inv_std * (grad_out - (sums[0] + centred * sums[1]) / row_total)


def adamw_step(weight, moment_one, moment_two, gradient, learn_rate, weight_decay, step_count):
    moment_new = BETA_ONE * moment_one + (1.0 - BETA_ONE) * gradient
    second_new = BETA_TWO * moment_two + (1.0 - BETA_TWO) * gradient * gradient
    fix_one = 1.0 - jnp.power(BETA_ONE, step_count)
    fix_two = 1.0 - jnp.power(BETA_TWO, step_count)
    update = moment_new / fix_one / (jnp.sqrt(second_new / fix_two) + ADAM_EPS)
    return (weight - learn_rate * (update + weight_decay * weight), moment_new, second_new)


def local(
    images,
    crop_image,
    slot_rows,
    squeeze_weight,
    squeeze_moment,
    squeeze_second,
    spatial_weight,
    spatial_moment,
    spatial_second,
    expand_weight,
    expand_moment,
    expand_second,
    hidden_weight,
    hidden_moment,
    hidden_second,
    project_weight,
    project_moment,
    project_second,
    prototypes,
    proto_moment,
    proto_second,
    norm_params,
    norm_moment,
    norm_second,
    queue_rows,
    queue_valid,
    queue_fill,
    iteration,
):
    dp_count = lax.axis_size("dp")
    dp_at = lax.axis_index("dp")
    chan_count = lax.axis_size("chan")
    chan_at = lax.axis_index("chan")
    crops_dev, map_side, _, in_width = images.shape
    map_area = map_side * map_side
    pixel_rows = crops_dev * map_area
    pixel_total = pixel_rows * dp_count
    crop_total = crops_dev * dp_count
    mid_local = squeeze_weight.shape[1]
    hid_local = hidden_weight.shape[1]
    out_local = in_width // chan_count
    slot_local = squeeze_weight.shape[0]
    slot_total = slot_rows.shape[0]
    mid_width = mid_local * chan_count
    hid_width = hid_local * chan_count

    squeeze_came = spread(squeeze_weight.astype(LOW), "dp")
    tap_local = spatial_weight.shape[0]
    convs_all = lax.all_gather(
        jnp.concatenate([spatial_weight.astype(LOW), expand_weight.astype(LOW)], axis=0), "dp"
    )

    channels = jnp.arange(in_width, dtype=jnp.int32)
    used = (slot_rows < in_width).astype(jnp.int32).reshape(dp_count, slot_local)
    loads = jnp.sum(used, axis=1)
    owners = jnp.arange(dp_count, dtype=jnp.int32)
    firsts = jnp.sum(jnp.where(owners[None, :] < owners[:, None], loads[None, :], 0), axis=1)
    own_used = block_at(used, dp_at, 1, 0)[0]
    own_first = block_at(firsts, dp_at, 1, 0)
    own_at = jnp.arange(slot_local, dtype=jnp.int32)
    own_rank = jnp.sum(jnp.where(own_at[None, :] < own_at[:, None], own_used[None, :], 0), axis=1)
    cell = slot_local // dp_count
    share = in_width // dp_count
    target = (own_first + own_rank) % dp_count * cell + own_rank // dp_count
    deal_hot = ((target[None, :] == own_at[:, None]) & (own_used[None, :] > 0)).astype(LOW)
    head_low = jnp.concatenate([hidden_weight.astype(LOW), project_weight.astype(LOW)], axis=1)
    dealt = contract(deal_hot, head_low, 1, 0).astype(LOW)
    ranks = (
        jnp.arange(cell, dtype=jnp.int32)[None, :] * dp_count + (dp_at - firsts[:, None]) % dp_count
    )
    share_at = jnp.where(ranks < loads[:, None], (firsts[:, None] + ranks) // dp_count, -1)
    share_at = share_at.reshape(slot_local)
    place, rank = slot_of_channel(slot_rows, in_width)
    slot_blocks = slot_rows.reshape(dp_count, slot_local)
    slot_sent = jnp.concatenate(
        [lax.dynamic_index_in_dim(slot_blocks, dp_at ^ r, 0, False) for r in send_order(dp_count)]
    )
    own_slots = slot_sent[:slot_local]
    place_dealt = (rank % dp_count * share + rank // dp_count)[:in_width]

    proto_count = prototypes.shape[1]
    proto_low = jnp.pad(prototypes.astype(LOW).T, ((0, -proto_count % 256), (0, 0)))
    proto_width = proto_low.shape[0]
    queue_len = queue_rows.shape[0]
    slot_index = dp_at * queue_len + jnp.arange(queue_len, dtype=jnp.int32)
    queue_live = ((queue_valid > 0) & (slot_index < queue_fill[0])).astype(WIDE)
    queue_live = jnp.pad(queue_live, (0, -queue_len % ROWS))
    queue_similarity = contract(
        jnp.pad(queue_rows, ((0, -queue_len % ROWS), (0, 0))), proto_low, 1, 1
    )
    queue_codes = jnp.where(
        (jnp.arange(proto_width) < proto_count)[None, :],
        jnp.exp(queue_similarity / EPS_SINK) * queue_live[:, None],
        0.0,
    )
    queue_mass = jnp.sum(queue_codes, axis=0)
    queue_codes = queue_codes.astype(LOW)
    squeeze_came, queue_codes, queue_mass, slot_sent, proto_low = join(
        squeeze_came, queue_codes, queue_mass, slot_sent, proto_low
    )
    straight = jnp.zeros((1,), jnp.int32)
    turned = (chan_at * out_local).astype(jnp.int32).reshape(1)
    squeeze_rows = pick_rows(place, straight, [squeeze_came], in_width, 0, slot_local)

    norm_rows = norm_params[:, 0, :]
    first_norm = norm_rows[:, :mid_local]
    second_norm = norm_rows[:, mid_local : 2 * mid_local]
    third_norm = norm_rows[:, 2 * mid_local : 2 * mid_local + out_local]
    head_norm = norm_rows[:, 2 * mid_local + out_local :]

    def inner_layer(pre_act, norm, token=None):
        sums = jnp.stack([jnp.sum(pre_act, axis=0), jnp.sum(pre_act * pre_act, axis=0)])
        near = sums[0] / pixel_rows
        if token is not None:
            sums = after(sums, token)
        raw_all = jnp.concatenate(gather_relative((pre_act - near).astype(LOW), "chan"), axis=1)
        average, inv_std = statistics(total(sums, "dp"), pixel_total)
        scale = inv_std * norm[0]
        affine = jnp.stack([scale, norm[1] - (average - near) * scale])
        affine_all = jnp.concatenate(gather_relative(affine, "chan"), axis=1)
        act_all = jax.nn.silu(raw_all.astype(WIDE) * affine_all[0] + affine_all[1]).astype(LOW)
        return act_all, average, inv_std

    step_count = iteration[0].astype(WIDE)

    def step(weight, moment, second, gradient, rate, decay=DECAY_RATE):
        return adamw_step(weight, moment, second, gradient, rate, decay, step_count)

    pixels = images.transpose(1, 2, 0, 3).reshape(pixel_rows, in_width)
    pre_one = contract(pixels, squeeze_rows, 1, 0)
    inner_one, average_one, inv_one = inner_layer(pre_one, first_norm)
    dealt = lax.all_to_all(after(dealt, average_one).reshape(dp_count, cell, -1), "dp", 0, 0)
    def relative_blocks(value, size, dim):
        return [block_at(value, chan_at ^ r, size, dim) for r in range(chan_count)]

    spatial_rel = assemble(
        convs_all, chan_at.astype(jnp.int32).reshape(1), tap_local, 9, chan_count
    ).reshape(3, 3, mid_width, mid_local)
    maps_one = inner_one.reshape(map_side, map_side, crops_dev, mid_width)
    conv_dims = lax.ConvDimensionNumbers((2, 3, 0, 1), (3, 2, 0, 1), (2, 3, 0, 1))
    pre_two = lax.conv_general_dilated(
        maps_one,
        spatial_rel,
        (1, 1),
        ((1, 1), (1, 1)),
        dimension_numbers=conv_dims,
        preferred_element_type=WIDE,
    ).reshape(pixel_rows, mid_local)
    pre_two, dealt = join(pre_two, dealt)
    share_hot = (share_at[None, :] == channels[:share, None]).astype(LOW)
    shared = contract(share_hot, dealt.reshape(slot_local, -1), 1, 0).astype(LOW)
    head_all = lax.all_gather(shared, "dp", axis=0, tiled=True)

    inner_two, average_two, inv_two = inner_layer(pre_two, second_norm, shared)

    expand_rows = pick_rows(place, turned, [convs_all], in_width, tap_local, slot_local)

    def swap_blocks(blocks):
        return jnp.concatenate(
            [blocks[0]] + [swap(blocks[r], "chan", r) for r in range(1, chan_count)], axis=1
        )

    expand_rel = swap_blocks(
        [expand_rows[r * out_local : (r + 1) * out_local] for r in range(chan_count)]
    )
    squeeze_rel = swap_blocks(relative_blocks(squeeze_rows, out_local, 0))
    pre_three = contract(inner_two, expand_rel, 1, 1)
    sent_three = [
        jnp.sum(pre_three, axis=0),
        jnp.sum(pre_three * pre_three, axis=0),
        queue_mass,
        crop_image.astype(WIDE),
    ]
    came_three = spread(jnp.concatenate(sent_three), "dp")
    sums_three = jnp.sum(came_three[:, : 2 * out_local], axis=0).reshape(2, out_local)
    queue_first = came_three[:, 2 * out_local :]
    average_three, inv_three = statistics(sums_three, pixel_total)
    centred_three = (pre_three - average_three) * inv_three
    residual_in = block_at(pixels, chan_at, out_local, 1).astype(WIDE)
    summed = centred_three * third_norm[0] + third_norm[1] + residual_in
    block_rows = jax.nn.silu(summed)
    block_out = block_rows.astype(LOW).reshape(map_side, map_side, crops_dev, out_local)
    block_out = block_out.transpose(2, 0, 1, 3)
    pooled = jnp.mean(block_rows.reshape(map_area, crops_dev, out_local), axis=0).astype(LOW)
    pooled_dev = lax.all_gather(pooled, "chan", axis=1, tiled=True)
    pooled_all = lax.all_gather(pooled_dev, "dp", axis=0, tiled=True)

    dealt_hot = (place_dealt[:, None] == channels[None, :]).astype(LOW)
    pooled_dealt = contract(pooled_dev, dealt_hot, 1, 0).astype(LOW)
    pooled_dealt, head_all = join(pooled_dealt, head_all)
    hidden_dev = contract(pooled_dealt, head_all[:, :hid_local], 1, 0)
    own_place = block_at(place_dealt, chan_at, hid_local, 0)
    own_dealt_hot = (own_place[:, None] == channels[None, :]).astype(LOW)
    project_rows = contract(own_dealt_hot, head_all[:, hid_local:], 1, 0).astype(LOW)
    near_head = jnp.mean(hidden_dev, axis=0, keepdims=True).astype(LOW)
    hidden_sent = (hidden_dev - near_head.astype(WIDE)).astype(LOW)
    hidden_came = spread(jnp.concatenate([hidden_sent, near_head], axis=0), "dp")
    hidden_rows = contract(
        (after(place_dealt, hidden_dev)[:, None] == channels[None, :]).astype(LOW),
        head_all[:, :hid_local],
        1,
        0,
    ).astype(LOW)
    hidden_came, hidden_rows = join(hidden_came, hidden_rows)
    hidden_pre = (
        hidden_came[:, :crops_dev].astype(WIDE) + hidden_came[:, crops_dev:].astype(WIDE)
    ).reshape(
        crop_total, hid_local
    )
    head_sums = jnp.stack([jnp.sum(hidden_pre, axis=0), jnp.sum(hidden_pre * hidden_pre, axis=0)])
    average_head, inv_head = statistics(head_sums, crop_total)
    centred_head = (hidden_pre - average_head) * inv_head
    normed_head = centred_head * head_norm[0] + head_norm[1]
    hidden_act = jax.nn.silu(normed_head).astype(LOW)
    project_out = total_hyper(contract(hidden_act, project_rows, 1, 0), "chan")
    block_rows_of = min(crop_total, max(BLOCK, crops_dev))
    labels = queue_first[:, proto_width:].reshape(-1, block_rows_of)
    crop_index = jnp.arange(block_rows_of, dtype=jnp.int32)
    same_image = (
        (labels[:, :, None] == labels[:, None, :])
        & (crop_index[:, None] != crop_index[None, :])
        & (crop_index[:, None] // crops_dev == crop_index[None, :] // crops_dev)
    )
    pairs = same_image.astype(LOW)

    codes, queue_codes, sent = call_first(
        proto_count, project_out, proto_low, queue_codes, queue_first[:, :proto_width]
    )
    came = lax.all_to_all(sent, "dp", 0, 0)
    log_norm = call_norm(proto_count, project_out, proto_low)
    for turn_index in range(2, SINK_ITERS):
        came = lax.all_to_all(call_next(proto_count, came, codes, queue_codes), "dp", 0, 0)
    came, pooled_all = join(came, pooled_all)
    score_gradient, project_low_grad, loss_total = call_last(
        proto_count, came, codes, project_out, log_norm, proto_low, pairs
    )
    loss = loss_total[0, :1] / crop_total
    normed_low = low_of(project_out)
    hidden_grad_act = contract(project_low_grad, project_rows, 1, 1) * silu_slope(normed_head)
    head_grads = jnp.stack(
        [jnp.sum(hidden_grad_act, axis=0), jnp.sum(hidden_grad_act * centred_head, axis=0)]
    )
    head_pre_low = backward_of_norm(
        hidden_grad_act, centred_head, inv_head, head_norm[0], head_grads, crop_total
    ).astype(LOW)
    pooled_terms = contract(block_at(head_pre_low, dp_at, crops_dev, 0), hidden_rows, 1, 1)
    pooled_grad = scatter_relative(relative_blocks(pooled_terms, out_local, 1), "chan", WIDE)

    spread_grad = jnp.broadcast_to(
        pooled_grad[None] / map_area, (map_area, crops_dev, out_local)
    ).reshape(pixel_rows, out_local)
    sum_grad = spread_grad * silu_slope(summed)
    third_grads = total(
        jnp.stack([jnp.sum(sum_grad, axis=0), jnp.sum(sum_grad * centred_three, axis=0)]), "dp"
    )
    project_grad = jnp.concatenate(
        gather_relative(contract(hidden_act, project_low_grad, 0, 0).astype(LOW), "chan")
    )
    third_grads, project_grad = join(third_grads, project_grad)
    third_low = backward_of_norm(
        sum_grad, centred_three, inv_three, third_norm[0], third_grads, pixel_total
    ).astype(LOW)

    def column_parts(terms):
        return [terms[:, r * mid_local : (r + 1) * mid_local] for r in range(chan_count)]

    def inner_sums(summed_terms, pre_act, average, inv_std, norm):
        centred = (pre_act - average) * inv_std
        grad = summed_terms * silu_slope(centred * norm[0] + norm[1])
        sums = jnp.stack([jnp.sum(grad, axis=0), jnp.sum(grad * centred, axis=0)])
        return grad, centred, sums

    def slot_terms(grad_rows, turned):
        slot_hot = ((slot_sent ^ (turned * out_local))[:, None] == channels[None, :]).astype(LOW)
        terms = contract(slot_hot, grad_rows, 1, 0).astype(LOW)
        return terms.reshape(dp_count, slot_local, mid_local)

    second_sum = scatter_relative(column_parts(contract(third_low, expand_rel, 1, 0)), "chan")
    expand_terms = contract(third_low, inner_two, 0, 0).astype(LOW)
    turned_hot = ((own_slots ^ (chan_at * hid_local))[:, None] == channels[None, :]).astype(LOW)
    slot_project = contract(turned_hot, project_grad, 1, 0)
    project_new = step(
        project_weight, project_moment, project_second, slot_project, hid_width ** (-0.5)
    )
    second_sum, expand_terms, *project_new = join(second_sum, expand_terms, *project_new)
    grad_two, centred_two, second_sums = inner_sums(
        second_sum, pre_two, average_two, inv_two, second_norm
    )
    expand_parts = column_parts(expand_terms)
    expand_grad = jnp.concatenate(
        [expand_parts[0]] + [swap(expand_parts[r], "chan", r) for r in range(1, chan_count)], axis=0
    )
    slot_expand = slot_terms(expand_grad, chan_at)
    own_hot = (own_slots[:, None] == channels[None, :]).astype(LOW)
    slot_hidden = contract(contract(pooled_all, own_hot, 1, 1).astype(LOW), head_pre_low, 0, 0)
    hidden_new = step(hidden_weight, hidden_moment, hidden_second, slot_hidden, in_width ** (-0.5))
    second_grads, slot_expand, *hidden_new = join(
        total(second_sums, "dp"), slot_expand, *hidden_new
    )
    expand_came = scatter_staged(slot_expand, "dp")
    second_low = backward_of_norm(
        grad_two, centred_two, inv_two, second_norm[0], second_grads, pixel_total
    ).astype(LOW)
    maps_two = second_low.reshape(map_side, map_side, crops_dev, mid_local)
    first_terms = lax.conv_general_dilated(
        maps_two,
        spatial_rel[::-1, ::-1].transpose(0, 1, 3, 2),
        (1, 1),
        ((1, 1), (1, 1)),
        dimension_numbers=conv_dims,
        preferred_element_type=WIDE,
    ).reshape(pixel_rows, mid_width)
    first_sum = scatter_relative(column_parts(first_terms), "chan")
    spatial_terms = lax.conv_general_dilated(
        maps_one,
        maps_two,
        (1, 1),
        ((1, 1), (1, 1)),
        dimension_numbers=lax.ConvDimensionNumbers((3, 2, 0, 1), (3, 2, 0, 1), (2, 3, 0, 1)),
        preferred_element_type=WIDE,
    ).reshape(9, mid_width, mid_local)
    spatial_sent = deal_rows(
        spatial_terms.astype(LOW).reshape(9 * mid_width, mid_local),
        jnp.stack([dp_at, chan_at]).astype(jnp.int32),
        dp_count,
        9,
        chan_count,
    )
    first_sum, spatial_sent = join(first_sum, spatial_sent)
    spatial_came = scatter_staged(spatial_sent, "dp")
    grad_one, centred_one, first_sums = inner_sums(
        first_sum, pre_one, average_one, inv_one, first_norm
    )
    first_grads = total_hyper(first_sums, "dp")
    first_low = backward_of_norm(
        grad_one, centred_one, inv_one, first_norm[0], first_grads, pixel_total
    ).astype(LOW)
    squeeze_grad = contract(pixels, first_low, 0, 0).astype(LOW)
    squeeze_terms = slot_terms(squeeze_grad, 0)
    squeeze_came = scatter_staged(squeeze_terms, "dp")
    first_all = jnp.concatenate(gather_relative(after(first_low, squeeze_terms), "chan"), axis=1)
    proto_grad = contract(after(score_gradient, squeeze_terms), normed_low, 0, 0)[:proto_count].T
    proto_new = step(prototypes, proto_moment, proto_second, proto_grad, 0.1)
    first_all, *proto_new = join(first_all, *proto_new)
    images_grad = contract(first_all, squeeze_rel, 1, 1) + sum_grad
    images_grad = images_grad.reshape(map_side, map_side, crops_dev, out_local).transpose(2, 0, 1, 3)
    spatial_came, expand_came, _ = join(spatial_came, expand_came, squeeze_terms)
    images_grad, squeeze_came = join(images_grad, squeeze_came)
    slot_squeeze, slot_spatial, slot_expand = [
        wide_sum(came) for came in (squeeze_came, spatial_came, expand_came)
    ]
    norm_gradient = jnp.concatenate([first_grads, second_grads, third_grads, head_grads], axis=1)
    norm_gradient = norm_gradient[::-1].reshape(norm_params.shape)
    return (
        block_out,
        loss,
        images_grad,
        *step(squeeze_weight, squeeze_moment, squeeze_second, slot_squeeze, in_width ** (-0.5)),
        *step(
            spatial_weight, spatial_moment, spatial_second, slot_spatial, (9 * mid_width) ** (-0.5)
        ),
        *step(expand_weight, expand_moment, expand_second, slot_expand, mid_width ** (-0.5)),
        *hidden_new,
        *project_new,
        *proto_new,
        *step(norm_params, norm_moment, norm_second, norm_gradient, 0.5, 0.0),
    )


def solution(mesh):
    rows, both, whole = P("dp", None), P("dp", "chan"), P()
    maps = P("dp", None, None, "chan")
    norm = P(None, "chan", None)
    placed = (
        (P("dp", None, None, None), P("dp"), whole)
        + (both,) * 12
        + (rows,) * 3
        + (whole,) * 3
        + (norm,) * 3
        + (rows, P("dp"), whole, whole)
    )
    return jax.shard_map(
        local,
        mesh=mesh,
        in_specs=placed,
        out_specs=(maps, whole, maps) + (both,) * 12 + (rows,) * 3 + (whole,) * 3 + (norm,) * 3,
        check_vma=False,
    )
```

```python
import math

import jax
import jax.numpy as jnp
from jax import lax
from jax.experimental import pallas as pl
from jax.experimental.pallas import tpu as pltpu
from jax.sharding import PartitionSpec as P

SINK_ITERS = 3
PRECISE = lax.Precision.HIGHEST
EPS_SINK = 0.05
SOFTMAX_WARMTH = 0.1
LOSS_MULTIPLIER = 256.0
NORM_EPS = 1e-05
BETA_ONE = 0.5
BETA_TWO = 0.5
ADAM_EPS = 1e-08
DECAY_RATE = 1e-06
LOW = jnp.bfloat16
WIDE = jnp.float32


def contract(left, right, left_dim, right_dim):
    return lax.dot_general(
        left, right, (((left_dim,), (right_dim,)), ((), ())), preferred_element_type=WIDE
    )


def silu_slope(value):
    sigma = jax.nn.sigmoid(value)
    return sigma * (1.0 + value * (1.0 - sigma))


def spread(value, axis):
    count = lax.axis_size(axis)
    return lax.all_to_all(jnp.broadcast_to(value[None], (count,) + value.shape), axis, 0, 0)


def total(value, axis):
    return jnp.sum(spread(value, axis).astype(WIDE), axis=0)


def swap(value, axis, bit):
    return lax.ppermute(value, axis, [(at, at ^ bit) for at in range(lax.axis_size(axis))])


def gather_relative(value, axis):
    held = {0: value}
    bit = lax.axis_size(axis) // 2
    while bit:
        keys = sorted(held)
        came = swap(jnp.stack([held[k] for k in keys]), axis, bit)
        held.update({k ^ bit: came[n] for n, k in enumerate(keys)})
        bit //= 2
    return [held[k] for k in range(lax.axis_size(axis))]


def invert_kernel(slots_ref, place_ref, rank_ref):
    count = slots_ref.shape[0]
    channels = place_ref.shape[0] - 128

    def step(at, rank):
        for n in range(16):
            slot = at * 16 + n
            channel = slots_ref[slot]
            place_ref[channel] = slot
            rank_ref[channel] = rank
            rank = rank + jnp.where(channel < channels, 1, 0)
        return rank

    lax.fori_loop(0, count // 16, step, jnp.int32(0))


def slot_of_channel(slot_rows, channels):
    smem = pl.BlockSpec(memory_space=pltpu.SMEM)
    return pl.pallas_call(
        invert_kernel,
        out_shape=[jax.ShapeDtypeStruct((channels + 128,), jnp.int32)] * 2,
        in_specs=[smem],
        out_specs=[smem] * 2,
        name="slot_of_channel",
    )(slot_rows)


def pick_kernel(first, count, place_ref, turn_ref, *refs):
    *blocks, out_ref, wide, picked = refs
    at = 0
    for block in blocks:
        for part in [block.at[k] for k in range(block.shape[0])] if len(block.shape) == 3 else [block]:
            wide[at : at + count, :] = part[first : first + count, :].astype(WIDE)
            at += count

    def step(group, carry):
        for n in range(8):
            row = group * 8 + n
            picked[pl.ds(row, 1), :] = wide[pl.ds(place_ref[(group * 8 ^ turn_ref[0]) + n], 1), :]
        return carry

    lax.fori_loop(0, out_ref.shape[0] // 8, step, 0)
    out_ref[...] = picked[...].astype(out_ref.dtype)


def pick_rows(place, turn, blocks, rows, first, count):
    width = blocks[0].shape[-1]
    held = sum(block.size // (width * block.shape[-2]) for block in blocks) * count
    vmem = pl.BlockSpec()
    return pl.pallas_call(
        lambda *refs: pick_kernel(first, count, *refs),
        out_shape=jax.ShapeDtypeStruct((rows, width), LOW),
        in_specs=[pl.BlockSpec(memory_space=pltpu.SMEM)] * 2 + [vmem] * len(blocks),
        out_specs=vmem,
        scratch_shapes=[pltpu.VMEM((held, width), WIDE), pltpu.VMEM((rows, width), WIDE)],
        compiler_params=pltpu.CompilerParams(vmem_limit_bytes=12 << 20),
        cost_estimate=pl.CostEstimate(
            flops=0, bytes_accessed=2 * (held + rows) * width, transcendentals=0
        ),
        name="pick_rows",
    )(place, turn, *blocks)


def assemble_kernel(taps, chan_count, rows, at_ref, held_ref, out_ref):
    per_tap = out_ref.shape[0] // taps
    per_chan = per_tap // chan_count
    size = math.gcd(rows, per_chan)
    for row in range(0, out_ref.shape[0], size):
        tap, inner = divmod(row, per_tap)
        chan, rest = divmod(inner, per_chan)
        target = pl.multiple_of((chan ^ at_ref[0]) * per_chan + tap * per_tap + rest, size)
        owner, source = divmod(row, rows)
        out_ref[pl.ds(target, size), :] = held_ref[owner, source : source + size, :]


def assemble(held, at, rows, taps, chan_count):
    vmem = pl.BlockSpec()
    return pl.pallas_call(
        lambda *refs: assemble_kernel(taps, chan_count, rows, *refs),
        out_shape=jax.ShapeDtypeStruct((rows * held.shape[0], held.shape[2]), LOW),
        in_specs=[pl.BlockSpec(memory_space=pltpu.SMEM), vmem],
        out_specs=vmem,
        compiler_params=pltpu.CompilerParams(vmem_limit_bytes=12 << 20),
        cost_estimate=pl.CostEstimate(
            flops=0, bytes_accessed=4 * rows * held.shape[0] * held.shape[2], transcendentals=0
        ),
        name="assemble",
    )(at, held)


def deal_kernel(taps, chan_count, order, at_ref, terms_ref, out_ref):
    rows = out_ref.shape[1]
    per_tap = terms_ref.shape[0] // taps
    per_chan = per_tap // chan_count
    size = math.gcd(rows, per_chan)
    for n, r in enumerate(order):
        for start in range(0, rows, size):
            row = (at_ref[0] ^ r) * rows + start
            tap, inner = row // per_tap, row % per_tap
            chan, rest = inner // per_chan, inner % per_chan
            source = tap * per_tap + (chan ^ at_ref[1]) * per_chan + rest
            source = pl.multiple_of(source, size)
            out_ref[n, start : start + size, :] = terms_ref[pl.ds(source, size), :]


def deal_rows(terms, at, owners, taps, chan_count):
    order = send_order(owners)
    vmem = pl.BlockSpec()
    return pl.pallas_call(
        lambda *refs: deal_kernel(taps, chan_count, order, *refs),
        out_shape=jax.ShapeDtypeStruct((owners, terms.shape[0] // owners, terms.shape[1]), LOW),
        in_specs=[pl.BlockSpec(memory_space=pltpu.SMEM), vmem],
        out_specs=vmem,
        compiler_params=pltpu.CompilerParams(vmem_limit_bytes=12 << 20),
        cost_estimate=pl.CostEstimate(flops=0, bytes_accessed=4 * terms.size, transcendentals=0),
        name="deal_rows",
    )(at, terms)


ROWS = 16
BLOCK = 128


def whole(count):
    return [pl.BlockSpec()] * count


def over_rows(total_rows, body, size=ROWS):
    def step(at, carry):
        body(pl.ds(pl.multiple_of(at * size, size), size))
        return carry

    lax.fori_loop(0, total_rows // size, step, 0)


def sum_rows(total_rows, width, body, size):
    def step(at, held):
        value = body(pl.ds(pl.multiple_of(at * size, size), size))
        for first in range(0, size, 8):
            held = held + value[first : first + 8]
        return held

    held = lax.fori_loop(0, total_rows // size, step, jnp.zeros((8, width), WIDE))
    return jnp.sum(held, axis=0, keepdims=True)


def inverse_of(row_sums):
    return 1.0 / jnp.where(row_sums > 0.0, row_sums, 1.0)


def known_columns(width, known):
    return lax.broadcasted_iota(jnp.int32, (1, width), 1) < known


def fill(target, value):
    for at in range(target.shape[0]):
        target[at] = value


def low_of(z):
    return (z * lax.rsqrt(jnp.sum(z * z, axis=1, keepdims=True) + 1e-06)).astype(LOW)


def weigh_columns(matrix, factors):
    factors = jnp.broadcast_to(factors.astype(LOW), (128, factors.shape[1]))
    return contract(matrix.astype(LOW), factors, 1, 1)


def in_all_tiles(value, width):
    return jnp.concatenate([value] * (width // 128), axis=1)


def first_turn(
    known, z_ref, first_ref, proto_any, queue_any, b_ref, bq_any, sent_any, proto, bq, sent, inv, row_inv, sems
):
    proto_in = pltpu.make_async_copy(proto_any, proto, sems.at[0])
    queue_in = pltpu.make_async_copy(queue_any, bq, sems.at[1])
    queue_out = pltpu.make_async_copy(bq, bq_any, sems.at[2])
    sent_out = pltpu.make_async_copy(sent, sent_any, sems.at[3])
    proto_in.start()
    queue_in.start()
    low = low_of(z_ref[...])
    proto_in.wait()
    b_ref[...] = contract(low, proto[...], 1, 1)
    lines, width = bq.shape
    total_rows = b_ref.shape[0]
    mask = known_columns(width, known)

    def exponentials(rows):
        value = jnp.where(mask, jnp.exp(b_ref[rows, :] * (1.0 / EPS_SINK)), 0.0)
        b_ref[rows, :] = value
        return value

    totals = sum_rows(total_rows, width, exponentials, 8)
    totals = totals + jnp.sum(first_ref[...], axis=0, keepdims=True)
    factors = jnp.where(mask, 1.0 / jnp.where(mask, totals * 0.125, 1.0), 0.0)
    inv[...] = jnp.broadcast_to(factors, inv.shape)
    queue_in.wait()
    row_inv[pl.ds(0, lines), :] = inverse_of(weigh_columns(bq[...], factors))

    def queue(rows):
        factor = jnp.concatenate([inv[...]] * 2, axis=0)
        value = bq[rows, :].astype(WIDE) * factor * in_all_tiles(row_inv[rows, :], width)
        bq[rows, :] = value.astype(LOW)
        return value

    queue_sums = sum_rows(lines, width, queue, 16)
    queue_out.start()
    row_inv[pl.ds(0, total_rows), :] = inverse_of(weigh_columns(b_ref[...], factors))

    def batch(rows):
        value = b_ref[rows, :] * inv[...] * in_all_tiles(row_inv[rows, :], width)
        b_ref[rows, :] = value
        return value

    batch_sums = sum_rows(total_rows, width, batch, 8)
    fill(sent, queue_sums + batch_sums * (1.0 / sent.shape[0]))
    sent_out.start()
    queue_out.wait()
    sent_out.wait()


def column_factor(known, came_ref):
    totals = jnp.sum(came_ref[...], axis=0)
    mask = known_columns(totals.shape[1], known)
    return jnp.where(mask, 1.0 / jnp.where(mask, totals, 1.0), 0.0)


def next_turn(known, came_ref, b_ref, bq_any, sent_any, bq, sent, row_inv, sems):
    queue_in = pltpu.make_async_copy(bq_any, bq, sems.at[0])
    sent_out = pltpu.make_async_copy(sent, sent_any, sems.at[1])
    queue_in.start()
    factors = column_factor(known, came_ref)

    def weigh(source, size):
        total_rows, width = source.shape
        row_inv[pl.ds(0, total_rows), :] = inverse_of(weigh_columns(source[...], factors))

        def body(rows):
            return source[rows, :].astype(WIDE) * in_all_tiles(row_inv[rows, :], width)

        return sum_rows(total_rows, width, body, size)

    batch_sums = weigh(b_ref, 8)
    queue_in.wait()
    fill(sent, weigh(bq, 16) + batch_sums * (1.0 / sent.shape[0]))
    sent_out.start()
    sent_out.wait()


def norm_of_scores(known, z_ref, proto_any, norm_ref, proto, scores, sems):
    proto_in = pltpu.make_async_copy(proto_any, proto, sems.at[0])
    proto_in.start()
    low = low_of(z_ref[...])
    proto_in.wait()
    scores[...] = contract(low, proto[...], 1, 1)
    mask = known_columns(scores.shape[1], known)

    def body(rows):
        raw = scores[rows, :] * (1.0 / SOFTMAX_WARMTH)
        top = jnp.max(jnp.where(mask, raw, -jnp.inf), axis=1, keepdims=True)
        mass = jnp.sum(jnp.where(mask, jnp.exp(raw - top), 0.0), axis=1, keepdims=True)
        norm_ref[rows, :] = top + jnp.log(mass)

    over_rows(scores.shape[0], body)


def last_turn(
    known,
    came_ref,
    b_ref,
    z_ref,
    norm_ref,
    proto_any,
    pairs_any,
    grad_any,
    low_grad_ref,
    loss_ref,
    proto,
    pairs,
    grad,
    scores,
    high,
    rest,
    held,
    inv,
    sems,
):
    proto_in = pltpu.make_async_copy(proto_any, proto, sems.at[0])
    pairs_in = pltpu.make_async_copy(pairs_any, pairs, sems.at[1])
    grad_out = pltpu.make_async_copy(grad, grad_any, sems.at[2])
    proto_in.start()
    pairs_in.start()
    factors = column_factor(known, came_ref)
    inv[...] = factors
    mask = known_columns(factors.shape[1], known)
    size = pairs.shape[1]
    loss_ref[...] = jnp.zeros(loss_ref.shape, WIDE)
    proto_in.wait()
    pairs_in.wait()

    def block(at, carry):
        def here(rows):
            return pl.ds(pl.multiple_of(at * size + rows, 8), ROWS)

        place = pl.ds(pl.multiple_of(at * size, size), size)
        z = z_ref[place, :]
        inv_len = lax.rsqrt(jnp.sum(z * z, axis=1, keepdims=True) + 1e-06)
        scores[...] = contract((z * inv_len).astype(LOW), proto[...], 1, 1)
        for first in range(0, size, ROWS):
            value = b_ref[here(first), :] * inv[...]
            value = value * (1.0 / jnp.sum(value, axis=1, keepdims=True))
            top = value.astype(LOW)
            high[first : first + ROWS, :] = top
            rest[first : first + ROWS, :] = (value - top.astype(WIDE)).astype(LOW)
        pair = pairs[at]
        others = jnp.sum(pair.astype(WIDE), axis=1, keepdims=True)
        inv_others = 1.0 / jnp.maximum(others, 1.0)
        held[...] = contract(pair, high[...], 1, 0) + contract(pair, rest[...], 1, 0)
        for first in range(0, size, ROWS):
            rows = slice(first, first + ROWS)
            targets = held[rows, :] * inv_others[rows]
            logs = scores[rows, :] * (1.0 / SOFTMAX_WARMTH) - norm_ref[here(first), :]
            loss_ref[...] -= jnp.sum(jnp.where(mask, targets * logs, 0.0))
            weight = jnp.sum(targets, axis=1, keepdims=True)
            value = (LOSS_MULTIPLIER / SOFTMAX_WARMTH) * (jnp.exp(logs) * weight - targets)
            grad[here(first), :] = jnp.where(mask, value, 0.0).astype(LOW)
        normed_grad = contract(grad[place, :], proto[...], 1, 0)
        normed = z * inv_len
        along = jnp.sum(normed * normed_grad, axis=1, keepdims=True)
        low_grad_ref[place, :] = (inv_len * (normed_grad - normed * along)).astype(LOW)
        return carry

    lax.fori_loop(0, pairs.shape[0], block, 0)
    grad_out.start()
    grad_out.wait()


def shape(dims, kind=WIDE):
    return jax.ShapeDtypeStruct(dims, kind)


def turn_call(kernel, known, outs, anywhere_out, close, anywhere, scratch, copies, aliases={}):
    near, far = pl.BlockSpec(memory_space=pltpu.VMEM), pl.BlockSpec(memory_space=pltpu.HBM)
    held = sum(value.size * value.dtype.itemsize for value in (*scratch, *close, *outs))
    return pl.pallas_call(
        lambda *refs: kernel(known, *refs),
        out_shape=outs,
        in_specs=[near] * len(close) + [far] * len(anywhere),
        out_specs=[far if at in anywhere_out else near for at in range(len(outs))],
        scratch_shapes=[pltpu.VMEM(value.shape, value.dtype) for value in scratch]
        + [pltpu.SemaphoreType.DMA((copies,))],
        compiler_params=pltpu.CompilerParams(vmem_limit_bytes=min(held + (8 << 20), 60 << 20)),
        input_output_aliases=aliases,
        name=kernel.__name__,
    )(*close, *[pltpu.with_memory_space_constraint(value, pltpu.HBM) for value in anywhere])


def call_first(known, z, proto, queue, first):
    rows, width, lines, owners = z.shape[0], proto.shape[0], queue.shape[0], first.shape[0]
    sent = shape((owners, 1, width))
    return turn_call(
        first_turn,
        known,
        [shape((rows, width)), shape(queue.shape, LOW), sent],
        (1, 2),
        (z, first),
        (proto, queue),
        [
            shape(proto.shape, LOW),
            shape(queue.shape, LOW),
            sent,
            shape((8, width)),
            shape((max(rows, lines), 128)),
        ],
        4,
        {3: 1},
    )


def call_next(known, came, b, bq):
    return turn_call(
        next_turn,
        known,
        [shape(came.shape)],
        (0,),
        (came, b),
        (bq,),
        [shape(bq.shape, LOW), shape(came.shape), shape((max(b.shape[0], bq.shape[0]), 128))],
        2,
    )[0]


def call_norm(known, z, proto):
    rows, width = z.shape[0], proto.shape[0]
    return turn_call(
        norm_of_scores,
        known,
        [shape((rows, 1))],
        (),
        (z,),
        (proto,),
        [shape(proto.shape, LOW), shape((rows, width))],
        1,
    )[0]


def call_last(known, came, b, z, norm, proto, pairs):
    width, size = b.shape[1], pairs.shape[1]
    part = (size, width)
    return turn_call(
        last_turn,
        known,
        [shape(b.shape, LOW), shape(z.shape, LOW), shape((8, 128))],
        (0,),
        (came, b, z, norm),
        (proto, pairs),
        [
            shape(proto.shape, LOW),
            shape(pairs.shape, LOW),
            shape(b.shape, LOW),
            shape(part),
            shape(part, LOW),
            shape(part, LOW),
            shape(part),
            shape((1, width)),
        ],
        3,
    )


def after(value, token):
    return lax.optimization_barrier((value, token))[0]


def join(*values):
    return lax.optimization_barrier(values)


def scatter_relative(parts, axis, sent=LOW):
    held = dict(enumerate(parts))
    bit = 1
    while bit < lax.axis_size(axis):
        keys = [k for k in sorted(held) if not k & bit]
        came = swap(jnp.stack([held[k | bit].astype(sent) for k in keys]), axis, bit)
        held = {k: held[k] + came[n].astype(WIDE) for n, k in enumerate(keys)}
        bit *= 2
    return held[0]


def send_order(count):
    low = max(count // 4, 1)
    order = list(range(0, count, low))
    bit = low // 2
    while bit:
        order = order + [r | bit for r in order]
        bit //= 2
    return order


def scatter_staged(blocks, axis):
    count = lax.axis_size(axis)
    low = max(count // 4, 1)
    held = blocks
    bit = 1
    while bit < low:
        half = held.shape[0] // 2
        came = swap(held[half:], axis, bit)
        held = (held[:half].astype(WIDE) + came.astype(WIDE)).astype(LOW)
        bit *= 2
    came = [swap(held[n], axis, n * low) for n in range(1, held.shape[0])]
    return held[0], came


def wide_sum(terms):
    kept, came = terms
    result = kept.astype(WIDE)
    for value in came:
        result = result + value.astype(WIDE)
    return result


def total_hyper(value, axis):
    bit = 1
    while bit < lax.axis_size(axis):
        value = value + swap(value, axis, bit)
        bit *= 2
    return value


def block_at(value, index, size, dim):
    return lax.dynamic_slice_in_dim(value, index * size, size, dim)


def statistics(sums, row_total):
    average = sums[0] / row_total
    variance = sums[1] / row_total - average * average
    return average, lax.rsqrt(variance + NORM_EPS)


def backward_of_norm(grad_out, centred, inv_std, gain_row, sums, row_total):
    return gain_row * inv_std * (grad_out - (sums[0] + centred * sums[1]) / row_total)


def adamw_step(weight, moment_one, moment_two, gradient, learn_rate, weight_decay, step_count):
    moment_new = BETA_ONE * moment_one + (1.0 - BETA_ONE) * gradient
    second_new = BETA_TWO * moment_two + (1.0 - BETA_TWO) * gradient * gradient
    fix_one = 1.0 - jnp.power(BETA_ONE, step_count)
    fix_two = 1.0 - jnp.power(BETA_TWO, step_count)
    update = moment_new / fix_one / (jnp.sqrt(second_new / fix_two) + ADAM_EPS)
    return (weight - learn_rate * (update + weight_decay * weight), moment_new, second_new)


def local(
    images,
    crop_image,
    slot_rows,
    squeeze_weight,
    squeeze_moment,
    squeeze_second,
    spatial_weight,
    spatial_moment,
    spatial_second,
    expand_weight,
    expand_moment,
    expand_second,
    hidden_weight,
    hidden_moment,
    hidden_second,
    project_weight,
    project_moment,
    project_second,
    prototypes,
    proto_moment,
    proto_second,
    norm_params,
    norm_moment,
    norm_second,
    queue_rows,
    queue_valid,
    queue_fill,
    iteration,
):
    dp_count = lax.axis_size("dp")
    dp_at = lax.axis_index("dp")
    chan_count = lax.axis_size("chan")
    chan_at = lax.axis_index("chan")
    crops_dev, map_side, _, in_width = images.shape
    map_area = map_side * map_side
    pixel_rows = crops_dev * map_area
    pixel_total = pixel_rows * dp_count
    crop_total = crops_dev * dp_count
    mid_local = squeeze_weight.shape[1]
    hid_local = hidden_weight.shape[1]
    out_local = in_width // chan_count
    slot_local = squeeze_weight.shape[0]
    slot_total = slot_rows.shape[0]
    mid_width = mid_local * chan_count
    hid_width = hid_local * chan_count

    squeeze_came = spread(squeeze_weight.astype(LOW), "dp")
    tap_local = spatial_weight.shape[0]
    convs_all = lax.all_gather(
        jnp.concatenate([spatial_weight.astype(LOW), expand_weight.astype(LOW)], axis=0), "dp"
    )

    channels = jnp.arange(in_width, dtype=jnp.int32)
    used = (slot_rows < in_width).astype(jnp.int32).reshape(dp_count, slot_local)
    loads = jnp.sum(used, axis=1)
    owners = jnp.arange(dp_count, dtype=jnp.int32)
    firsts = jnp.sum(jnp.where(owners[None, :] < owners[:, None], loads[None, :], 0), axis=1)
    own_used = block_at(used, dp_at, 1, 0)[0]
    own_first = block_at(firsts, dp_at, 1, 0)
    own_at = jnp.arange(slot_local, dtype=jnp.int32)
    own_rank = jnp.sum(jnp.where(own_at[None, :] < own_at[:, None], own_used[None, :], 0), axis=1)
    cell = slot_local // dp_count
    share = in_width // dp_count
    target = (own_first + own_rank) % dp_count * cell + own_rank // dp_count
    deal_hot = ((target[None, :] == own_at[:, None]) & (own_used[None, :] > 0)).astype(LOW)
    head_low = jnp.concatenate([hidden_weight.astype(LOW), project_weight.astype(LOW)], axis=1)
    dealt = contract(deal_hot, head_low, 1, 0).astype(LOW)
    ranks = (
        jnp.arange(cell, dtype=jnp.int32)[None, :] * dp_count + (dp_at - firsts[:, None]) % dp_count
    )
    share_at = jnp.where(ranks < loads[:, None], (firsts[:, None] + ranks) // dp_count, -1)
    share_at = share_at.reshape(slot_local)
    place, rank = slot_of_channel(slot_rows, in_width)
    slot_blocks = slot_rows.reshape(dp_count, slot_local)
    slot_sent = jnp.concatenate(
        [lax.dynamic_index_in_dim(slot_blocks, dp_at ^ r, 0, False) for r in send_order(dp_count)]
    )
    own_slots = slot_sent[:slot_local]
    place_dealt = (rank % dp_count * share + rank // dp_count)[:in_width]

    proto_count = prototypes.shape[1]
    proto_low = jnp.pad(prototypes.astype(LOW).T, ((0, -proto_count % 256), (0, 0)))
    proto_width = proto_low.shape[0]
    queue_len = queue_rows.shape[0]
    slot_index = dp_at * queue_len + jnp.arange(queue_len, dtype=jnp.int32)
    queue_live = ((queue_valid > 0) & (slot_index < queue_fill[0])).astype(WIDE)
    queue_live = jnp.pad(queue_live, (0, -queue_len % ROWS))
    queue_similarity = contract(
        jnp.pad(queue_rows, ((0, -queue_len % ROWS), (0, 0))), proto_low, 1, 1
    )
    queue_codes = jnp.where(
        (jnp.arange(proto_width) < proto_count)[None, :],
        jnp.exp(queue_similarity / EPS_SINK) * queue_live[:, None],
        0.0,
    )
    queue_mass = jnp.sum(queue_codes, axis=0)
    queue_codes = queue_codes.astype(LOW)
    squeeze_came, queue_codes, queue_mass, slot_sent, proto_low = join(
        squeeze_came, queue_codes, queue_mass, slot_sent, proto_low
    )
    straight = jnp.zeros((1,), jnp.int32)
    turned = (chan_at * out_local).astype(jnp.int32).reshape(1)
    squeeze_rows = pick_rows(place, straight, [squeeze_came], in_width, 0, slot_local)

    norm_rows = norm_params[:, 0, :]
    first_norm = norm_rows[:, :mid_local]
    second_norm = norm_rows[:, mid_local : 2 * mid_local]
    third_norm = norm_rows[:, 2 * mid_local : 2 * mid_local + out_local]
    head_norm = norm_rows[:, 2 * mid_local + out_local :]

    def inner_layer(pre_act, norm, token=None):
        sums = jnp.stack([jnp.sum(pre_act, axis=0), jnp.sum(pre_act * pre_act, axis=0)])
        near = sums[0] / pixel_rows
        if token is not None:
            sums = after(sums, token)
        raw_all = jnp.concatenate(gather_relative((pre_act - near).astype(LOW), "chan"), axis=1)
        average, inv_std = statistics(total(sums, "dp"), pixel_total)
        scale = inv_std * norm[0]
        affine = jnp.stack([scale, norm[1] - (average - near) * scale])
        affine_all = jnp.concatenate(gather_relative(affine, "chan"), axis=1)
        act_all = jax.nn.silu(raw_all.astype(WIDE) * affine_all[0] + affine_all[1]).astype(LOW)
        return act_all, average, inv_std

    step_count = iteration[0].astype(WIDE)

    def step(weight, moment, second, gradient, rate, decay=DECAY_RATE):
        return adamw_step(weight, moment, second, gradient, rate, decay, step_count)

    pixels = images.transpose(1, 2, 0, 3).reshape(pixel_rows, in_width)
    pre_one = contract(pixels, squeeze_rows, 1, 0)
    inner_one, average_one, inv_one = inner_layer(pre_one, first_norm)
    dealt = lax.all_to_all(after(dealt, average_one).reshape(dp_count, cell, -1), "dp", 0, 0)
    def relative_blocks(value, size, dim):
        return [block_at(value, chan_at ^ r, size, dim) for r in range(chan_count)]

    spatial_rel = assemble(
        convs_all, chan_at.astype(jnp.int32).reshape(1), tap_local, 9, chan_count
    ).reshape(3, 3, mid_width, mid_local)
    maps_one = inner_one.reshape(map_side, map_side, crops_dev, mid_width)
    conv_dims = lax.ConvDimensionNumbers((2, 3, 0, 1), (3, 2, 0, 1), (2, 3, 0, 1))
    pre_two = lax.conv_general_dilated(
        maps_one,
        spatial_rel,
        (1, 1),
        ((1, 1), (1, 1)),
        dimension_numbers=conv_dims,
        preferred_element_type=WIDE,
    ).reshape(pixel_rows, mid_local)
    pre_two, dealt = join(pre_two, dealt)
    share_hot = (share_at[None, :] == channels[:share, None]).astype(LOW)
    shared = contract(share_hot, dealt.reshape(slot_local, -1), 1, 0).astype(LOW)
    head_all = lax.all_gather(shared, "dp", axis=0, tiled=True)

    inner_two, average_two, inv_two = inner_layer(pre_two, second_norm, shared)

    expand_rows = pick_rows(place, turned, [convs_all], in_width, tap_local, slot_local)

    def swap_blocks(blocks):
        return jnp.concatenate(
            [blocks[0]] + [swap(blocks[r], "chan", r) for r in range(1, chan_count)], axis=1
        )

    expand_rel = swap_blocks(
        [expand_rows[r * out_local : (r + 1) * out_local] for r in range(chan_count)]
    )
    squeeze_rel = swap_blocks(relative_blocks(squeeze_rows, out_local, 0))
    pre_three = contract(inner_two, expand_rel, 1, 1)
    sent_three = [
        jnp.sum(pre_three, axis=0),
        jnp.sum(pre_three * pre_three, axis=0),
        queue_mass,
        crop_image.astype(WIDE),
    ]
    came_three = spread(jnp.concatenate(sent_three), "dp")
    sums_three = jnp.sum(came_three[:, : 2 * out_local], axis=0).reshape(2, out_local)
    queue_first = came_three[:, 2 * out_local :]
    average_three, inv_three = statistics(sums_three, pixel_total)
    centred_three = (pre_three - average_three) * inv_three
    residual_in = block_at(pixels, chan_at, out_local, 1).astype(WIDE)
    summed = centred_three * third_norm[0] + third_norm[1] + residual_in
    block_rows = jax.nn.silu(summed)
    block_out = block_rows.astype(LOW).reshape(map_side, map_side, crops_dev, out_local)
    block_out = block_out.transpose(2, 0, 1, 3)
    pooled = jnp.mean(block_rows.reshape(map_area, crops_dev, out_local), axis=0).astype(LOW)
    pooled_dev = lax.all_gather(pooled, "chan", axis=1, tiled=True)
    pooled_all = lax.all_gather(pooled_dev, "dp", axis=0, tiled=True)

    dealt_hot = (place_dealt[:, None] == channels[None, :]).astype(LOW)
    pooled_dealt = contract(pooled_dev, dealt_hot, 1, 0).astype(LOW)
    pooled_dealt, head_all = join(pooled_dealt, head_all)
    hidden_dev = contract(pooled_dealt, head_all[:, :hid_local], 1, 0)
    own_place = block_at(place_dealt, chan_at, hid_local, 0)
    own_dealt_hot = (own_place[:, None] == channels[None, :]).astype(LOW)
    project_rows = contract(own_dealt_hot, head_all[:, hid_local:], 1, 0).astype(LOW)
    near_head = jnp.mean(hidden_dev, axis=0, keepdims=True).astype(LOW)
    hidden_sent = (hidden_dev - near_head.astype(WIDE)).astype(LOW)
    hidden_came = spread(jnp.concatenate([hidden_sent, near_head], axis=0), "dp")
    hidden_rows = contract(
        (after(place_dealt, hidden_dev)[:, None] == channels[None, :]).astype(LOW),
        head_all[:, :hid_local],
        1,
        0,
    ).astype(LOW)
    hidden_came, hidden_rows = join(hidden_came, hidden_rows)
    hidden_pre = (
        hidden_came[:, :crops_dev].astype(WIDE) + hidden_came[:, crops_dev:].astype(WIDE)
    ).reshape(
        crop_total, hid_local
    )
    head_sums = jnp.stack([jnp.sum(hidden_pre, axis=0), jnp.sum(hidden_pre * hidden_pre, axis=0)])
    average_head, inv_head = statistics(head_sums, crop_total)
    centred_head = (hidden_pre - average_head) * inv_head
    normed_head = centred_head * head_norm[0] + head_norm[1]
    hidden_act = jax.nn.silu(normed_head).astype(LOW)
    project_out = total_hyper(contract(hidden_act, project_rows, 1, 0), "chan")
    block_rows_of = min(crop_total, max(BLOCK, crops_dev))
    labels = queue_first[:, proto_width:].reshape(-1, block_rows_of)
    crop_index = jnp.arange(block_rows_of, dtype=jnp.int32)
    same_image = (
        (labels[:, :, None] == labels[:, None, :])
        & (crop_index[:, None] != crop_index[None, :])
        & (crop_index[:, None] // crops_dev == crop_index[None, :] // crops_dev)
    )
    pairs = same_image.astype(LOW)

    codes, queue_codes, sent = call_first(
        proto_count, project_out, proto_low, queue_codes, queue_first[:, :proto_width]
    )
    came = lax.all_to_all(sent, "dp", 0, 0)
    log_norm = call_norm(proto_count, project_out, proto_low)
    for turn_index in range(2, SINK_ITERS):
        came = lax.all_to_all(call_next(proto_count, came, codes, queue_codes), "dp", 0, 0)
    came, pooled_all = join(came, pooled_all)
    score_gradient, project_low_grad, loss_total = call_last(
        proto_count, came, codes, project_out, log_norm, proto_low, pairs
    )
    loss = loss_total[0, :1] / crop_total
    normed_low = low_of(project_out)
    hidden_grad_act = contract(project_low_grad, project_rows, 1, 1) * silu_slope(normed_head)
    head_grads = jnp.stack(
        [jnp.sum(hidden_grad_act, axis=0), jnp.sum(hidden_grad_act * centred_head, axis=0)]
    )
    head_pre_low = backward_of_norm(
        hidden_grad_act, centred_head, inv_head, head_norm[0], head_grads, crop_total
    ).astype(LOW)
    pooled_terms = contract(block_at(head_pre_low, dp_at, crops_dev, 0), hidden_rows, 1, 1)
    pooled_grad = scatter_relative(relative_blocks(pooled_terms, out_local, 1), "chan", WIDE)

    spread_grad = jnp.broadcast_to(
        pooled_grad[None] / map_area, (map_area, crops_dev, out_local)
    ).reshape(pixel_rows, out_local)
    sum_grad = spread_grad * silu_slope(summed)
    third_grads = total(
        jnp.stack([jnp.sum(sum_grad, axis=0), jnp.sum(sum_grad * centred_three, axis=0)]), "dp"
    )
    project_grad = jnp.concatenate(
        gather_relative(contract(hidden_act, project_low_grad, 0, 0).astype(LOW), "chan")
    )
    third_grads, project_grad = join(third_grads, project_grad)
    third_low = backward_of_norm(
        sum_grad, centred_three, inv_three, third_norm[0], third_grads, pixel_total
    ).astype(LOW)

    def column_parts(terms):
        return [terms[:, r * mid_local : (r + 1) * mid_local] for r in range(chan_count)]

    def inner_sums(summed_terms, pre_act, average, inv_std, norm):
        centred = (pre_act - average) * inv_std
        grad = summed_terms * silu_slope(centred * norm[0] + norm[1])
        sums = jnp.stack([jnp.sum(grad, axis=0), jnp.sum(grad * centred, axis=0)])
        return grad, centred, sums

    def slot_terms(grad_rows, turned):
        slot_hot = ((slot_sent ^ (turned * out_local))[:, None] == channels[None, :]).astype(LOW)
        terms = contract(slot_hot, grad_rows, 1, 0).astype(LOW)
        return terms.reshape(dp_count, slot_local, mid_local)

    second_sum = scatter_relative(column_parts(contract(third_low, expand_rel, 1, 0)), "chan")
    expand_terms = contract(third_low, inner_two, 0, 0).astype(LOW)
    turned_hot = ((own_slots ^ (chan_at * hid_local))[:, None] == channels[None, :]).astype(LOW)
    slot_project = contract(turned_hot, project_grad, 1, 0)
    project_new = step(
        project_weight, project_moment, project_second, slot_project, hid_width ** (-0.5)
    )
    second_sum, expand_terms, *project_new = join(second_sum, expand_terms, *project_new)
    grad_two, centred_two, second_sums = inner_sums(
        second_sum, pre_two, average_two, inv_two, second_norm
    )
    expand_parts = column_parts(expand_terms)
    expand_grad = jnp.concatenate(
        [expand_parts[0]] + [swap(expand_parts[r], "chan", r) for r in range(1, chan_count)], axis=0
    )
    slot_expand = slot_terms(expand_grad, chan_at)
    own_hot = (own_slots[:, None] == channels[None, :]).astype(LOW)
    slot_hidden = contract(contract(pooled_all, own_hot, 1, 1).astype(LOW), head_pre_low, 0, 0)
    hidden_new = step(hidden_weight, hidden_moment, hidden_second, slot_hidden, in_width ** (-0.5))
    second_grads, slot_expand, *hidden_new = join(
        total(second_sums, "dp"), slot_expand, *hidden_new
    )
    expand_came = scatter_staged(slot_expand, "dp")
    second_low = backward_of_norm(
        grad_two, centred_two, inv_two, second_norm[0], second_grads, pixel_total
    ).astype(LOW)
    maps_two = second_low.reshape(map_side, map_side, crops_dev, mid_local)
    first_terms = lax.conv_general_dilated(
        maps_two,
        spatial_rel[::-1, ::-1].transpose(0, 1, 3, 2),
        (1, 1),
        ((1, 1), (1, 1)),
        dimension_numbers=conv_dims,
        preferred_element_type=WIDE,
    ).reshape(pixel_rows, mid_width)
    first_sum = scatter_relative(column_parts(first_terms), "chan")
    spatial_terms = lax.conv_general_dilated(
        maps_one,
        maps_two,
        (1, 1),
        ((1, 1), (1, 1)),
        dimension_numbers=lax.ConvDimensionNumbers((3, 2, 0, 1), (3, 2, 0, 1), (2, 3, 0, 1)),
        preferred_element_type=WIDE,
    ).reshape(9, mid_width, mid_local)
    spatial_sent = deal_rows(
        spatial_terms.astype(LOW).reshape(9 * mid_width, mid_local),
        jnp.stack([dp_at, chan_at]).astype(jnp.int32),
        dp_count,
        9,
        chan_count,
    )
    first_sum, spatial_sent = join(first_sum, spatial_sent)
    spatial_came = scatter_staged(spatial_sent, "dp")
    grad_one, centred_one, first_sums = inner_sums(
        first_sum, pre_one, average_one, inv_one, first_norm
    )
    first_grads = total_hyper(first_sums, "dp")
    first_low = backward_of_norm(
        grad_one, centred_one, inv_one, first_norm[0], first_grads, pixel_total
    ).astype(LOW)
    squeeze_grad = contract(pixels, first_low, 0, 0).astype(LOW)
    squeeze_terms = slot_terms(squeeze_grad, 0)
    squeeze_came = scatter_staged(squeeze_terms, "dp")
    first_all = jnp.concatenate(gather_relative(after(first_low, squeeze_terms), "chan"), axis=1)
    proto_grad = contract(after(score_gradient, squeeze_terms), normed_low, 0, 0)[:proto_count].T
    proto_new = step(prototypes, proto_moment, proto_second, proto_grad, 0.1)
    first_all, *proto_new = join(first_all, *proto_new)
    images_grad = contract(first_all, squeeze_rel, 1, 1) + sum_grad
    images_grad = images_grad.reshape(map_side, map_side, crops_dev, out_local).transpose(2, 0, 1, 3)
    spatial_came, expand_came, _ = join(spatial_came, expand_came, squeeze_terms)
    images_grad, squeeze_came = join(images_grad, squeeze_came)
    slot_squeeze, slot_spatial, slot_expand = [
        wide_sum(came) for came in (squeeze_came, spatial_came, expand_came)
    ]
    norm_gradient = jnp.concatenate([first_grads, second_grads, third_grads, head_grads], axis=1)
    norm_gradient = norm_gradient[::-1].reshape(norm_params.shape)
    return (
        block_out,
        loss,
        images_grad,
        *step(squeeze_weight, squeeze_moment, squeeze_second, slot_squeeze, in_width ** (-0.5)),
        *step(
            spatial_weight, spatial_moment, spatial_second, slot_spatial, (9 * mid_width) ** (-0.5)
        ),
        *step(expand_weight, expand_moment, expand_second, slot_expand, mid_width ** (-0.5)),
        *hidden_new,
        *project_new,
        *proto_new,
        *step(norm_params, norm_moment, norm_second, norm_gradient, 0.5, 0.0),
    )


def solution(mesh):
    rows, both, whole = P("dp", None), P("dp", "chan"), P()
    maps = P("dp", None, None, "chan")
    norm = P(None, "chan", None)
    placed = (
        (P("dp", None, None, None), P("dp"), whole)
        + (both,) * 12
        + (rows,) * 3
        + (whole,) * 3
        + (norm,) * 3
        + (rows, P("dp"), whole, whole)
    )
    return jax.shard_map(
        local,
        mesh=mesh,
        in_specs=placed,
        out_specs=(maps, whole, maps) + (both,) * 12 + (rows,) * 3 + (whole,) * 3 + (norm,) * 3,
        check_vma=False,
    )
```
